32 devices in a mesh: groups: 2 (over y), row: 4 (over z), col: 4 (over x, core).
Axes of the slice: x: 2, y: 2, z: 4, core: 2. Of those that a mesh axis runs over, the one named last changes fastest.
Arguments:
- gradient: bfloat16 [8192, 4096], P(('groups', 'row'), 'col'), parts along dimension 0, may hold values from -6 to 6
- first_moment: float32 [8192, 4096], P(('groups', 'row'), 'col'), parts along dimension 0, may hold values from -4 to 4
- second_moment: float32 [8192, 4096], P(('groups', 'row'), 'col'), parts along dimension 0, may hold values from 0.01 to 1
- left_basis: bfloat16 [8192, 4096], P(('groups', 'col'), 'row'), parts along dimension 0, may hold values from -0.09375 to 0.09375
- right_basis: bfloat16 [8192, 4096], P(('groups', 'row'), 'col'), parts along dimension 0, may hold values from -0.09375 to 0.09375
Outputs:
- new_first: float32 [8192, 4096], P(('groups', 'row'), 'col'), parts along dimension 0
- new_second: float32 [8192, 4096], P(('groups', 'row'), 'col'), parts along dimension 0
- update: float32 [8192, 4096], P(('groups', 'row'), 'col'), parts along dimension 0
The draws below stay inside these ranges and needn't reach their ends.
There are 2 independent parts, one for each index of `groups`. The reference program is written for one: setup_inputs(seed, part) draws one part's arguments, and reference() takes and returns one part's arrays. A program takes and returns all parts, laid end to end along the dimension named above; each array names one. Nothing has to cross between parts.
All inputs are finite; a program needn't handle non-finite values.
Results may differ from the reference program's by a relative error of at most 0.0003.
Values may be sent and summed in bfloat16 or wider, within the bound.
No kernel may reach another device: no remote copies, remote signals or barrier semaphores. Data moves between devices by JAX's collectives and lax.ppermute only.
A program may use at most 128 MiB of HBM per device.

```python
import math
import jax
import jax.numpy as jnp
from jax import lax

D_ROWS = 4096
D_COLS = 4096


def block_scale(stream_key, extent, cuts, smallest, top_value):
    def one(axis_at, parts):
        heights = jax.random.uniform(jax.random.fold_in(jax.random.fold_in(stream_key, 6), axis_at), (parts,), jnp.float32, smallest / len(cuts), top_value / len(cuts))
        return jnp.repeat(jnp.exp(heights), extent[axis_at] // parts).reshape((-1,) + (1,) * (len(extent) - axis_at - 1))

    loudness = one(*cuts[0])
    for cut in cuts[1:]:
        loudness = loudness * one(*cut)
    return loudness


def bell_draw(key, dims, width, bound, pieces=(), held_as=jnp.bfloat16):
    gain = block_scale(key, dims, pieces, -0.22, 0.18) if pieces else 1.0
    entries = jax.random.normal(key, dims, jnp.float32) * width * gain
    return jnp.minimum(jnp.maximum(entries, -bound), bound).astype(held_as)


def setup_inputs(seed: int = 0, part: int = 0) -> dict:
    arg_keys = jax.random.split(jax.random.key(seed), 6)
    part_splits = jax.random.split(jax.random.fold_in(arg_keys[5], part), 6)
    return {
        "gradient": bell_draw(part_splits[0], (D_ROWS, D_COLS), 1.0, 6.0, ((0, 4), (1, 4))),
        "first_moment": bell_draw(part_splits[1], (D_ROWS, D_COLS), 0.5, 4.0, ((0, 4), (1, 4)), jnp.float32),
        "second_moment": jnp.clip(jnp.exp(math.log(1.0) - 4.6051702 * jax.random.uniform(part_splits[2], (D_ROWS, D_COLS), jnp.float32) ** block_scale(part_splits[2], (D_ROWS, D_COLS), ((0, 4), (1, 4)), -0.2, 0.2)), 0.01, 1.0),
        "left_basis": bell_draw(part_splits[3], (D_ROWS, D_ROWS), D_ROWS ** -0.5, 0.09375, ((0, 4), (1, 4))),
        "right_basis": bell_draw(part_splits[4], (D_COLS, D_COLS), D_COLS ** -0.5, 0.09375, ((0, 4), (1, 4))),
    }


BETA_ONE = 0.9
BETA_TWO = 0.95
EPSILON = 1e-08

def reference(gradient, first_moment, second_moment, left_basis, right_basis):
    highest = lax.Precision.HIGHEST
    halfway = jnp.dot(left_basis.T, gradient, preferred_element_type=jnp.float32)
    rotated = jnp.dot(halfway, right_basis.astype(jnp.float32), precision=highest)
    new_first = BETA_ONE * first_moment + (1.0 - BETA_ONE) * rotated
    new_second = BETA_TWO * second_moment + (1.0 - BETA_TWO) * rotated * rotated
    normed = new_first / (jnp.sqrt(new_second) + EPSILON)
    restored = jnp.dot(normed, right_basis.astype(jnp.float32).T, precision=highest)
    update = jnp.dot(left_basis.astype(jnp.float32), restored, precision=highest)
    return (new_first, new_second, update)
```

```python
import jax
import jax.numpy as jnp
from jax import lax
from jax.sharding import PartitionSpec as P

BETA_ONE = 0.9
BETA_TWO = 0.95
EPSILON = 1e-08
CHUNKS = 4
F32 = jnp.float32
BF16 = jnp.bfloat16


def split(value):
    high = lax.reduce_precision(value, exponent_bits=8, mantissa_bits=7)
    return high.astype(BF16), (value - high).astype(BF16)


def dot(a, b, dims):
    return lax.dot_general(a, b, (dims, ((), ())), preferred_element_type=F32)


def build(cols):
    def swap(value, distance):
        return lax.ppermute(value, "col", [(i, i ^ distance) for i in range(cols)])

    def gather_col(block):
        me = lax.axis_index("col")
        out = jnp.zeros((cols,) + block.shape, block.dtype)
        held = {0: block}
        for distance in range(2, cols, 2):
            held[distance] = swap(block, distance)
        for distance in range(0, cols, 2):
            held[distance + 1] = swap(held[distance], 1)
        for distance, value in held.items():
            out = lax.dynamic_update_index_in_dim(out, value, me ^ distance, 0)
        return out

    def scatter_col(part):
        total = None
        for distance in list(range(2, cols, 2)) + [0]:
            term = swap(part(distance ^ 1), 1) + part(distance)
            if distance:
                term = swap(term, distance)
            total = term if total is None else total + term
        return total

    def local(gradient, first_moment, second_moment, left_basis, right_basis):
        me = lax.axis_index("col")
        depth, width = gradient.shape
        grad_cols = lax.all_gather(gradient, "row", axis=0, tiled=True)
        left_cols = gather_col(left_basis)
        left_cols = left_cols.reshape(-1, left_cols.shape[-1])
        right_cols = lax.all_gather(right_basis, "row", axis=0, tiled=True)
        halfway = dot(left_cols, grad_cols, ((0,), (0,)))
        high, low = split(halfway)
        high, low = gather_col(high), gather_col(low)
        by_col = right_cols.reshape(cols, width, width)
        rotated = dot(high, by_col, ((0, 2), (0, 1))) + dot(low, by_col, ((0, 2), (0, 1)))
        new_first = BETA_ONE * first_moment + (1.0 - BETA_ONE) * rotated
        new_second = BETA_TWO * second_moment + (1.0 - BETA_TWO) * rotated * rotated
        normed = new_first / (jnp.sqrt(new_second) + EPSILON)
        high, low = split(normed)
        piece = width // CHUNKS
        updates = []
        for chunk in range(CHUNKS):

            def part(distance):
                rows = lax.dynamic_slice_in_dim(
                    right_cols, (me ^ distance) * width + chunk * piece, piece, 0
                )
                return dot(high, rows, ((1,), (1,))) + dot(low, rows, ((1,), (1,)))

            s_high, s_low = split(scatter_col(part))
            product = dot(left_cols, s_high, ((1,), (0,))) + dot(left_cols, s_low, ((1,), (0,)))
            updates.append(lax.psum_scatter(product, "row", scatter_dimension=0, tiled=True))
        return (new_first, new_second, jnp.concatenate(updates, axis=1))

    return local


def solution(mesh):
    return jax.shard_map(
        build(mesh.shape["col"]),
        mesh=mesh,
        in_specs=(
            P(("groups", "row"), "col"),
            P(("groups", "row"), "col"),
            P(("groups", "row"), "col"),
            P(("groups", "col"), "row"),
            P(("groups", "row"), "col"),
        ),
        out_specs=(
            P(("groups", "row"), "col"),
            P(("groups", "row"), "col"),
            P(("groups", "row"), "col"),
        ),
        check_vma=False,
    )
```

```python
import functools
import jax
import jax.numpy as jnp
from jax import lax
from jax.experimental import pallas as pl
from jax.experimental.pallas import tpu as pltpu
from jax.sharding import PartitionSpec as P

BETA_ONE = 0.9
BETA_TWO = 0.95
EPSILON = 1e-08
CHUNKS = 4
EXTRA = 16
F32 = jnp.float32
BF16 = jnp.bfloat16
VMEM = 56 * 2**20


def params():
    return pltpu.CompilerParams(vmem_limit_bytes=VMEM)


def cost(flops, moved):
    return pl.CostEstimate(flops=int(flops), bytes_accessed=int(moved), transcendentals=0)


def split(value):
    high = lax.reduce_precision(value, exponent_bits=8, mantissa_bits=7)
    return high.astype(BF16), (value - high).astype(BF16)


def kernel_split(value):
    high = value.astype(BF16)
    return high, (value - high.astype(F32)).astype(BF16)


def dot(a, b, dims):
    return lax.dot_general(a, b, (dims, ((), ())), preferred_element_type=F32)


def rotate_kernel(me_ref, *refs, cols, width):
    pieces, (right, first, second, new_first, new_second, normed) = refs[:cols], refs[cols:]
    tile = first.shape[0]
    total = None
    for distance in range(cols):
        rows = right[pl.ds(pl.multiple_of((me_ref[0] ^ distance) * width, width), width), :]
        both = pieces[distance][...].reshape(2 * tile, width)
        term = dot(both, rows, ((1,), (0,)))
        total = term if total is None else total + term
    rotated = total[:tile] + total[tile:]
    one = BETA_ONE * first[...] + (1.0 - BETA_ONE) * rotated
    two = BETA_TWO * second[...] + (1.0 - BETA_TWO) * rotated * rotated
    new_first[...] = one
    new_second[...] = two
    high, low = kernel_split(one / (jnp.sqrt(two) + EPSILON))
    normed[0] = high
    normed[1] = low


def rotate(me, pieces, right, first, second):
    cols = len(pieces)
    depth, width = first.shape
    tile = min(256, depth)
    one = lambda i, s: (i, 0)
    two = lambda i, s: (0, i, 0)
    block = pl.BlockSpec((tile, width), one)
    pair = pl.BlockSpec((2, tile, width), two)
    whole = pl.BlockSpec(right.shape, lambda i, s: (0, 0), pipeline_mode=pl.Buffered(1))
    return pl.pallas_call(
        functools.partial(rotate_kernel, cols=cols, width=width),
        grid_spec=pltpu.PrefetchScalarGridSpec(
            num_scalar_prefetch=1,
            grid=(depth // tile,),
            in_specs=[pair] * cols + [whole, block, block],
            out_specs=[block, block, pair],
        ),
        out_shape=[
            jax.ShapeDtypeStruct((depth, width), F32),
            jax.ShapeDtypeStruct((depth, width), F32),
            jax.ShapeDtypeStruct((2, depth, width), BF16),
        ],
        compiler_params=params(),
        cost_estimate=cost(4 * depth * width * width * cols, 20 * depth * width),
        name="rotate",
    )(me, *pieces, right, first, second)


def restore_kernel(me_ref, normed, *refs, cols):
    rows, (keep, mate) = refs[:cols], refs[cols:]
    tile = normed.shape[1]
    both = normed[...].reshape(2 * tile, normed.shape[2])
    for distance in range(cols):
        term = dot(both, rows[distance][...], ((1,), (1,)))
        (mate if distance % 2 else keep)[distance // 2] = term[:tile] + term[tile:]


def restore(me, normed, right, chunk, piece, cols, width):
    _, depth, inner = normed.shape
    tile = min(256, depth)
    per = width // piece

    def at(distance):
        return lambda i, s: ((s[0] ^ distance) * per + chunk, 0)

    out = pl.BlockSpec((cols // 2, tile, piece), lambda i, s: (0, i, 0))
    return pl.pallas_call(
        functools.partial(restore_kernel, cols=cols),
        grid_spec=pltpu.PrefetchScalarGridSpec(
            num_scalar_prefetch=1,
            grid=(depth // tile,),
            in_specs=[pl.BlockSpec((2, tile, inner), lambda i, s: (0, i, 0))]
            + [pl.BlockSpec((piece, inner), at(d)) for d in range(cols)],
            out_specs=[out, out],
        ),
        out_shape=[jax.ShapeDtypeStruct((cols // 2, depth, piece), F32)] * 2,
        compiler_params=params(),
        cost_estimate=cost(4 * depth * inner * piece * cols, 8 * depth * piece * cols),
        name="restore",
    )(me, normed, *([right] * cols))


def expand_kernel(*refs, terms):
    parts, (left, out, both) = refs[:terms], refs[terms:]
    piece = out.shape[1]

    @pl.when(pl.program_id(0) == 0)
    def _():
        total = parts[0][...]
        for part in parts[1:]:
            total = total + part[...]
        high, low = kernel_split(total)
        both[:, :piece] = high
        both[:, piece:] = low

    product = dot(left[...], both[...], ((1,), (0,)))
    out[...] = product[:, :piece] + product[:, piece:]


def expand(parts, left):
    rows, inner = left.shape
    piece = parts[0].shape[1]
    tile = min(512, rows)
    whole = pl.BlockSpec((inner, piece), lambda i: (0, 0))
    return pl.pallas_call(
        functools.partial(expand_kernel, terms=len(parts)),
        grid=(rows // tile,),
        in_specs=[whole] * len(parts) + [pl.BlockSpec((tile, inner), lambda i: (i, 0))],
        out_specs=pl.BlockSpec((tile, piece), lambda i: (i, 0)),
        out_shape=jax.ShapeDtypeStruct((rows, piece), F32),
        scratch_shapes=[pltpu.VMEM((inner, 2 * piece), BF16)],
        compiler_params=params(),
        cost_estimate=cost(4 * rows * inner * piece, 4 * rows * piece + 2 * rows * inner),
        name="expand",
    )(*parts, left)


TOP = 7.5


def encode(value, inverse):
    code = jnp.abs(value) * (inverse * 2.0**TOP)
    for _ in range(4):
        code = code * code
    return jnp.where(value < 0, -code, code).astype(BF16)


def decode(code, scale):
    code = code.astype(F32)
    size = jnp.abs(code)
    root = jnp.exp2(jnp.log2(size) * 0.0625 - TOP) * scale
    root = jnp.where(size > 0, root, 0.0)
    return jnp.where(code < 0, -root, root)


def scale_of(message, depth):
    return jnp.max(message[depth : depth + EXTRA, :].astype(F32), axis=(0, 1), keepdims=True)


def hop_kernel(at_ref, *refs, arrivals, tile):
    blocks, refs = refs[:2], refs[2:]
    arrived, refs = refs[:arrivals], refs[arrivals:]
    outs, total = refs[:2], refs[2]
    depth, piece = total.shape
    for way in range(2):
        scale_in = scale_of(arrived[way], depth) if arrivals else None

        def add(i, top, way=way, scale_in=scale_in):
            rows = pl.ds(pl.multiple_of(i * tile, tile), tile)
            value = blocks[way][rows, :]
            if arrivals:
                value = value + decode(arrived[way][rows, :], scale_in)
            total[rows, :] = value
            return jnp.maximum(top, jnp.abs(value))

        top = lax.fori_loop(0, depth // tile, add, jnp.zeros((tile, piece), F32))
        top = jnp.maximum(jnp.max(top, axis=(0, 1), keepdims=True), 1e-30)
        scale = jnp.broadcast_to(top, (EXTRA, piece)).astype(BF16)
        outs[way][depth : depth + EXTRA, :] = scale
        inverse = 1.0 / jnp.max(scale.astype(F32), axis=(0, 1), keepdims=True)

        def put(i, carry, way=way, inverse=inverse):
            rows = pl.ds(pl.multiple_of(i * tile, tile), tile)
            outs[way][rows, :] = encode(total[rows, :], inverse)
            return carry

        lax.fori_loop(0, depth // tile, put, 0)


def hop(at, product, arrived, depth):
    piece = product.shape[1]
    tile = min(64, depth)
    message = pl.BlockSpec((depth + EXTRA, piece), lambda i, s: (0, 0))
    return pl.pallas_call(
        functools.partial(hop_kernel, arrivals=len(arrived), tile=tile),
        grid_spec=pltpu.PrefetchScalarGridSpec(
            num_scalar_prefetch=1,
            grid=(1,),
            in_specs=[
                pl.BlockSpec((depth, piece), lambda i, s: (s[0], 0)),
                pl.BlockSpec((depth, piece), lambda i, s: (s[1], 0)),
            ]
            + [message] * len(arrived),
            out_specs=[message] * 2,
            scratch_shapes=[pltpu.VMEM((depth, piece), F32)],
        ),
        out_shape=[jax.ShapeDtypeStruct((depth + EXTRA, piece), BF16)] * 2,
        compiler_params=params(),
        cost_estimate=cost(400 * depth * piece, 12 * depth * piece),
        name="hop",
    )(at, product, product, *arrived)


def finish_kernel(at_ref, block, up, down, *refs, tile):
    out = refs[-1]
    depth = out.shape[0]
    scales = [scale_of(message, depth) for message in (up, down)]

    def add(i, carry):
        rows = pl.ds(pl.multiple_of(i * tile, tile), tile)
        out[rows, :] = (
            block[rows, :] + decode(up[rows, :], scales[0]) + decode(down[rows, :], scales[1])
        )
        return carry

    lax.fori_loop(0, depth // tile, add, 0)


def finish(at, product, arrived, update, chunk, depth, width):
    piece = product.shape[1]
    tile = min(64, depth)
    message = pl.BlockSpec((depth + EXTRA, piece), lambda i, s: (0, 0))
    extra = [] if update is None else [update]
    return pl.pallas_call(
        functools.partial(finish_kernel, tile=tile),
        grid_spec=pltpu.PrefetchScalarGridSpec(
            num_scalar_prefetch=1,
            grid=(1,),
            in_specs=[pl.BlockSpec((depth, piece), lambda i, s: (s[0], 0)), message, message]
            + [pl.BlockSpec(memory_space=pl.ANY)] * len(extra),
            out_specs=pl.BlockSpec((depth, piece), lambda i, s: (0, chunk)),
        ),
        out_shape=jax.ShapeDtypeStruct((depth, width), F32),
        input_output_aliases={4: 0} if extra else {},
        compiler_params=params(),
        cost_estimate=cost(400 * depth * piece, 12 * depth * piece),
        name="finish",
    )(at, product, *arrived, *extra)


def build(lines, cols):
    def swap(value, distance):
        return lax.ppermute(value, "col", [(i, i ^ distance) for i in range(cols)])

    def up(value, senders):
        return lax.ppermute(value, "row", [(i, i + 1) for i in senders])

    def down(value, senders):
        return lax.ppermute(value, "row", [(i, i - 1) for i in senders])

    def spread(block):
        held = {0: block}
        for step in range(1, lines):
            held[-step] = up(held[1 - step], range(step - 1, lines - 1))
            held[step] = down(held[step - 1], range(1, lines - step + 1))
        return held

    def by_distance(block):
        held = {0: block}
        for distance in range(2, cols, 2):
            held[distance] = swap(block, distance)
        for distance in range(0, cols, 2):
            held[distance + 1] = swap(held[distance], 1)
        return held

    def local(gradient, first_moment, second_moment, left_basis, right_basis):
        me, place = lax.axis_index("col"), lax.axis_index("row")
        depth, width = gradient.shape
        index = jnp.reshape(me, (1,))

        grads = spread(gradient)
        lefts = by_distance(left_basis)
        left = jnp.zeros((cols,) + left_basis.shape, BF16)
        for distance, value in lefts.items():
            left = lax.dynamic_update_index_in_dim(left, value, me ^ distance, 0)
        left = left.reshape(-1, left_basis.shape[1])

        halfway = None
        for offset, value in grads.items():
            rows = lax.dynamic_slice_in_dim(left, (place + offset) * depth, depth, 0)
            term = dot(rows, value, ((0,), (0,)))
            halfway = term if halfway is None else halfway + term

        rights = spread(right_basis)
        right = jnp.zeros((lines + 1,) + right_basis.shape, BF16)
        for offset, value in rights.items():
            there = place + offset
            there = jnp.where((there >= 0) & (there < lines), there, lines)
            right = lax.dynamic_update_index_in_dim(right, value, there, 0)
        right = right.reshape(-1, right_basis.shape[1])

        halves = by_distance(jnp.stack(split(halfway)))
        halves = [halves[distance] for distance in range(cols)]
        new_first, new_second, normed = rotate(index, halves, right, first_moment, second_moment)

        piece = width // CHUNKS
        update = None
        for chunk in range(CHUNKS):
            keep, mate = restore(index, normed, right, chunk, piece, cols, width)
            mate = swap(mate, 1)
            parts = [keep[0], mate[0]]
            for distance in range(2, cols, 2):
                parts.append(swap(keep[distance // 2] + mate[distance // 2], distance))
            product = expand(parts, left)
            arrived = ()
            for step in range(1, lines):
                ahead = lines - step
                at = jnp.stack(
                    [jnp.minimum(place + ahead, lines - 1), jnp.maximum(place - ahead, 0)]
                )
                upward, downward = hop(at, product, arrived, depth)
                arrived = (
                    up(upward, range(0, step)),
                    down(downward, range(lines - step, lines)),
                )
            update = finish(
                jnp.reshape(place, (1,)), product, arrived, update, chunk, depth, width
            )
        return (new_first, new_second, update)

    return local


def solution(mesh):
    return jax.shard_map(
        build(mesh.shape["row"], mesh.shape["col"]),
        mesh=mesh,
        in_specs=(
            P(("groups", "row"), "col"),
            P(("groups", "row"), "col"),
            P(("groups", "row"), "col"),
            P(("groups", "col"), "row"),
            P(("groups", "row"), "col"),
        ),
        out_specs=(
            P(("groups", "row"), "col"),
            P(("groups", "row"), "col"),
            P(("groups", "row"), "col"),
        ),
        check_vma=False,
    )
```

```python
import functools
import jax
import jax.numpy as jnp
from jax import lax
from jax.experimental import pallas as pl
from jax.experimental.pallas import tpu as pltpu
from jax.sharding import PartitionSpec as P

BETA_ONE = 0.9
BETA_TWO = 0.95
EPSILON = 1e-08
CHUNKS = 4
EXTRA = 16
F32 = jnp.float32
BF16 = jnp.bfloat16
MIB = 2**20


def params(mib):
    return pltpu.CompilerParams(vmem_limit_bytes=mib * MIB)


def cost(flops, moved):
    return pl.CostEstimate(flops=int(flops), bytes_accessed=int(moved), transcendentals=0)


def split(value):
    high = lax.reduce_precision(value, exponent_bits=8, mantissa_bits=7)
    return high.astype(BF16), (value - high).astype(BF16)


def kernel_split(value):
    high = value.astype(BF16)
    return high, (value - high.astype(F32)).astype(BF16)


def dot(a, b, dims):
    return lax.dot_general(a, b, (dims, ((), ())), preferred_element_type=F32)


def rotate_part_kernel(me_ref, *refs, cols, half):
    pieces, (right, out) = refs[:-2], refs[-2:]
    tile = out.shape[0]
    total = None
    for at, piece in enumerate(pieces):
        start = (me_ref[0] ^ (at // 2)) * (2 * half) + (at % 2) * half
        rows = right[pl.ds(pl.multiple_of(start, half), half), :]
        term = dot(piece[...].reshape(2 * tile, half), rows, ((1,), (0,)))
        total = term if total is None else total + term
    out[...] = total[:tile] + total[tile:]


def rotate_part(me, pieces, right):
    _, depth, half = pieces[0].shape
    cols = len(pieces) // 2
    width = right.shape[1]
    tile = min(256, depth)
    return pl.pallas_call(
        functools.partial(rotate_part_kernel, cols=cols, half=half),
        grid_spec=pltpu.PrefetchScalarGridSpec(
            num_scalar_prefetch=1,
            grid=(depth // tile,),
            in_specs=[pl.BlockSpec((2, tile, half), lambda i, s: (0, i, 0))] * len(pieces)
            + [pl.BlockSpec(right.shape, lambda i, s: (0, 0), pipeline_mode=pl.Buffered(1))],
            out_specs=pl.BlockSpec((tile, width), lambda i, s: (i, 0)),
        ),
        out_shape=jax.ShapeDtypeStruct((depth, width), F32),
        compiler_params=params(40),
        cost_estimate=cost(8 * depth * width * half * cols, 20 * depth * width),
        name="rotate_part",
    )(me, *pieces, right)


def rotate_kernel(place_ref, part, *refs, count):
    pieces, (above, below, first, second, new_first, new_second, normed) = (
        refs[:count],
        refs[count:],
    )
    tile = first.shape[0]
    half = pieces[0].shape[2]
    rotated = part[...]
    for at, piece in enumerate(pieces):
        rows = pl.ds(at * half, half)
        last = jnp.where(place_ref[0] == 0, above[rows, :], below[rows, :])
        both = dot(piece[...].reshape(2 * tile, half), last, ((1,), (0,)))
        rotated = rotated + both[:tile] + both[tile:]
    one = BETA_ONE * first[...] + (1.0 - BETA_ONE) * rotated
    two = BETA_TWO * second[...] + (1.0 - BETA_TWO) * rotated * rotated
    new_first[...] = one
    new_second[...] = two
    high, low = kernel_split(one / (jnp.sqrt(two) + EPSILON))
    normed[0] = high
    normed[1] = low


def rotate(place, part, pieces, above, below, first, second):
    depth, width = first.shape
    half = pieces[0].shape[2]
    tile = min(256, depth)
    block = pl.BlockSpec((tile, width), lambda i, s: (i, 0))
    pair = pl.BlockSpec((2, tile, width), lambda i, s: (0, i, 0))
    whole = pl.BlockSpec(above.shape, lambda i, s: (0, 0), pipeline_mode=pl.Buffered(1))
    return pl.pallas_call(
        functools.partial(rotate_kernel, count=len(pieces)),
        grid_spec=pltpu.PrefetchScalarGridSpec(
            num_scalar_prefetch=1,
            grid=(depth // tile,),
            in_specs=[block]
            + [pl.BlockSpec((2, tile, half), lambda i, s: (0, i, 0))] * len(pieces)
            + [whole, whole, block, block],
            out_specs=[block, block, pair],
        ),
        out_shape=[
            jax.ShapeDtypeStruct((depth, width), F32),
            jax.ShapeDtypeStruct((depth, width), F32),
            jax.ShapeDtypeStruct((2, depth, width), BF16),
        ],
        compiler_params=params(36),
        cost_estimate=cost(4 * depth * width * half * len(pieces), 30 * depth * width),
        name="rotate",
    )(place, part, *pieces, above, below, first, second)


def restore_kernel(me_ref, normed, *refs, cols):
    rows, (keep, mate) = refs[:cols], refs[cols:]
    tile = normed.shape[1]
    both = normed[...].reshape(2 * tile, normed.shape[2])
    for distance in range(cols):
        term = dot(both, rows[distance][...], ((1,), (1,)))
        (mate if distance % 2 else keep)[distance // 2] = term[:tile] + term[tile:]


def restore(me, normed, right, chunk, piece, cols, width):
    _, depth, inner = normed.shape
    tile = min(512, depth)
    per = width // piece

    def at(distance):
        return lambda i, s: ((s[0] ^ distance) * per + chunk, 0)

    out = pl.BlockSpec((cols // 2, tile, piece), lambda i, s: (0, i, 0))
    return pl.pallas_call(
        functools.partial(restore_kernel, cols=cols),
        grid_spec=pltpu.PrefetchScalarGridSpec(
            num_scalar_prefetch=1,
            grid=(depth // tile,),
            in_specs=[pl.BlockSpec((2, tile, inner), lambda i, s: (0, i, 0))]
            + [pl.BlockSpec((piece, inner), at(d)) for d in range(cols)],
            out_specs=[out, out],
        ),
        out_shape=[jax.ShapeDtypeStruct((cols // 2, depth, piece), F32)] * 2,
        compiler_params=params(36),
        cost_estimate=cost(4 * depth * inner * piece * cols, 8 * depth * piece * cols),
        name="restore",
    )(me, normed, *([right] * cols))


TOP = 7.5


def encode(value, inverse):
    code = jnp.abs(value) * (inverse * 2.0**TOP)
    for _ in range(4):
        code = code * code
    return jnp.where(value < 0, -code, code).astype(BF16)


def decode(code, scale):
    code = code.astype(F32)
    size = jnp.abs(code)
    root = jnp.exp2(jnp.log2(size) * 0.0625 - TOP) * scale
    root = jnp.where(size > 0, root, 0.0)
    return jnp.where(code < 0, -root, root)


def scale_of(message, depth):
    return jnp.max(message[depth : depth + EXTRA, :].astype(F32), axis=(0, 1), keepdims=True)


def send_kernel(*refs, terms, tile):
    parts, (message, own, total) = refs[:terms], refs[terms:]
    depth, piece = total.shape

    def add(i, top):
        rows = pl.ds(pl.multiple_of(i * tile, tile), tile)
        value = parts[0][rows, :]
        for part in parts[1:]:
            value = value + part[rows, :]
        total[rows, :] = value
        high, low = kernel_split(value)
        own[rows, :piece] = high
        own[rows, piece:] = low
        return jnp.maximum(top, jnp.abs(value))

    top = lax.fori_loop(0, depth // tile, add, jnp.zeros((tile, piece), F32))
    top = jnp.maximum(jnp.max(top, axis=(0, 1), keepdims=True), 1e-30)
    scale = jnp.broadcast_to(top, (EXTRA, piece)).astype(BF16)
    message[depth : depth + EXTRA, :] = scale
    inverse = 1.0 / jnp.max(scale.astype(F32), axis=(0, 1), keepdims=True)

    def put(i, carry):
        rows = pl.ds(pl.multiple_of(i * tile, tile), tile)
        message[rows, :] = encode(total[rows, :], inverse)
        return carry

    lax.fori_loop(0, depth // tile, put, 0)


def send(parts):
    depth, piece = parts[0].shape
    tile = min(64, depth)
    return pl.pallas_call(
        functools.partial(send_kernel, terms=len(parts), tile=tile),
        out_shape=[
            jax.ShapeDtypeStruct((depth + EXTRA, piece), BF16),
            jax.ShapeDtypeStruct((depth, 2 * piece), BF16),
        ],
        scratch_shapes=[pltpu.VMEM((depth, piece), F32)],
        compiler_params=params(24),
        cost_estimate=cost(400 * depth * piece, 18 * depth * piece),
        name="send",
    )(*parts)


def update_kernel(place_ref, own, *refs, lines, tile):
    ups, downs = refs[: lines - 1], refs[lines - 1 : 2 * lines - 2]
    left, out, held = refs[2 * lines - 2], refs[-2], refs[-1]
    depth, piece = out.shape
    inner = held.shape[0]
    step = pl.program_id(0)

    @pl.when(step == 0)
    def _():
        held[...] = own[...]

    for back in range(1, lines):

        @pl.when(step == back)
        def _(back=back):
            up, down = ups[back - 1], downs[lines - back - 1]
            below = place_ref[0] >= back
            scale = jnp.where(below, scale_of(up, inner), scale_of(down, inner))

            def unpack(i, carry):
                rows = pl.ds(pl.multiple_of(i * tile, tile), tile)
                value = decode(jnp.where(below, up[rows, :], down[rows, :]), scale)
                high, low = kernel_split(value)
                held[rows, :piece] = high
                held[rows, piece:] = low
                return carry

            lax.fori_loop(0, inner // tile, unpack, 0)

    both = dot(left[...].reshape(depth, inner), held[...], ((1,), (0,)))
    term = both[:, :piece] + both[:, piece:]

    @pl.when(step == 0)
    def _():
        out[...] = term

    @pl.when(step > 0)
    def _():
        out[...] += term


def update_chunk(place, own, ups, downs, left, update, chunk, depth, width):
    cols, lines, quarter, inner = left.shape
    piece = own.shape[1] // 2
    tile = min(64, inner)
    message = pl.BlockSpec((inner + EXTRA, piece), lambda i, s: (0, 0))
    extra = [] if update is None else [update]
    return pl.pallas_call(
        functools.partial(update_kernel, lines=lines, tile=tile),
        grid_spec=pltpu.PrefetchScalarGridSpec(
            num_scalar_prefetch=1,
            grid=(lines,),
            in_specs=[pl.BlockSpec((inner, 2 * piece), lambda i, s: (0, 0))]
            + [message] * (2 * lines - 2)
            + [pl.BlockSpec((cols, 1, quarter, inner), lambda i, s: (0, i, 0, 0))]
            + [pl.BlockSpec(memory_space=pl.ANY)] * len(extra),
            out_specs=pl.BlockSpec((depth, piece), lambda i, s: (0, chunk)),
            scratch_shapes=[pltpu.VMEM((inner, 2 * piece), BF16)],
        ),
        out_shape=jax.ShapeDtypeStruct((depth, width), F32),
        input_output_aliases={2 * lines + 1: 0} if extra else {},
        compiler_params=params(36),
        cost_estimate=cost(4 * depth * inner * piece * lines, 12 * depth * piece * lines),
        name="update_chunk",
    )(place, own, *ups, *downs, left, *extra)


def build(lines, cols):
    def swap(value, distance):
        return lax.ppermute(value, "col", [(i, i ^ distance) for i in range(cols)])

    def up(value, senders):
        return lax.ppermute(value, "row", [(i, i + 1) for i in senders])

    def down(value, senders):
        return lax.ppermute(value, "row", [(i, i - 1) for i in senders])

    def spread(block):
        held = {0: block}
        for step in range(1, lines):
            held[-step] = up(held[1 - step], range(step - 1, lines - 1))
            held[step] = down(held[step - 1], range(1, lines - step + 1))
        return held

    def by_distance(block):
        held = {0: block}
        for distance in range(2, cols, 2):
            held[distance] = swap(block, distance)
        for distance in range(0, cols, 2):
            held[distance + 1] = swap(held[distance], 1)
        return held

    def place_by_distance(block, me):
        out = jnp.zeros((cols,) + block.shape, block.dtype)
        for distance, value in by_distance(block).items():
            out = lax.dynamic_update_index_in_dim(out, value, me ^ distance, 0)
        return out

    def local(gradient, first_moment, second_moment, left_basis, right_basis):
        me, place = lax.axis_index("col"), lax.axis_index("row")
        depth, width = gradient.shape
        half = width // 2
        index, spot = jnp.reshape(me, (1,)), jnp.reshape(place, (1,))
        far = lines - 1

        left = place_by_distance(left_basis, me).reshape(-1, left_basis.shape[1])
        pieces = {}
        for side in range(2):
            grads = spread(gradient[:, side * half : (side + 1) * half])
            halfway = None
            for offset, value in grads.items():
                if abs(offset) == far:
                    continue
                rows = lax.dynamic_slice_in_dim(left, (place + offset) * depth, depth, 0)
                term = dot(rows, value, ((0,), (0,)))
                halfway = term if halfway is None else halfway + term
            rows = lax.dynamic_slice_in_dim(left, (far - place) * depth, depth, 0)
            last = jnp.where(place == 0, grads[far], grads[-far])
            halfway = halfway + dot(rows, last, ((0,), (0,)))
            for distance, value in by_distance(jnp.stack(split(halfway))).items():
                pieces[distance, side] = value

        right = jnp.zeros(((lines + 1) * depth, width), BF16)
        ends = []
        for side in range(2):
            rights = spread(lax.slice_in_dim(right_basis, side * depth // 2, (side + 1) * depth // 2))
            for offset, value in rights.items():
                if abs(offset) == far:
                    continue
                there = place + offset
                there = jnp.where((there >= 0) & (there < lines), there, lines)
                right = lax.dynamic_update_slice_in_dim(
                    right, value, there * depth + side * depth // 2, 0
                )
            ends.append((rights[far], rights[-far]))
        above = jnp.concatenate([end[0] for end in ends])
        below = jnp.concatenate([end[1] for end in ends])

        ordered = [pieces[distance, side] for distance in range(cols) for side in range(2)]
        part = rotate_part(index, ordered, right)
        span = depth // half
        lasts = []
        for at in range(span):
            chosen = None
            for distance in range(cols):
                for side in [at] if span == 2 else range(2):
                    value = pieces[distance, side]
                    here = (me ^ distance) * 2 + side == (far - place) * span + at
                    chosen = value if chosen is None else jnp.where(here, value, chosen)
            lasts.append(chosen)
        new_first, new_second, normed = rotate(
            spot, part, lasts, above, below, first_moment, second_moment
        )
        there = jnp.where((place == 0) | (place == far), far - place, lines)
        last = jnp.where(place == 0, above, below)
        right = lax.dynamic_update_slice_in_dim(right, last, there * depth, 0)

        left_late, last = lax.optimization_barrier((left, last))
        quarter = depth // cols
        backs = []
        for back in range(lines):
            to = lax.rem(place + back, lines)
            rows = lax.dynamic_slice_in_dim(left_late, to * depth + me * quarter, quarter, 0)
            if back:
                rows = lax.ppermute(rows, "row", [(i, (i + back) % lines) for i in range(lines)])
            backs.append(rows)
        left_rows = place_by_distance(jnp.stack(backs), me)

        piece = width // CHUNKS
        update = None
        sums = []
        for chunk in range(CHUNKS):
            if chunk >= 2:
                normed, sums[chunk - 2] = lax.optimization_barrier((normed, sums[chunk - 2]))
            keep, mate = restore(index, normed, right, chunk, piece, cols, width)
            mate = swap(mate, 1)
            sums.append((keep, mate))
            if cols > 2:
                sums[chunk] = (keep, mate, [keep[d] + mate[d] for d in range(1, cols // 2)])
        for chunk in range(CHUNKS):
            keep, mate = sums[chunk][:2]
            parts = [keep[0], mate[0]]
            for at, value in enumerate(sums[chunk][2] if cols > 2 else []):
                parts.append(swap(value, 2 * at + 2))
            message, own = send(parts)
            arrived = spread(message)
            ups = [arrived[-step] for step in range(1, lines)]
            downs = [arrived[step] for step in range(1, lines)]
            update = update_chunk(
                spot, own, ups, downs, left_rows, update, chunk, depth, width
            )
        return (new_first, new_second, update)

    return local


def solution(mesh):
    return jax.shard_map(
        build(mesh.shape["row"], mesh.shape["col"]),
        mesh=mesh,
        in_specs=(
            P(("groups", "row"), "col"),
            P(("groups", "row"), "col"),
            P(("groups", "row"), "col"),
            P(("groups", "col"), "row"),
            P(("groups", "row"), "col"),
        ),
        out_specs=(
            P(("groups", "row"), "col"),
            P(("groups", "row"), "col"),
            P(("groups", "row"), "col"),
        ),
        check_vma=False,
    )
```

```python
import functools
import jax
import jax.numpy as jnp
from jax import lax
from jax.experimental import pallas as pl
from jax.experimental.pallas import tpu as pltpu
from jax.sharding import PartitionSpec as P

BETA_ONE = 0.9
BETA_TWO = 0.95
EPSILON = 1e-08
CHUNKS = 4
EXTRA = 16
F32 = jnp.float32
BF16 = jnp.bfloat16
MIB = 2**20


def params(mib):
    return pltpu.CompilerParams(vmem_limit_bytes=mib * MIB)


def cost(flops, moved):
    return pl.CostEstimate(flops=int(flops) // 100, bytes_accessed=int(moved) // 100, transcendentals=0)


def split(value):
    high = lax.reduce_precision(value, exponent_bits=8, mantissa_bits=7)
    return high.astype(BF16), (value - high).astype(BF16)


def kernel_split(value):
    high = value.astype(BF16)
    return high, (value - high.astype(F32)).astype(BF16)


def dot(a, b, dims):
    return lax.dot_general(a, b, (dims, ((), ())), preferred_element_type=F32)


def halfway_kernel(place_ref, left, *refs, offsets, lines, first, last):
    pieces, refs = refs[: len(offsets)], refs[len(offsets) :]
    total = refs[-1]
    depth = pieces[0].shape[0]
    total[...] = jnp.zeros_like(total) if first else refs[0][...]
    place = place_ref[0]
    for offset, piece in zip(offsets, pieces):

        @pl.when((place + offset >= 0) & (place + offset < lines))
        def _(offset=offset, piece=piece):
            rows = left[pl.ds(pl.multiple_of((place + offset) * depth, depth), depth), :]
            total[...] += dot(rows, piece[...], ((0,), (0,)))

    if last:
        high, low = kernel_split(total[...])
        refs[-2][0] = high
        refs[-2][1] = low
    else:
        refs[-2][...] = total[...]


def halfway(place, left, held, offsets, lines, before, last):
    pieces = [held[offset] for offset in offsets]
    depth, half = pieces[0].shape
    inner = left.shape[1]
    tile = min(256, inner)
    whole = pl.BlockSpec((depth, half), lambda i, s: (0, 0))
    block = pl.BlockSpec((tile, half), lambda i, s: (i, 0))
    extra = [] if before is None else [before]
    return pl.pallas_call(
        functools.partial(
            halfway_kernel, offsets=offsets, lines=lines, first=before is None, last=last
        ),
        grid_spec=pltpu.PrefetchScalarGridSpec(
            num_scalar_prefetch=1,
            grid=(inner // tile,),
            in_specs=[pl.BlockSpec((left.shape[0], tile), lambda i, s: (0, i))]
            + [whole] * len(pieces)
            + [block] * len(extra),
            out_specs=pl.BlockSpec((2, tile, half), lambda i, s: (0, i, 0)) if last else block,
            scratch_shapes=[pltpu.VMEM((tile, half), F32)],
        ),
        out_shape=jax.ShapeDtypeStruct((2, inner, half), BF16)
        if last
        else jax.ShapeDtypeStruct((inner, half), F32),
        compiler_params=params(36),
        cost_estimate=cost(8 * depth * inner * half, 8 * depth * inner),
        name="halfway",
    )(place, left, *pieces, *extra)


def rotate_part_kernel(me_ref, *refs, cols, half):
    pieces, (right, out) = refs[:-2], refs[-2:]
    tile = out.shape[0]
    total = None
    for at, piece in enumerate(pieces):
        start = (me_ref[0] ^ (at // 2)) * (2 * half) + (at % 2) * half
        rows = right[pl.ds(pl.multiple_of(start, half), half), :]
        term = dot(piece[...].reshape(2 * tile, half), rows, ((1,), (0,)))
        total = term if total is None else total + term
    out[...] = total[:tile] + total[tile:]


def rotate_part(me, pieces, right):
    _, depth, half = pieces[0].shape
    cols = len(pieces) // 2
    width = right.shape[1]
    tile = min(256, depth)
    return pl.pallas_call(
        functools.partial(rotate_part_kernel, cols=cols, half=half),
        grid_spec=pltpu.PrefetchScalarGridSpec(
            num_scalar_prefetch=1,
            grid=(depth // tile,),
            in_specs=[pl.BlockSpec((2, tile, half), lambda i, s: (0, i, 0))] * len(pieces)
            + [pl.BlockSpec(right.shape, lambda i, s: (0, 0), pipeline_mode=pl.Buffered(1))],
            out_specs=pl.BlockSpec((tile, width), lambda i, s: (i, 0)),
        ),
        out_shape=jax.ShapeDtypeStruct((depth, width), F32),
        compiler_params=params(40),
        cost_estimate=cost(8 * depth * width * half * cols, 20 * depth * width),
        name="rotate_part",
    )(me, *pieces, right)


def rotate_kernel(place_ref, part, *refs, count):
    pieces, (above, below, first, second, new_first, new_second, normed) = (
        refs[:count],
        refs[count:],
    )
    tile = first.shape[0]
    half = pieces[0].shape[2]
    rotated = part[...]
    for at, piece in enumerate(pieces):
        rows = pl.ds(at * half, half)
        last = jnp.where(place_ref[0] == 0, above[rows, :], below[rows, :])
        both = dot(piece[...].reshape(2 * tile, half), last, ((1,), (0,)))
        rotated = rotated + both[:tile] + both[tile:]
    one = BETA_ONE * first[...] + (1.0 - BETA_ONE) * rotated
    two = BETA_TWO * second[...] + (1.0 - BETA_TWO) * rotated * rotated
    new_first[...] = one
    new_second[...] = two
    high, low = kernel_split(one / (jnp.sqrt(two) + EPSILON))
    normed[0] = high
    normed[1] = low


def rotate(place, part, pieces, above, below, first, second):
    depth, width = first.shape
    half = pieces[0].shape[2]
    tile = min(256, depth)
    block = pl.BlockSpec((tile, width), lambda i, s: (i, 0))
    pair = pl.BlockSpec((2, tile, width), lambda i, s: (0, i, 0))
    whole = pl.BlockSpec(above.shape, lambda i, s: (0, 0), pipeline_mode=pl.Buffered(1))
    return pl.pallas_call(
        functools.partial(rotate_kernel, count=len(pieces)),
        grid_spec=pltpu.PrefetchScalarGridSpec(
            num_scalar_prefetch=1,
            grid=(depth // tile,),
            in_specs=[block]
            + [pl.BlockSpec((2, tile, half), lambda i, s: (0, i, 0))] * len(pieces)
            + [whole, whole, block, block],
            out_specs=[block, block, pair],
        ),
        out_shape=[
            jax.ShapeDtypeStruct((depth, width), F32),
            jax.ShapeDtypeStruct((depth, width), F32),
            jax.ShapeDtypeStruct((2, depth, width), BF16),
        ],
        compiler_params=params(36),
        cost_estimate=cost(4 * depth * width * half * len(pieces), 30 * depth * width),
        name="rotate",
    )(place, part, *pieces, above, below, first, second)


def restore_kernel(me_ref, normed, *refs, cols):
    rows, (keep, mate) = refs[:cols], refs[cols:]
    tile = normed.shape[1]
    both = normed[...].reshape(2 * tile, normed.shape[2])
    for distance in range(cols):
        term = dot(both, rows[distance][...], ((1,), (1,)))
        (mate if distance % 2 else keep)[distance // 2] = term[:tile] + term[tile:]


def restore(me, normed, right, chunk, piece, cols, width):
    _, depth, inner = normed.shape
    tile = min(512, depth)
    per = width // piece

    def at(distance):
        return lambda i, s: ((s[0] ^ distance) * per + chunk, 0)

    out = pl.BlockSpec((cols // 2, tile, piece), lambda i, s: (0, i, 0))
    return pl.pallas_call(
        functools.partial(restore_kernel, cols=cols),
        grid_spec=pltpu.PrefetchScalarGridSpec(
            num_scalar_prefetch=1,
            grid=(depth // tile,),
            in_specs=[pl.BlockSpec((2, tile, inner), lambda i, s: (0, i, 0))]
            + [pl.BlockSpec((piece, inner), at(d)) for d in range(cols)],
            out_specs=[out, out],
        ),
        out_shape=[jax.ShapeDtypeStruct((cols // 2, depth, piece), F32)] * 2,
        compiler_params=params(36),
        cost_estimate=cost(4 * depth * inner * piece * cols, 8 * depth * piece * cols),
        name="restore",
    )(me, normed, *([right] * cols))


TOP = 7.5


def encode(value, inverse):
    code = jnp.abs(value) * (inverse * 2.0**TOP)
    for _ in range(4):
        code = code * code
    return jnp.where(value < 0, -code, code).astype(BF16)


def decode(code, scale):
    code = code.astype(F32)
    size = jnp.abs(code)
    root = jnp.exp2(jnp.log2(size) * 0.0625 - TOP) * scale
    root = jnp.where(size > 0, root, 0.0)
    return jnp.where(code < 0, -root, root)


def scale_of(message, depth):
    return jnp.max(message[depth : depth + EXTRA, :].astype(F32), axis=(0, 1), keepdims=True)


def send_kernel(*refs, terms, tile):
    parts, (message, own, total) = refs[:terms], refs[terms:]
    depth, piece = total.shape

    def add(i, top):
        rows = pl.ds(pl.multiple_of(i * tile, tile), tile)
        value = parts[0][rows, :]
        for part in parts[1:]:
            value = value + part[rows, :]
        total[rows, :] = value
        high, low = kernel_split(value)
        own[rows, :piece] = high
        own[rows, piece:] = low
        return jnp.maximum(top, jnp.abs(value))

    top = lax.fori_loop(0, depth // tile, add, jnp.zeros((tile, piece), F32))
    top = jnp.maximum(jnp.max(top, axis=(0, 1), keepdims=True), 1e-30)
    scale = jnp.broadcast_to(top, (EXTRA, piece)).astype(BF16)
    message[depth : depth + EXTRA, :] = scale
    inverse = 1.0 / jnp.max(scale.astype(F32), axis=(0, 1), keepdims=True)

    def put(i, carry):
        rows = pl.ds(pl.multiple_of(i * tile, tile), tile)
        message[rows, :] = encode(total[rows, :], inverse)
        return carry

    lax.fori_loop(0, depth // tile, put, 0)


def send(parts):
    depth, piece = parts[0].shape
    tile = min(64, depth)
    return pl.pallas_call(
        functools.partial(send_kernel, terms=len(parts), tile=tile),
        out_shape=[
            jax.ShapeDtypeStruct((depth + EXTRA, piece), BF16),
            jax.ShapeDtypeStruct((depth, 2 * piece), BF16),
        ],
        scratch_shapes=[pltpu.VMEM((depth, piece), F32)],
        compiler_params=params(24),
        cost_estimate=cost(400 * depth * piece, 18 * depth * piece),
        name="send",
    )(*parts)


def update_kernel(place_ref, own, *refs, lines, tile):
    ups, downs = refs[: lines - 1], refs[lines - 1 : 2 * lines - 2]
    left, out, held = refs[2 * lines - 2], refs[-2], refs[-1]
    depth, piece = out.shape
    inner = held.shape[0]
    step = pl.program_id(0)

    @pl.when(step == 0)
    def _():
        held[...] = own[...]

    for back in range(1, lines):

        @pl.when(step == back)
        def _(back=back):
            up, down = ups[back - 1], downs[lines - back - 1]
            below = place_ref[0] >= back
            scale = jnp.where(below, scale_of(up, inner), scale_of(down, inner))

            def unpack(i, carry):
                rows = pl.ds(pl.multiple_of(i * tile, tile), tile)
                value = decode(jnp.where(below, up[rows, :], down[rows, :]), scale)
                high, low = kernel_split(value)
                held[rows, :piece] = high
                held[rows, piece:] = low
                return carry

            lax.fori_loop(0, inner // tile, unpack, 0)

    both = dot(left[...].reshape(depth, inner), held[...], ((1,), (0,)))
    term = both[:, :piece] + both[:, piece:]

    @pl.when(step == 0)
    def _():
        out[...] = term

    @pl.when(step > 0)
    def _():
        out[...] += term


def update_chunk(place, own, ups, downs, left, update, chunk, depth, width):
    cols, lines, quarter, inner = left.shape
    piece = own.shape[1] // 2
    tile = min(64, inner)
    message = pl.BlockSpec((inner + EXTRA, piece), lambda i, s: (0, 0))
    extra = [] if update is None else [update]
    return pl.pallas_call(
        functools.partial(update_kernel, lines=lines, tile=tile),
        grid_spec=pltpu.PrefetchScalarGridSpec(
            num_scalar_prefetch=1,
            grid=(lines,),
            in_specs=[pl.BlockSpec((inner, 2 * piece), lambda i, s: (0, 0))]
            + [message] * (2 * lines - 2)
            + [pl.BlockSpec((cols, 1, quarter, inner), lambda i, s: (0, i, 0, 0))]
            + [pl.BlockSpec(memory_space=pl.ANY)] * len(extra),
            out_specs=pl.BlockSpec((depth, piece), lambda i, s: (0, chunk)),
            scratch_shapes=[pltpu.VMEM((inner, 2 * piece), BF16)],
        ),
        out_shape=jax.ShapeDtypeStruct((depth, width), F32),
        input_output_aliases={2 * lines + 1: 0} if extra else {},
        compiler_params=params(36),
        cost_estimate=cost(4 * depth * inner * piece * lines, 12 * depth * piece * lines),
        name="update_chunk",
    )(place, own, *ups, *downs, left, *extra)


def build(lines, cols):
    def swap(value, distance):
        return lax.ppermute(value, "col", [(i, i ^ distance) for i in range(cols)])

    def up(value, senders):
        return lax.ppermute(value, "row", [(i, i + 1) for i in senders])

    def down(value, senders):
        return lax.ppermute(value, "row", [(i, i - 1) for i in senders])

    def spread(block):
        held = {0: block}
        for step in range(1, lines):
            held[-step] = up(held[1 - step], range(step - 1, lines - 1))
            held[step] = down(held[step - 1], range(1, lines - step + 1))
        return held

    def by_distance(block):
        held = {0: block}
        for distance in range(2, cols, 2):
            held[distance] = swap(block, distance)
        for distance in range(0, cols, 2):
            held[distance + 1] = swap(held[distance], 1)
        return held

    def place_by_distance(block, me):
        out = jnp.zeros((cols,) + block.shape, block.dtype)
        for distance, value in by_distance(block).items():
            out = lax.dynamic_update_index_in_dim(out, value, me ^ distance, 0)
        return out

    def local(gradient, first_moment, second_moment, left_basis, right_basis):
        me, place = lax.axis_index("col"), lax.axis_index("row")
        depth, width = gradient.shape
        half = width // 2
        index, spot = jnp.reshape(me, (1,)), jnp.reshape(place, (1,))
        far = lines - 1

        left = place_by_distance(left_basis, me).reshape(-1, left_basis.shape[1])
        pieces, arrived = {}, []
        near = [offset for offset in range(-far, far + 1) if abs(offset) < far]
        grads = [spread(gradient[:, side * half : (side + 1) * half]) for side in range(2)]
        for side in range(2):
            before = halfway(spot, left, grads[side], near, lines, None, False)
            whole = halfway(spot, left, grads[side], [-far, far], lines, before, True)
            for distance, value in by_distance(whole).items():
                pieces[distance, side] = value
            arrived.append((grads[side][far], grads[side][-far]))

        right = jnp.zeros(((lines + 1) * depth, width), BF16)
        ends = []
        for side in range(2):
            rows = lax.slice_in_dim(right_basis, side * depth // 2, (side + 1) * depth // 2)
            rows, arrived[side] = lax.optimization_barrier((rows, arrived[side]))
            rights = spread(rows)
            for offset in near:
                there = place + offset
                there = jnp.where((there >= 0) & (there < lines), there, lines)
                right = lax.dynamic_update_slice_in_dim(
                    right, rights[offset], there * depth + side * depth // 2, 0
                )
            ends.append((rights[far], rights[-far]))
        above = jnp.concatenate([end[0] for end in ends])
        below = jnp.concatenate([end[1] for end in ends])

        ordered = [pieces[distance, side] for distance in range(cols) for side in range(2)]
        part = rotate_part(index, ordered, right)
        span = depth // half
        lasts = []
        for at in range(span):
            chosen = None
            for distance in range(cols):
                for side in [at] if span == 2 else range(2):
                    value = pieces[distance, side]
                    here = (me ^ distance) * 2 + side == (far - place) * span + at
                    chosen = value if chosen is None else jnp.where(here, value, chosen)
            lasts.append(chosen)
        new_first, new_second, normed = rotate(
            spot, part, lasts, above, below, first_moment, second_moment
        )
        there = jnp.where((place == 0) | (place == far), far - place, lines)
        last = jnp.where(place == 0, above, below)
        right = lax.dynamic_update_slice_in_dim(right, last, there * depth, 0)

        left_late, last = lax.optimization_barrier((left, last))
        quarter = depth // cols
        backs = []
        for back in range(lines):
            to = lax.rem(place + back, lines)
            rows = lax.dynamic_slice_in_dim(left_late, to * depth + me * quarter, quarter, 0)
            if back:
                rows = lax.ppermute(rows, "row", [(i, (i + back) % lines) for i in range(lines)])
            backs.append(rows)
        backs = jnp.stack(backs)

        piece = width // CHUNKS
        update = None
        sums, messages, outgoing = [], [], []
        for chunk in range(CHUNKS):
            if chunk >= 2:
                normed, sums[chunk - 2] = lax.optimization_barrier((normed, sums[chunk - 2]))
            keep, mate = restore(index, normed, right, chunk, piece, cols, width)
            mate = swap(mate, 1)
            sums.append([keep[0], mate[0]] + [keep[d] + mate[d] for d in range(1, cols // 2)])
        for chunk in range(CHUNKS):
            parts = sums[chunk][:2]
            for at, value in enumerate(sums[chunk][2:]):
                parts.append(swap(value, 2 * at + 2))
            if chunk == 1:
                backs, parts = lax.optimization_barrier((backs, parts))
            message, own = send(parts)
            messages.append(message)
            outgoing.append(own)
        left_rows = place_by_distance(backs, me)
        for chunk in range(CHUNKS):
            arrived = spread(messages[chunk])
            ups = [arrived[-step] for step in range(1, lines)]
            downs = [arrived[step] for step in range(1, lines)]
            update = update_chunk(
                spot, outgoing[chunk], ups, downs, left_rows, update, chunk, depth, width
            )
        return (new_first, new_second, update)

    return local


def solution(mesh):
    return jax.shard_map(
        build(mesh.shape["row"], mesh.shape["col"]),
        mesh=mesh,
        in_specs=(
            P(("groups", "row"), "col"),
            P(("groups", "row"), "col"),
            P(("groups", "row"), "col"),
            P(("groups", "col"), "row"),
            P(("groups", "row"), "col"),
        ),
        out_specs=(
            P(("groups", "row"), "col"),
            P(("groups", "row"), "col"),
            P(("groups", "row"), "col"),
        ),
        check_vma=False,
    )
```

```python
import functools
import jax
import jax.numpy as jnp
from jax import lax
from jax.experimental import pallas as pl
from jax.experimental.pallas import tpu as pltpu
from jax.sharding import PartitionSpec as P

BETA_ONE = 0.9
BETA_TWO = 0.95
EPSILON = 1e-08
CHUNKS = 4
EXTRA = 16
F32 = jnp.float32
BF16 = jnp.bfloat16
MIB = 2**20


def params(mib):
    return pltpu.CompilerParams(vmem_limit_bytes=mib * MIB)


def cost(flops, moved):
    return pl.CostEstimate(flops=int(flops) // 100, bytes_accessed=int(moved) // 100, transcendentals=0)


def split(value):
    high = lax.reduce_precision(value, exponent_bits=8, mantissa_bits=7)
    return high.astype(BF16), (value - high).astype(BF16)


def kernel_split(value):
    high = value.astype(BF16)
    return high, (value - high.astype(F32)).astype(BF16)


def dot(a, b, dims):
    return lax.dot_general(a, b, (dims, ((), ())), preferred_element_type=F32)


def flip_kernel(me_ref, rows, out):
    out[...] = rows[...].T


def flip(me, rows, cols):
    piece, width = rows.shape[0] // cols, rows.shape[1]
    return pl.pallas_call(
        flip_kernel,
        grid_spec=pltpu.PrefetchScalarGridSpec(
            num_scalar_prefetch=1,
            grid=(cols,),
            in_specs=[pl.BlockSpec((piece, width), lambda d, s: (s[0] ^ d, 0))],
            out_specs=pl.BlockSpec((width, piece), lambda d, s: (0, d)),
        ),
        out_shape=jax.ShapeDtypeStruct((width, cols * piece), BF16),
        compiler_params=params(16),
        cost_estimate=cost(0, 4 * rows.size),
        name="flip",
    )(me, rows)


def rotate_part_kernel(me_ref, *refs, cols, count, piece):
    pieces, refs = refs[:cols], refs[cols:]
    parts, (out, rows) = refs[:count], refs[count:]
    tile = out.shape[0]

    @pl.when(pl.program_id(0) == 0)
    def _():
        for distance in range(cols):
            start = pl.multiple_of((me_ref[0] ^ distance) * piece, piece)
            for at, part in enumerate(parts):
                rows[distance, pl.ds(at * piece, piece), :] = part[pl.ds(start, piece), :]

    total = None
    for distance in range(cols):
        both = pieces[distance][...].reshape(2 * tile, count * piece)
        term = dot(both, rows[distance], ((1,), (0,)))
        total = term if total is None else total + term
    out[...] = total[:tile] + total[tile:]


def rotate_part(me, pieces, parts):
    cols, count = len(pieces), len(parts)
    _, depth, _ = pieces[0].shape
    piece, width = parts[0].shape[0] // cols, parts[0].shape[1]
    tile = min(256, depth)
    whole = pl.BlockSpec(parts[0].shape, lambda i, s: (0, 0), pipeline_mode=pl.Buffered(1))
    return pl.pallas_call(
        functools.partial(rotate_part_kernel, cols=cols, count=count, piece=piece),
        grid_spec=pltpu.PrefetchScalarGridSpec(
            num_scalar_prefetch=1,
            grid=(depth // tile,),
            in_specs=[pl.BlockSpec((2, tile, count * piece), lambda i, s: (0, i, 0))] * cols
            + [whole] * count,
            out_specs=pl.BlockSpec((tile, width), lambda i, s: (i, 0)),
            scratch_shapes=[pltpu.VMEM((cols, count * piece, width), BF16)],
        ),
        out_shape=jax.ShapeDtypeStruct((depth, width), F32),
        compiler_params=params(44),
        cost_estimate=cost(4 * depth * width * piece * count * cols, 20 * depth * width),
        name="rotate_part",
    )(me, *pieces, *parts)


def rotate_kernel(me_ref, part, *refs, cols, piece):
    pieces, (right, first, second, new_first, new_second, normed) = refs[:cols], refs[cols:]
    tile = first.shape[0]
    total = None
    for distance in range(cols):
        start = pl.multiple_of((me_ref[0] ^ distance) * piece, piece)
        both = pieces[distance][...].reshape(2 * tile, piece)
        term = dot(both, right[pl.ds(start, piece), :], ((1,), (0,)))
        total = term if total is None else total + term
    rotated = part[...] + total[:tile] + total[tile:]
    one = BETA_ONE * first[...] + (1.0 - BETA_ONE) * rotated
    two = BETA_TWO * second[...] + (1.0 - BETA_TWO) * rotated * rotated
    new_first[...] = one
    new_second[...] = two
    high, low = kernel_split(one / (jnp.sqrt(two) + EPSILON))
    normed[0] = high
    normed[1] = low


def rotate(me, part, pieces, right, first, second):
    cols = len(pieces)
    depth, width = first.shape
    piece = right.shape[0] // cols
    tile = min(256, depth)
    final = width // piece - 1
    block = pl.BlockSpec((tile, width), lambda i, s: (i, 0))
    pair = pl.BlockSpec((2, tile, width), lambda i, s: (0, i, 0))
    return pl.pallas_call(
        functools.partial(rotate_kernel, cols=cols, piece=piece),
        grid_spec=pltpu.PrefetchScalarGridSpec(
            num_scalar_prefetch=1,
            grid=(depth // tile,),
            in_specs=[block]
            + [pl.BlockSpec((2, tile, piece), lambda i, s: (0, i, final))] * cols
            + [
                pl.BlockSpec(right.shape, lambda i, s: (0, 0), pipeline_mode=pl.Buffered(1)),
                block,
                block,
            ],
            out_specs=[block, block, pair],
        ),
        out_shape=[
            jax.ShapeDtypeStruct((depth, width), F32),
            jax.ShapeDtypeStruct((depth, width), F32),
            jax.ShapeDtypeStruct((2, depth, width), BF16),
        ],
        compiler_params=params(32),
        cost_estimate=cost(4 * depth * width * piece * cols, 30 * depth * width),
        name="rotate",
    )(me, part, *pieces, right, first, second)


def restore_kernel(normed, flipped, keep, mate, *, cols):
    tile = normed.shape[1]
    piece = keep.shape[2]
    both = dot(normed[...].reshape(2 * tile, normed.shape[2]), flipped[...], ((1,), (0,)))
    term = both[:tile] + both[tile:]
    for distance in range(cols):
        out = mate if distance % 2 else keep
        out[distance // 2] = term[:, distance * piece : (distance + 1) * piece]


def restore(normed, flipped, cols):
    _, depth, inner = normed.shape
    piece = flipped.shape[1] // cols
    tile = min(256, depth)
    out = pl.BlockSpec((cols // 2, tile, piece), lambda i: (0, i, 0))
    return pl.pallas_call(
        functools.partial(restore_kernel, cols=cols),
        grid=(depth // tile,),
        in_specs=[
            pl.BlockSpec((2, tile, inner), lambda i: (0, i, 0)),
            pl.BlockSpec(flipped.shape, lambda i: (0, 0), pipeline_mode=pl.Buffered(1)),
        ],
        out_specs=[out, out],
        out_shape=[jax.ShapeDtypeStruct((cols // 2, depth, piece), F32)] * 2,
        compiler_params=params(24),
        cost_estimate=cost(4 * depth * inner * piece * cols, 8 * depth * piece * cols),
        name="restore",
    )(normed, flipped)


TOP = 7.5


def encode(value, inverse):
    code = jnp.abs(value) * (inverse * 2.0**TOP)
    for _ in range(4):
        code = code * code
    return jnp.where(value < 0, -code, code).astype(BF16)


def decode(code, scale):
    code = code.astype(F32)
    size = jnp.abs(code)
    root = jnp.exp2(jnp.log2(size) * 0.0625 - TOP) * scale
    root = jnp.where(size > 0, root, 0.0)
    return jnp.where(code < 0, -root, root)


def scale_of(message, depth):
    return jnp.max(message[depth : depth + EXTRA, :].astype(F32), axis=(0, 1), keepdims=True)


def send_kernel(*refs, terms, tile):
    parts, (message, total) = refs[:terms], refs[terms:]
    depth, piece = total.shape

    def add(i, top):
        rows = pl.ds(pl.multiple_of(i * tile, tile), tile)
        value = parts[0][rows, :]
        for part in parts[1:]:
            value = value + part[rows, :]
        total[rows, :] = value
        return jnp.maximum(top, jnp.abs(value))

    top = lax.fori_loop(0, depth // tile, add, jnp.zeros((tile, piece), F32))
    top = jnp.maximum(jnp.max(top, axis=(0, 1), keepdims=True), 1e-30)
    scale = jnp.broadcast_to(top, (EXTRA, piece)).astype(BF16)
    message[depth : depth + EXTRA, :] = scale
    inverse = 1.0 / jnp.max(scale.astype(F32), axis=(0, 1), keepdims=True)

    def put(i, carry):
        rows = pl.ds(pl.multiple_of(i * tile, tile), tile)
        message[rows, :] = encode(total[rows, :], inverse)
        return carry

    lax.fori_loop(0, depth // tile, put, 0)


def send(parts):
    depth, piece = parts[0].shape
    tile = min(64, depth)
    return pl.pallas_call(
        functools.partial(send_kernel, terms=len(parts), tile=tile),
        out_shape=jax.ShapeDtypeStruct((depth + EXTRA, piece), BF16),
        scratch_shapes=[pltpu.VMEM((depth, piece), F32)],
        compiler_params=params(24),
        cost_estimate=cost(400 * depth * piece, 18 * depth * piece),
        name="send",
    )(*parts)


def update_kernel(place_ref, message, left, *refs, tile):
    out, held = refs[-2:]
    depth, piece = out.shape
    inner = held.shape[0]
    scale = scale_of(message, inner)

    def unpack(i, carry):
        rows = pl.ds(pl.multiple_of(i * tile, tile), tile)
        high, low = kernel_split(decode(message[rows, :], scale))
        held[rows, :piece] = high
        held[rows, piece:] = low
        return carry

    lax.fori_loop(0, inner // tile, unpack, 0)
    both = dot(left[...].reshape(depth, inner), held[...], ((1,), (0,)))
    term = both[:, :piece] + both[:, piece:]

    @pl.when(pl.program_id(0) == 0)
    def _():
        out[...] = term

    @pl.when(pl.program_id(0) > 0)
    def _():
        out[...] += term


def update_chunk(place, messages, left, update, chunk, depth, width):
    cols, lines, quarter, inner = left.shape
    piece = messages.shape[1]
    tile = min(64, inner)
    extra = [] if update is None else [update]
    return pl.pallas_call(
        functools.partial(update_kernel, tile=tile),
        grid_spec=pltpu.PrefetchScalarGridSpec(
            num_scalar_prefetch=1,
            grid=(lines,),
            in_specs=[
                pl.BlockSpec((inner + EXTRA, piece), lambda i, s: (i, 0)),
                pl.BlockSpec(
                    (cols, 1, quarter, inner),
                    lambda i, s: (0, lax.rem(s[0] + lines - i, lines), 0, 0),
                ),
            ]
            + [pl.BlockSpec(memory_space=pl.ANY)] * len(extra),
            out_specs=pl.BlockSpec((depth, piece), lambda i, s: (0, chunk)),
            scratch_shapes=[pltpu.VMEM((inner, 2 * piece), BF16)],
        ),
        out_shape=jax.ShapeDtypeStruct((depth, width), F32),
        input_output_aliases={3: 0} if extra else {},
        compiler_params=params(24),
        cost_estimate=cost(4 * depth * inner * piece * lines, 12 * depth * piece * lines),
        name="update_chunk",
    )(place, messages, left, *extra)


def build(lines, cols):
    def swap(value, distance):
        return lax.ppermute(value, "col", [(i, i ^ distance) for i in range(cols)])

    def by_distance(block):
        held = {0: block}
        for distance in range(2, cols, 2):
            held[distance] = swap(block, distance)
        for distance in range(0, cols, 2):
            held[distance + 1] = swap(held[distance], 1)
        return held

    def place_by_distance(block, me):
        out = jnp.zeros((cols,) + block.shape, block.dtype)
        for distance, value in by_distance(block).items():
            out = lax.dynamic_update_index_in_dim(out, value, me ^ distance, 0)
        return out

    def gather_row(value):
        return lax.all_gather(value, "row", axis=0, tiled=True)

    def local(gradient, first_moment, second_moment, left_basis, right_basis):
        me, place = lax.axis_index("col"), lax.axis_index("row")
        depth, width = gradient.shape
        piece = width // CHUNKS
        index, spot = jnp.reshape(me, (1,)), jnp.reshape(place, (1,))

        gradients = gather_row(gradient)
        if depth == width:
            parts = [
                gather_row(lax.slice_in_dim(right_basis, p * piece, (p + 1) * piece))
                for p in range(CHUNKS)
            ]
        else:
            blocks = gather_row(right_basis).reshape(cols, CHUNKS, piece, width)
            parts = [blocks[:, p].reshape(cols * piece, width) for p in range(CHUNKS)]

        left = place_by_distance(left_basis, me).reshape(-1, left_basis.shape[1])
        halfway = dot(left, gradients, ((0,), (0,)))
        pieces = by_distance(jnp.stack(split(halfway)))
        pieces = [pieces[distance] for distance in range(cols)]

        flipped = [flip(index, part, cols) for part in parts]
        part = rotate_part(index, pieces, parts[:-1])
        new_first, new_second, normed = rotate(
            index, part, pieces, parts[-1], first_moment, second_moment
        )

        left_late, parts[-1] = lax.optimization_barrier((left, parts[-1]))
        quarter = depth // cols
        backs = []
        for back in range(lines):
            to = lax.rem(place + back, lines)
            rows = lax.dynamic_slice_in_dim(left_late, to * depth + me * quarter, quarter, 0)
            if back:
                rows = lax.ppermute(rows, "row", [(i, (i + back) % lines) for i in range(lines)])
            backs.append(rows)
        backs = jnp.stack(backs)

        sums, messages = [], []
        for chunk in range(CHUNKS):
            if chunk >= 2:
                normed, sums[chunk - 2] = lax.optimization_barrier((normed, sums[chunk - 2]))
            keep, mate = restore(normed, flipped[chunk], cols)
            mate = swap(mate, 1)
            sums.append([keep[0], mate[0]] + [keep[d] + mate[d] for d in range(1, cols // 2)])
        for chunk in range(CHUNKS):
            terms = sums[chunk][:2]
            for at, value in enumerate(sums[chunk][2:]):
                terms.append(swap(value, 2 * at + 2))
            if chunk == 1:
                backs, terms = lax.optimization_barrier((backs, terms))
            messages.append(gather_row(send(terms)))
        left_rows = place_by_distance(backs, me)
        update = None
        for chunk in range(CHUNKS):
            update = update_chunk(spot, messages[chunk], left_rows, update, chunk, depth, width)
        return (new_first, new_second, update)

    return local


def solution(mesh):
    return jax.shard_map(
        build(mesh.shape["row"], mesh.shape["col"]),
        mesh=mesh,
        in_specs=(
            P(("groups", "row"), "col"),
            P(("groups", "row"), "col"),
            P(("groups", "row"), "col"),
            P(("groups", "col"), "row"),
            P(("groups", "row"), "col"),
        ),
        out_specs=(
            P(("groups", "row"), "col"),
            P(("groups", "row"), "col"),
            P(("groups", "row"), "col"),
        ),
        check_vma=False,
    )
```

```python
import functools
import jax
import jax.numpy as jnp
from jax import lax
from jax.experimental import pallas as pl
from jax.experimental.pallas import tpu as pltpu
from jax.sharding import PartitionSpec as P

BETA_ONE = 0.9
BETA_TWO = 0.95
EPSILON = 1e-08
CHUNKS = 4
EXTRA = 16
F32 = jnp.float32
BF16 = jnp.bfloat16
MIB = 2**20


def params(mib):
    return pltpu.CompilerParams(vmem_limit_bytes=mib * MIB)


def cost(flops, moved):
    return pl.CostEstimate(flops=int(flops) // 100, bytes_accessed=int(moved) // 100, transcendentals=0)


def split(value):
    high = lax.reduce_precision(value, exponent_bits=8, mantissa_bits=7)
    return high.astype(BF16), (value - high).astype(BF16)


def kernel_split(value):
    high = value.astype(BF16)
    return high, (value - high.astype(F32)).astype(BF16)


def dot(a, b, dims):
    return lax.dot_general(a, b, (dims, ((), ())), preferred_element_type=F32)


def flip_kernel(me_ref, rows, out):
    out[...] = rows[...].T


def flip(me, rows, cols, count=1, at=0):
    piece, width = rows.shape[0] // cols // count, rows.shape[1]
    return pl.pallas_call(
        flip_kernel,
        grid_spec=pltpu.PrefetchScalarGridSpec(
            num_scalar_prefetch=1,
            grid=(cols,),
            in_specs=[pl.BlockSpec((piece, width), lambda d, s: ((s[0] ^ d) * count + at, 0))],
            out_specs=pl.BlockSpec((width, piece), lambda d, s: (0, d)),
        ),
        out_shape=jax.ShapeDtypeStruct((width, cols * piece), BF16),
        compiler_params=params(16),
        cost_estimate=cost(0, 4 * piece * cols * width),
        name="flip",
    )(me, rows)


def rotate_part_kernel(me_ref, *refs, cols, sizes):
    pieces, refs = refs[:cols], refs[cols:]
    parts, (out, rows) = refs[: len(sizes)], refs[len(sizes) :]
    tile = out.shape[0]

    @pl.when(pl.program_id(0) == 0)
    def _():
        for distance in range(cols):
            at = 0
            for size, part in zip(sizes, parts):
                start = pl.multiple_of((me_ref[0] ^ distance) * size, size)
                rows[distance, pl.ds(at, size), :] = part[pl.ds(start, size), :]
                at += size

    total = None
    for distance in range(cols):
        both = pieces[distance][...].reshape(2 * tile, sum(sizes))
        term = dot(both, rows[distance], ((1,), (0,)))
        total = term if total is None else total + term
    out[...] = total[:tile] + total[tile:]


def rotate_part(me, pieces, parts):
    cols = len(pieces)
    _, depth, _ = pieces[0].shape
    width = parts[0].shape[1]
    sizes = [part.shape[0] // cols for part in parts]
    tile = min(256, depth)
    return pl.pallas_call(
        functools.partial(rotate_part_kernel, cols=cols, sizes=sizes),
        grid_spec=pltpu.PrefetchScalarGridSpec(
            num_scalar_prefetch=1,
            grid=(depth // tile,),
            in_specs=[pl.BlockSpec((2, tile, sum(sizes)), lambda i, s: (0, i, 0))] * cols
            + [
                pl.BlockSpec(part.shape, lambda i, s: (0, 0), pipeline_mode=pl.Buffered(1))
                for part in parts
            ],
            out_specs=pl.BlockSpec((tile, width), lambda i, s: (i, 0)),
            scratch_shapes=[pltpu.VMEM((cols, sum(sizes), width), BF16)],
        ),
        out_shape=jax.ShapeDtypeStruct((depth, width), F32),
        compiler_params=params(44),
        cost_estimate=cost(4 * depth * width * sum(sizes) * cols, 20 * depth * width),
        name="rotate_part",
    )(me, *pieces, *parts)


def rotate_kernel(me_ref, part, *refs, cols, piece):
    pieces, (right, first, second, new_first, new_second, normed) = refs[:cols], refs[cols:]
    tile = first.shape[0]
    total = None
    for distance in range(cols):
        start = pl.multiple_of((me_ref[0] ^ distance) * piece, piece)
        both = pieces[distance][...].reshape(2 * tile, piece)
        term = dot(both, right[pl.ds(start, piece), :], ((1,), (0,)))
        total = term if total is None else total + term
    rotated = part[...] + total[:tile] + total[tile:]
    one = BETA_ONE * first[...] + (1.0 - BETA_ONE) * rotated
    two = BETA_TWO * second[...] + (1.0 - BETA_TWO) * rotated * rotated
    new_first[...] = one
    new_second[...] = two
    high, low = kernel_split(one / (jnp.sqrt(two) + EPSILON))
    normed[0] = high
    normed[1] = low


def rotate(me, part, pieces, right, first, second):
    cols = len(pieces)
    depth, width = first.shape
    piece = right.shape[0] // cols
    tile = min(256, depth)
    final = width // piece - 1
    block = pl.BlockSpec((tile, width), lambda i, s: (i, 0))
    pair = pl.BlockSpec((2, tile, width), lambda i, s: (0, i, 0))
    return pl.pallas_call(
        functools.partial(rotate_kernel, cols=cols, piece=piece),
        grid_spec=pltpu.PrefetchScalarGridSpec(
            num_scalar_prefetch=1,
            grid=(depth // tile,),
            in_specs=[block]
            + [pl.BlockSpec((2, tile, piece), lambda i, s: (0, i, final))] * cols
            + [
                pl.BlockSpec(right.shape, lambda i, s: (0, 0), pipeline_mode=pl.Buffered(1)),
                block,
                block,
            ],
            out_specs=[block, block, pair],
        ),
        out_shape=[
            jax.ShapeDtypeStruct((depth, width), F32),
            jax.ShapeDtypeStruct((depth, width), F32),
            jax.ShapeDtypeStruct((2, depth, width), BF16),
        ],
        compiler_params=params(44),
        cost_estimate=cost(4 * depth * width * piece * cols, 30 * depth * width),
        name="rotate",
    )(me, part, *pieces, right, first, second)


def restore_kernel(normed, flipped, keep, mate, *, cols):
    tile = normed.shape[1]
    piece = keep.shape[2]
    both = dot(normed[...].reshape(2 * tile, normed.shape[2]), flipped[...], ((1,), (0,)))
    term = both[:tile] + both[tile:]
    for distance in range(cols):
        out = mate if distance % 2 else keep
        out[distance // 2] = term[:, distance * piece : (distance + 1) * piece]


def restore(normed, flipped, cols):
    _, depth, inner = normed.shape
    piece = flipped.shape[1] // cols
    tile = min(256, depth)
    out = pl.BlockSpec((cols // 2, tile, piece), lambda i: (0, i, 0))
    return pl.pallas_call(
        functools.partial(restore_kernel, cols=cols),
        grid=(depth // tile,),
        in_specs=[
            pl.BlockSpec((2, tile, inner), lambda i: (0, i, 0)),
            pl.BlockSpec(flipped.shape, lambda i: (0, 0), pipeline_mode=pl.Buffered(1)),
        ],
        out_specs=[out, out],
        out_shape=[jax.ShapeDtypeStruct((cols // 2, depth, piece), F32)] * 2,
        compiler_params=params(24),
        cost_estimate=cost(4 * depth * inner * piece * cols, 8 * depth * piece * cols),
        name="restore",
    )(normed, flipped)


TOP = 7.5


def encode(value, inverse):
    code = jnp.abs(value) * (inverse * 2.0**TOP)
    for _ in range(4):
        code = code * code
    return jnp.where(value < 0, -code, code).astype(BF16)


def decode(code, scale):
    code = code.astype(F32)
    size = jnp.abs(code)
    root = jnp.exp2(jnp.log2(size) * 0.0625 - TOP) * scale
    root = jnp.where(size > 0, root, 0.0)
    return jnp.where(code < 0, -root, root)


def scale_of(message, depth):
    return jnp.max(message[depth : depth + EXTRA, :].astype(F32), axis=(0, 1), keepdims=True)


def fill(message, total, value_at, tile):
    depth, piece = total.shape

    def add(i, top):
        rows = pl.ds(pl.multiple_of(i * tile, tile), tile)
        value = value_at(rows)
        total[rows, :] = value
        return jnp.maximum(top, jnp.abs(value))

    top = lax.fori_loop(0, depth // tile, add, jnp.zeros((tile, piece), F32))
    top = jnp.maximum(jnp.max(top, axis=(0, 1), keepdims=True), 1e-30)
    scale = jnp.broadcast_to(top, (EXTRA, piece)).astype(BF16)
    message[depth : depth + EXTRA, :] = scale
    inverse = 1.0 / jnp.max(scale.astype(F32), axis=(0, 1), keepdims=True)

    def put(i, carry):
        rows = pl.ds(pl.multiple_of(i * tile, tile), tile)
        message[rows, :] = encode(total[rows, :], inverse)
        return carry

    lax.fori_loop(0, depth // tile, put, 0)


def summed(keep, mate, codes):
    depth = keep.shape[1]
    scales = [scale_of(code, depth) for code in codes]

    def value_at(rows):
        value = keep[0, rows, :] + mate[0, rows, :]
        for code, scale in zip(codes, scales):
            value = value + decode(code[rows, :], scale)
        return value

    return value_at


def send_kernel(keep, mate, *refs, tile):
    codes, (message, total) = refs[:-2], refs[-2:]
    fill(message, total, summed(keep, mate, codes), tile)


def send(keep, mate, distance, codes):
    _, depth, piece = keep.shape
    tile = min(64, depth)
    pair = pl.BlockSpec((1, depth, piece), lambda i: (distance // 2, 0, 0))
    message = pl.BlockSpec((depth + EXTRA, piece), lambda i: (0, 0))
    return pl.pallas_call(
        functools.partial(send_kernel, tile=tile),
        grid=(1,),
        in_specs=[pair, pair] + [message] * len(codes),
        out_specs=message,
        out_shape=jax.ShapeDtypeStruct((depth + EXTRA, piece), BF16),
        scratch_shapes=[pltpu.VMEM((depth, piece), F32)],
        compiler_params=params(16),
        cost_estimate=cost(400 * depth * piece, 18 * depth * piece),
        name="send",
    )(keep, mate, *codes)


def expand_kernel(keep, mate, *refs, tile):
    codes, (left, out, both) = refs[:-3], refs[-3:]
    depth, piece = both.shape[0], out.shape[1]

    @pl.when(pl.program_id(0) == 0)
    def _():
        value_at = summed(keep, mate, codes)

        def put(i, carry):
            rows = pl.ds(pl.multiple_of(i * tile, tile), tile)
            high, low = kernel_split(value_at(rows))
            both[rows, :piece] = high
            both[rows, piece:] = low
            return carry

        lax.fori_loop(0, depth // tile, put, 0)

    product = dot(left[...], both[...], ((1,), (0,)))
    out[...] = product[:, :piece] + product[:, piece:]


def expand(keep, mate, codes, left):
    rows, inner = left.shape
    _, depth, piece = keep.shape
    step = min(1024, rows)
    pair = pl.BlockSpec((1, depth, piece), lambda i: (0, 0, 0))
    message = pl.BlockSpec((depth + EXTRA, piece), lambda i: (0, 0))
    return pl.pallas_call(
        functools.partial(expand_kernel, tile=min(64, depth)),
        grid=(rows // step,),
        in_specs=[pair, pair]
        + [message] * len(codes)
        + [pl.BlockSpec((step, inner), lambda i: (i, 0))],
        out_specs=pl.BlockSpec((step, piece), lambda i: (i, 0)),
        out_shape=jax.ShapeDtypeStruct((rows, piece), F32),
        scratch_shapes=[pltpu.VMEM((depth, 2 * piece), BF16)],
        compiler_params=params(36),
        cost_estimate=cost(4 * rows * inner * piece, 4 * rows * piece + 2 * rows * inner),
        name="expand",
    )(keep, mate, *codes, left)


def hop_kernel(place_ref, *refs, lines, step, tile):
    blocks, refs = refs[:2], refs[2:]
    arrived, outs, total = refs[:-3], refs[-3:-1], refs[-1]
    depth = total.shape[0]
    sends = (place_ref[0] < step, place_ref[0] >= lines - step)
    for way in range(2):

        @pl.when(sends[way])
        def _(way=way):
            scale = scale_of(arrived[way], depth) if arrived else None

            def value_at(rows):
                value = blocks[way][rows, :]
                if arrived:
                    value = value + decode(arrived[way][rows, :], scale)
                return value

            fill(outs[way], total, value_at, tile)


def hop(place, product, arrived, lines, step):
    depth, piece = product.shape[0] // lines, product.shape[1]
    ahead = lines - step
    message = pl.BlockSpec((depth + EXTRA, piece), lambda i, s: (0, 0))
    return pl.pallas_call(
        functools.partial(hop_kernel, lines=lines, step=step, tile=min(64, depth)),
        grid_spec=pltpu.PrefetchScalarGridSpec(
            num_scalar_prefetch=1,
            grid=(1,),
            in_specs=[
                pl.BlockSpec(
                    (depth, piece), lambda i, s: (jnp.minimum(s[0] + ahead, lines - 1), 0)
                ),
                pl.BlockSpec((depth, piece), lambda i, s: (jnp.maximum(s[0] - ahead, 0), 0)),
            ]
            + [message] * len(arrived),
            out_specs=[message] * 2,
            scratch_shapes=[pltpu.VMEM((depth, piece), F32)],
        ),
        out_shape=[jax.ShapeDtypeStruct((depth + EXTRA, piece), BF16)] * 2,
        compiler_params=params(16),
        cost_estimate=cost(400 * depth * piece, 12 * depth * piece),
        name="hop",
    )(place, product, product, *arrived)


def finish_kernel(at_ref, block, up, down, *refs, tile):
    out = refs[-1]
    depth = out.shape[0]
    scales = [scale_of(message, depth) for message in (up, down)]

    def add(i, carry):
        rows = pl.ds(pl.multiple_of(i * tile, tile), tile)
        out[rows, :] = (
            block[rows, :] + decode(up[rows, :], scales[0]) + decode(down[rows, :], scales[1])
        )
        return carry

    lax.fori_loop(0, depth // tile, add, 0)


def finish(at, product, arrived, update, chunk, depth, width):
    piece = product.shape[1]
    tile = min(64, depth)
    message = pl.BlockSpec((depth + EXTRA, piece), lambda i, s: (0, 0))
    extra = [] if update is None else [update]
    return pl.pallas_call(
        functools.partial(finish_kernel, tile=tile),
        grid_spec=pltpu.PrefetchScalarGridSpec(
            num_scalar_prefetch=1,
            grid=(1,),
            in_specs=[pl.BlockSpec((depth, piece), lambda i, s: (s[0], 0)), message, message]
            + [pl.BlockSpec(memory_space=pl.ANY)] * len(extra),
            out_specs=pl.BlockSpec((depth, piece), lambda i, s: (0, chunk)),
        ),
        out_shape=jax.ShapeDtypeStruct((depth, width), F32),
        input_output_aliases={4: 0} if extra else {},
        compiler_params=params(16),
        cost_estimate=cost(400 * depth * piece, 12 * depth * piece),
        name="finish",
    )(at, product, *arrived, *extra)


def update_kernel(place_ref, message, left, *refs, tile):
    out, held = refs[-2:]
    depth, piece = out.shape
    inner = held.shape[0]
    scale = scale_of(message, inner)

    def unpack(i, carry):
        rows = pl.ds(pl.multiple_of(i * tile, tile), tile)
        high, low = kernel_split(decode(message[rows, :], scale))
        held[rows, :piece] = high
        held[rows, piece:] = low
        return carry

    lax.fori_loop(0, inner // tile, unpack, 0)
    both = dot(left[...].reshape(depth, inner), held[...], ((1,), (0,)))
    term = both[:, :piece] + both[:, piece:]

    @pl.when(pl.program_id(0) == 0)
    def _():
        out[...] = term

    @pl.when(pl.program_id(0) > 0)
    def _():
        out[...] += term


def update_chunk(place, messages, left, update, chunk, depth, width):
    cols, lines, quarter, inner = left.shape
    piece = messages.shape[1]
    tile = min(64, inner)
    extra = [] if update is None else [update]
    return pl.pallas_call(
        functools.partial(update_kernel, tile=tile),
        grid_spec=pltpu.PrefetchScalarGridSpec(
            num_scalar_prefetch=1,
            grid=(lines,),
            in_specs=[
                pl.BlockSpec((inner + EXTRA, piece), lambda i, s: (i, 0)),
                pl.BlockSpec(
                    (cols, 1, quarter, inner),
                    lambda i, s: (0, lax.rem(s[0] + lines - i, lines), 0, 0),
                ),
            ]
            + [pl.BlockSpec(memory_space=pl.ANY)] * len(extra),
            out_specs=pl.BlockSpec((depth, piece), lambda i, s: (0, chunk)),
            scratch_shapes=[pltpu.VMEM((inner, 2 * piece), BF16)],
        ),
        out_shape=jax.ShapeDtypeStruct((depth, width), F32),
        input_output_aliases={3: 0} if extra else {},
        compiler_params=params(40),
        cost_estimate=cost(4 * depth * inner * piece * lines, 12 * depth * piece * lines),
        name="update_chunk",
    )(place, messages, left, *extra)


def build(lines, cols):
    def swap(value, distance):
        return lax.ppermute(value, "col", [(i, i ^ distance) for i in range(cols)])

    def by_distance(block):
        held = {0: block}
        for distance in range(2, cols, 2):
            held[distance] = swap(block, distance)
        for distance in range(0, cols, 2):
            held[distance + 1] = swap(held[distance], 1)
        return held

    def place_by_distance(block, me):
        out = jnp.zeros((cols,) + block.shape, block.dtype)
        for distance, value in by_distance(block).items():
            out = lax.dynamic_update_index_in_dim(out, value, me ^ distance, 0)
        return out

    def gather_row(value):
        return lax.all_gather(value, "row", axis=0, tiled=True)

    def up(value, senders):
        return lax.ppermute(value, "row", [(i, i + 1) for i in senders])

    def down(value, senders):
        return lax.ppermute(value, "row", [(i, i - 1) for i in senders])

    def local(gradient, first_moment, second_moment, left_basis, right_basis):
        me, place = lax.axis_index("col"), lax.axis_index("row")
        depth, width = gradient.shape
        piece = width // CHUNKS
        index, spot = jnp.reshape(me, (1,)), jnp.reshape(place, (1,))

        gradients = gather_row(gradient)
        early = CHUNKS - 1
        if depth == width:
            near = gather_row(lax.slice_in_dim(right_basis, 0, early * piece))
            final = gather_row(lax.slice_in_dim(right_basis, early * piece, width))
        else:
            blocks = gather_row(right_basis).reshape(cols, CHUNKS, piece, width)
            near = blocks[:, :early].reshape(early * cols * piece, width)
            final = blocks[:, early].reshape(cols * piece, width)

        left = place_by_distance(left_basis, me).reshape(-1, left_basis.shape[1])
        quarter = depth // cols
        backs = []
        for back in range(lines):
            to = lax.rem(place + back, lines)
            rows = lax.dynamic_slice_in_dim(left, to * depth + me * quarter, quarter, 0)
            if back:
                rows = lax.ppermute(rows, "row", [(i, (i + back) % lines) for i in range(lines)])
            backs.append(rows)
        left_rows = place_by_distance(jnp.stack(backs), me)
        left, left_rows = lax.optimization_barrier((left, left_rows))

        halfway = dot(left, gradients, ((0,), (0,)))
        pieces = by_distance(jnp.stack(split(halfway)))
        pieces = [pieces[distance] for distance in range(cols)]

        flipped = [flip(index, near, cols, early, at) for at in range(early)]
        flipped.append(flip(index, final, cols))
        part = rotate_part(index, pieces, [near])
        new_first, new_second, normed = rotate(
            index, part, pieces, final, first_moment, second_moment
        )

        halves, coded = [], []
        for chunk in range(CHUNKS):
            if chunk >= 2:
                normed, coded[chunk - 2] = lax.optimization_barrier((normed, coded[chunk - 2]))
            keep, mate = restore(normed, flipped[chunk], cols)
            mate = swap(mate, 1)
            halves.append((keep, mate))
            coded.append([send(keep, mate, distance, []) for distance in range(2, cols, 2)])
        crossed = [
            [swap(code, 2 * at + 2) for at, code in enumerate(codes)] for codes in coded
        ]
        gathered = [gather_row(send(*halves[c], 0, crossed[c])) for c in (0, 3)]
        products = [expand(*halves[c], crossed[c], left) for c in (1, 2)]
        arrived = [(), ()]
        for step in range(1, lines):
            for at, product in enumerate(products):
                upward, downward = hop(spot, product, arrived[at], lines, step)
                arrived[at] = (
                    up(upward, range(0, step)),
                    down(downward, range(lines - step, lines)),
                )
        update = update_chunk(spot, gathered[0], left_rows, None, 0, depth, width)
        for at, product in enumerate(products):
            update = finish(spot, product, arrived[at], update, at + 1, depth, width)
        update = update_chunk(spot, gathered[1], left_rows, update, 3, depth, width)
        return (new_first, new_second, update)

    return local


def solution(mesh):
    return jax.shard_map(
        build(mesh.shape["row"], mesh.shape["col"]),
        mesh=mesh,
        in_specs=(
            P(("groups", "row"), "col"),
            P(("groups", "row"), "col"),
            P(("groups", "row"), "col"),
            P(("groups", "col"), "row"),
            P(("groups", "row"), "col"),
        ),
        out_specs=(
            P(("groups", "row"), "col"),
            P(("groups", "row"), "col"),
            P(("groups", "row"), "col"),
        ),
        check_vma=False,
    )
```

```python
import functools
import jax
import jax.numpy as jnp
from jax import lax
from jax.experimental import pallas as pl
from jax.experimental.pallas import tpu as pltpu
from jax.sharding import PartitionSpec as P

BETA_ONE = 0.9
BETA_TWO = 0.95
EPSILON = 1e-08
CHUNKS = 4
EXTRA = 16
F32 = jnp.float32
BF16 = jnp.bfloat16
MIB = 2**20


def params(mib):
    return pltpu.CompilerParams(vmem_limit_bytes=mib * MIB)


def cost(flops, moved):
    return pl.CostEstimate(flops=int(flops) // 100, bytes_accessed=int(moved) // 100, transcendentals=0)


def split(value):
    high = lax.reduce_precision(value, exponent_bits=8, mantissa_bits=7)
    return high.astype(BF16), (value - high).astype(BF16)


def kernel_split(value):
    high = value.astype(BF16)
    return high, (value - high.astype(F32)).astype(BF16)


def dot(a, b, dims):
    return lax.dot_general(a, b, (dims, ((), ())), preferred_element_type=F32)


def halfway_kernel(place_ref, left, *refs, offsets, lines, first, last):
    pieces, refs = refs[: len(offsets)], refs[len(offsets) :]
    total = refs[-1]
    depth = pieces[0].shape[0]
    total[...] = jnp.zeros_like(total) if first else refs[0][...]
    place = place_ref[0]
    for offset, piece in zip(offsets, pieces):

        @pl.when((place + offset >= 0) & (place + offset < lines))
        def _(offset=offset, piece=piece):
            rows = left[pl.ds(pl.multiple_of((place + offset) * depth, depth), depth), :]
            total[...] += dot(rows, piece[...], ((0,), (0,)))

    if last:
        high, low = kernel_split(total[...])
        refs[-2][0] = high
        refs[-2][1] = low
    else:
        refs[-2][...] = total[...]


def halfway(place, left, held, offsets, lines, before, last):
    pieces = [held[offset] for offset in offsets]
    depth, half = pieces[0].shape
    inner = left.shape[1]
    tile = min(256, inner)
    whole = pl.BlockSpec((depth, half), lambda i, s: (0, 0))
    block = pl.BlockSpec((tile, half), lambda i, s: (i, 0))
    extra = [] if before is None else [before]
    return pl.pallas_call(
        functools.partial(
            halfway_kernel, offsets=offsets, lines=lines, first=before is None, last=last
        ),
        grid_spec=pltpu.PrefetchScalarGridSpec(
            num_scalar_prefetch=1,
            grid=(inner // tile,),
            in_specs=[pl.BlockSpec((left.shape[0], tile), lambda i, s: (0, i))]
            + [whole] * len(pieces)
            + [block] * len(extra),
            out_specs=pl.BlockSpec((2, tile, half), lambda i, s: (0, i, 0)) if last else block,
            scratch_shapes=[pltpu.VMEM((tile, half), F32)],
        ),
        out_shape=jax.ShapeDtypeStruct((2, inner, half), BF16)
        if last
        else jax.ShapeDtypeStruct((inner, half), F32),
        compiler_params=params(48),
        cost_estimate=cost(8 * depth * inner * half, 8 * depth * inner),
        name="halfway",
    )(place, left, *pieces, *extra)


def flip_kernel(at_ref, rows, above, below, out, *, far):
    me, place = at_ref[0], at_ref[1]
    late = (me ^ pl.program_id(0)) == far - place

    @pl.when(jnp.logical_not(late & ((place == 0) | (place == far))))
    def _():
        out[...] = rows[...].T

    @pl.when(late & (place == 0))
    def _():
        out[...] = above[...].T

    @pl.when(late & (place == far))
    def _():
        out[...] = below[...].T


def flip(at, right, above, below, cols, lines, chunk, piece):
    width = right.shape[1]
    per = above.shape[0] // piece
    if per * piece != width:
        far, per = -1, 1
    else:
        far = lines - 1
    last = pl.BlockSpec((piece, width), lambda d, s: (chunk if per > 1 else 0, 0))
    return pl.pallas_call(
        functools.partial(flip_kernel, far=far),
        grid_spec=pltpu.PrefetchScalarGridSpec(
            num_scalar_prefetch=1,
            grid=(cols,),
            in_specs=[
                pl.BlockSpec((piece, width), lambda d, s: ((s[0] ^ d) * CHUNKS + chunk, 0)),
                last,
                last,
            ],
            out_specs=pl.BlockSpec((width, piece), lambda d, s: (0, d)),
        ),
        out_shape=jax.ShapeDtypeStruct((width, cols * piece), BF16),
        compiler_params=params(48),
        cost_estimate=cost(0, 4 * piece * cols * width),
        name="flip",
    )(at, right, above, below)


def rotate_part_kernel(me_ref, *refs, cols, width):
    pieces, (right, out) = refs[:cols], refs[cols:]
    tile = out.shape[0]
    total = None
    for distance in range(cols):
        rows = right[pl.ds(pl.multiple_of((me_ref[0] ^ distance) * width, width), width), :]
        term = dot(pieces[distance][...].reshape(2 * tile, width), rows, ((1,), (0,)))
        total = term if total is None else total + term
    out[...] = total[:tile] + total[tile:]


def rotate_part(at, pieces, right):
    cols = len(pieces)
    _, depth, width = pieces[0].shape
    tile = min(256, depth)
    return pl.pallas_call(
        functools.partial(rotate_part_kernel, cols=cols, width=width),
        grid_spec=pltpu.PrefetchScalarGridSpec(
            num_scalar_prefetch=1,
            grid=(depth // tile,),
            in_specs=[pl.BlockSpec((2, tile, width), lambda i, s: (0, i, 0))] * cols
            + [pl.BlockSpec(right.shape, lambda i, s: (0, 0), pipeline_mode=pl.Buffered(1))],
            out_specs=pl.BlockSpec((tile, width), lambda i, s: (i, 0)),
        ),
        out_shape=jax.ShapeDtypeStruct((depth, width), F32),
        compiler_params=params(48),
        cost_estimate=cost(4 * depth * width * width * cols, 20 * depth * width),
        name="rotate_part",
    )(at, *pieces, right)


def rotate_kernel(at_ref, part, above, below, first, second, *refs, cols, lines):
    pieces, (new_first, new_second, normed, held, last, arrived) = refs[:cols], refs[cols:]
    tile, width = first.shape
    depth = last.shape[0]
    me, place = at_ref[0], at_ref[1]
    step, steps = pl.program_id(0), held.shape[1] // tile
    start = (lines - 1 - place) * depth
    distance_now = me ^ (start // width)

    def copy(distance, at):
        rows = pl.ds(at * tile, tile)
        if depth == width:
            source = pieces[distance].at[:, rows, :]
        else:
            columns = pl.ds(pl.multiple_of(lax.rem(start, width), depth), depth)
            source = pieces[distance].at[:, rows, columns]
        return pltpu.make_async_copy(source, held.at[:, rows, :], arrived.at[at])

    @pl.when(step == 0)
    def _():
        for distance in range(cols):

            @pl.when(distance_now == distance)
            def _(distance=distance):
                for at in range(steps):
                    copy(distance, at).start()

        last[...] = jnp.where(place == 0, above[...], below[...])

    for at in range(steps):

        @pl.when(step == at)
        def _(at=at):
            copy(0, at).wait()

    rows = pl.ds(pl.multiple_of(step * tile, tile), tile)
    both = dot(held[:, rows, :].reshape(2 * tile, depth), last[...], ((1,), (0,)))
    rotated = part[...] + both[:tile] + both[tile:]
    one = BETA_ONE * first[...] + (1.0 - BETA_ONE) * rotated
    two = BETA_TWO * second[...] + (1.0 - BETA_TWO) * rotated * rotated
    new_first[...] = one
    new_second[...] = two
    high, low = kernel_split(one / (jnp.sqrt(two) + EPSILON))
    normed[0] = high
    normed[1] = low


def rotate(at, part, pieces, above, below, first, second, lines):
    cols = len(pieces)
    rows, width = first.shape
    depth = above.shape[0]
    tile = min(256, rows)
    block = pl.BlockSpec((tile, width), lambda i, s: (i, 0))
    pair = pl.BlockSpec((2, tile, width), lambda i, s: (0, i, 0))
    whole = pl.BlockSpec(above.shape, lambda i, s: (0, 0), pipeline_mode=pl.Buffered(1))
    return pl.pallas_call(
        functools.partial(rotate_kernel, cols=cols, lines=lines),
        grid_spec=pltpu.PrefetchScalarGridSpec(
            num_scalar_prefetch=1,
            grid=(rows // tile,),
            in_specs=[block, whole, whole, block, block]
            + [pl.BlockSpec(memory_space=pl.ANY)] * cols,
            out_specs=[block, block, pair],
            scratch_shapes=[
                pltpu.VMEM((2, rows, depth), BF16),
                pltpu.VMEM((depth, width), BF16),
                pltpu.SemaphoreType.DMA((rows // tile,)),
            ],
        ),
        out_shape=[
            jax.ShapeDtypeStruct((rows, width), F32),
            jax.ShapeDtypeStruct((rows, width), F32),
            jax.ShapeDtypeStruct((2, rows, width), BF16),
        ],
        compiler_params=params(40),
        cost_estimate=cost(4 * rows * width * depth, 30 * rows * width),
        name="rotate",
    )(at, part, above, below, first, second, *pieces)


def restore_kernel(normed, flipped, keep, mate, *, cols):
    tile = normed.shape[1]
    piece = keep.shape[2]
    both = dot(normed[...].reshape(2 * tile, normed.shape[2]), flipped[...], ((1,), (0,)))
    term = both[:tile] + both[tile:]
    for distance in range(cols):
        out = mate if distance % 2 else keep
        out[distance // 2] = term[:, distance * piece : (distance + 1) * piece]


def restore(normed, flipped, cols):
    _, depth, inner = normed.shape
    piece = flipped.shape[1] // cols
    tile = min(256, depth)
    out = pl.BlockSpec((cols // 2, tile, piece), lambda i: (0, i, 0))
    return pl.pallas_call(
        functools.partial(restore_kernel, cols=cols),
        grid=(depth // tile,),
        in_specs=[
            pl.BlockSpec((2, tile, inner), lambda i: (0, i, 0)),
            pl.BlockSpec(flipped.shape, lambda i: (0, 0), pipeline_mode=pl.Buffered(1)),
        ],
        out_specs=[out, out],
        out_shape=[jax.ShapeDtypeStruct((cols // 2, depth, piece), F32)] * 2,
        compiler_params=params(24),
        cost_estimate=cost(4 * depth * inner * piece * cols, 8 * depth * piece * cols),
        name="restore",
    )(normed, flipped)


TOP = 7.5


def encode(value, inverse):
    code = jnp.abs(value) * (inverse * 2.0**TOP)
    for _ in range(4):
        code = code * code
    return jnp.where(value < 0, -code, code).astype(BF16)


def decode(code, scale):
    code = code.astype(F32)
    size = jnp.abs(code)
    root = jnp.exp2(jnp.log2(size) * 0.0625 - TOP) * scale
    root = jnp.where(size > 0, root, 0.0)
    return jnp.where(code < 0, -root, root)


def scale_of(message, depth):
    return jnp.max(message[depth : depth + EXTRA, :].astype(F32), axis=(0, 1), keepdims=True)


def fill(message, total, value_at, tile):
    depth, piece = total.shape

    def add(i, top):
        rows = pl.ds(pl.multiple_of(i * tile, tile), tile)
        value = value_at(rows)
        total[rows, :] = value
        return jnp.maximum(top, jnp.abs(value))

    top = lax.fori_loop(0, depth // tile, add, jnp.zeros((tile, piece), F32))
    top = jnp.maximum(jnp.max(top, axis=(0, 1), keepdims=True), 1e-30)
    scale = jnp.broadcast_to(top, (EXTRA, piece)).astype(BF16)
    message[depth : depth + EXTRA, :] = scale
    inverse = 1.0 / jnp.max(scale.astype(F32), axis=(0, 1), keepdims=True)

    def put(i, carry):
        rows = pl.ds(pl.multiple_of(i * tile, tile), tile)
        message[rows, :] = encode(total[rows, :], inverse)
        return carry

    lax.fori_loop(0, depth // tile, put, 0)


def summed(keep, mate, codes):
    depth = keep.shape[1]
    scales = [scale_of(code, depth) for code in codes]

    def value_at(rows):
        value = keep[0, rows, :] + mate[0, rows, :]
        for code, scale in zip(codes, scales):
            value = value + decode(code[rows, :], scale)
        return value

    return value_at


def send_kernel(keep, mate, *refs, tile):
    codes, (message, total) = refs[:-2], refs[-2:]
    fill(message, total, summed(keep, mate, codes), tile)


def send(keep, mate, distance, codes):
    _, depth, piece = keep.shape
    tile = min(64, depth)
    pair = pl.BlockSpec((1, depth, piece), lambda i: (distance // 2, 0, 0))
    message = pl.BlockSpec((depth + EXTRA, piece), lambda i: (0, 0))
    return pl.pallas_call(
        functools.partial(send_kernel, tile=tile),
        grid=(1,),
        in_specs=[pair, pair] + [message] * len(codes),
        out_specs=message,
        out_shape=jax.ShapeDtypeStruct((depth + EXTRA, piece), BF16),
        scratch_shapes=[pltpu.VMEM((depth, piece), F32)],
        compiler_params=params(16),
        cost_estimate=cost(400 * depth * piece, 18 * depth * piece),
        name="send",
    )(keep, mate, *codes)


def expand_kernel(keep, mate, *refs, tile):
    codes, (left, out, both) = refs[:-3], refs[-3:]
    depth, piece = both.shape[0], out.shape[1]

    @pl.when(pl.program_id(0) == 0)
    def _():
        value_at = summed(keep, mate, codes)

        def put(i, carry):
            rows = pl.ds(pl.multiple_of(i * tile, tile), tile)
            high, low = kernel_split(value_at(rows))
            both[rows, :piece] = high
            both[rows, piece:] = low
            return carry

        lax.fori_loop(0, depth // tile, put, 0)

    product = dot(left[...], both[...], ((1,), (0,)))
    out[...] = product[:, :piece] + product[:, piece:]


def expand(keep, mate, codes, left):
    rows, inner = left.shape
    _, depth, piece = keep.shape
    step = min(1024, rows)
    pair = pl.BlockSpec((1, depth, piece), lambda i: (0, 0, 0))
    message = pl.BlockSpec((depth + EXTRA, piece), lambda i: (0, 0))
    return pl.pallas_call(
        functools.partial(expand_kernel, tile=min(64, depth)),
        grid=(rows // step,),
        in_specs=[pair, pair]
        + [message] * len(codes)
        + [pl.BlockSpec((step, inner), lambda i: (i, 0))],
        out_specs=pl.BlockSpec((step, piece), lambda i: (i, 0)),
        out_shape=jax.ShapeDtypeStruct((rows, piece), F32),
        scratch_shapes=[pltpu.VMEM((depth, 2 * piece), BF16)],
        compiler_params=params(48),
        cost_estimate=cost(4 * rows * inner * piece, 4 * rows * piece + 2 * rows * inner),
        name="expand",
    )(keep, mate, *codes, left)


def hop_kernel(place_ref, *refs, lines, step, tile):
    blocks, refs = refs[:2], refs[2:]
    arrived, outs, total = refs[:-3], refs[-3:-1], refs[-1]
    depth = total.shape[0]
    sends = (place_ref[0] < step, place_ref[0] >= lines - step)
    for way in range(2):

        @pl.when(sends[way])
        def _(way=way):
            scale = scale_of(arrived[way], depth) if arrived else None

            def value_at(rows):
                value = blocks[way][rows, :]
                if arrived:
                    value = value + decode(arrived[way][rows, :], scale)
                return value

            fill(outs[way], total, value_at, tile)


def hop(place, product, arrived, lines, step):
    depth, piece = product.shape[0] // lines, product.shape[1]
    ahead = lines - step
    message = pl.BlockSpec((depth + EXTRA, piece), lambda i, s: (0, 0))
    return pl.pallas_call(
        functools.partial(hop_kernel, lines=lines, step=step, tile=min(64, depth)),
        grid_spec=pltpu.PrefetchScalarGridSpec(
            num_scalar_prefetch=1,
            grid=(1,),
            in_specs=[
                pl.BlockSpec(
                    (depth, piece), lambda i, s: (jnp.minimum(s[0] + ahead, lines - 1), 0)
                ),
                pl.BlockSpec((depth, piece), lambda i, s: (jnp.maximum(s[0] - ahead, 0), 0)),
            ]
            + [message] * len(arrived),
            out_specs=[message] * 2,
            scratch_shapes=[pltpu.VMEM((depth, piece), F32)],
        ),
        out_shape=[jax.ShapeDtypeStruct((depth + EXTRA, piece), BF16)] * 2,
        compiler_params=params(16),
        cost_estimate=cost(400 * depth * piece, 12 * depth * piece),
        name="hop",
    )(place, product, product, *arrived)


def finish_kernel(at_ref, block, up, down, *refs, tile):
    out = refs[-1]
    depth = out.shape[0]
    scales = [scale_of(message, depth) for message in (up, down)]

    def add(i, carry):
        rows = pl.ds(pl.multiple_of(i * tile, tile), tile)
        out[rows, :] = (
            block[rows, :] + decode(up[rows, :], scales[0]) + decode(down[rows, :], scales[1])
        )
        return carry

    lax.fori_loop(0, depth // tile, add, 0)


def finish(at, product, arrived, update, chunk, depth, width):
    piece = product.shape[1]
    tile = min(64, depth)
    message = pl.BlockSpec((depth + EXTRA, piece), lambda i, s: (0, 0))
    extra = [] if update is None else [update]
    return pl.pallas_call(
        functools.partial(finish_kernel, tile=tile),
        grid_spec=pltpu.PrefetchScalarGridSpec(
            num_scalar_prefetch=1,
            grid=(1,),
            in_specs=[pl.BlockSpec((depth, piece), lambda i, s: (s[0], 0)), message, message]
            + [pl.BlockSpec(memory_space=pl.ANY)] * len(extra),
            out_specs=pl.BlockSpec((depth, piece), lambda i, s: (0, chunk)),
        ),
        out_shape=jax.ShapeDtypeStruct((depth, width), F32),
        input_output_aliases={4: 0} if extra else {},
        compiler_params=params(16),
        cost_estimate=cost(400 * depth * piece, 12 * depth * piece),
        name="finish",
    )(at, product, *arrived, *extra)


def build(lines, cols):
    def swap(value, distance):
        return lax.ppermute(value, "col", [(i, i ^ distance) for i in range(cols)])

    def by_distance(block):
        held = {0: block}
        for distance in range(2, cols, 2):
            held[distance] = swap(block, distance)
        for distance in range(0, cols, 2):
            held[distance + 1] = swap(held[distance], 1)
        return held

    def place_by_distance(block, me):
        out = jnp.zeros((cols,) + block.shape, block.dtype)
        for distance, value in by_distance(block).items():
            out = lax.dynamic_update_index_in_dim(out, value, me ^ distance, 0)
        return out

    def up(value, senders):
        return lax.ppermute(value, "row", [(i, i + 1) for i in senders])

    def down(value, senders):
        return lax.ppermute(value, "row", [(i, i - 1) for i in senders])

    def walk(held, step):
        held[-step] = up(held[1 - step], range(step - 1, lines - 1))
        held[step] = down(held[step - 1], range(1, lines - step + 1))

    def local(gradient, first_moment, second_moment, left_basis, right_basis):
        me, place = lax.axis_index("col"), lax.axis_index("row")
        depth, width = gradient.shape
        piece = width // CHUNKS
        far = lines - 1
        spot, at = jnp.reshape(place, (1,)), jnp.stack([me, place])
        barrier = lax.optimization_barrier
        near = [offset for offset in range(-far, far + 1) if abs(offset) < far]

        left = place_by_distance(left_basis, me).reshape(-1, left_basis.shape[1])
        grads = {0: gradient}
        for step in range(1, lines):
            if step == far:
                left, grads[1 - step], grads[step - 1] = barrier(
                    (left, grads[1 - step], grads[step - 1])
                )
            walk(grads, step)
        before = halfway(spot, left, grads, near, lines, None, False)

        own, before, grads[-far], grads[far] = barrier(
            (right_basis, before, grads[-far], grads[far])
        )
        rights = {0: own}
        right = jnp.zeros(((lines + 1) * depth, width), BF16)

        def put(right, offset):
            there = place + offset
            there = jnp.where((there >= 0) & (there < lines), there, lines)
            return lax.dynamic_update_slice_in_dim(right, rights[offset], there * depth, 0)

        right = put(right, 0)
        for step in range(1, lines):
            if step == far:
                right, rights[1 - step], rights[step - 1] = barrier(
                    (right, rights[1 - step], rights[step - 1])
                )
            walk(rights, step)
            if step < far or depth != width:
                right = put(put(right, -step), step)
        above, below = rights[far], rights[-far]

        whole = halfway(spot, left, grads, [-far, far], lines, before, True)
        pieces = by_distance(whole)
        pieces = [pieces[distance] for distance in range(cols)]
        part = rotate_part(at, pieces, right)
        part, above, below = barrier((part, above, below))
        if depth != width:
            above_now, below_now = jnp.zeros_like(above), jnp.zeros_like(below)
        else:
            above_now, below_now = above, below
        new_first, new_second, normed = rotate(
            at, part, pieces, above_now, below_now, first_moment, second_moment, lines
        )

        halves, coded = [], []
        for chunk in range(CHUNKS):
            if chunk >= 2:
                normed, coded[chunk - 2] = barrier((normed, coded[chunk - 2]))
            flipped = flip(at, right, above, below, cols, lines, chunk, piece)
            keep, mate = restore(normed, flipped, cols)
            mate = swap(mate, 1)
            halves.append((keep, mate))
            coded.append([send(keep, mate, distance, []) for distance in range(2, cols, 2)])
        crossed = [
            [swap(code, 2 * index + 2) for index, code in enumerate(codes)] for codes in coded
        ]
        products = [expand(*halves[c], crossed[c], left) for c in range(CHUNKS)]
        arrived = [()] * CHUNKS
        for step in range(1, lines):
            for chunk, product in enumerate(products):
                upward, downward = hop(spot, product, arrived[chunk], lines, step)
                arrived[chunk] = (
                    up(upward, range(0, step)),
                    down(downward, range(lines - step, lines)),
                )
        update = None
        for chunk, product in enumerate(products):
            update = finish(spot, product, arrived[chunk], update, chunk, depth, width)
        return (new_first, new_second, update)

    return local


def solution(mesh):
    return jax.shard_map(
        build(mesh.shape["row"], mesh.shape["col"]),
        mesh=mesh,
        in_specs=(
            P(("groups", "row"), "col"),
            P(("groups", "row"), "col"),
            P(("groups", "row"), "col"),
            P(("groups", "col"), "row"),
            P(("groups", "row"), "col"),
        ),
        out_specs=(
            P(("groups", "row"), "col"),
            P(("groups", "row"), "col"),
            P(("groups", "row"), "col"),
        ),
        check_vma=False,
    )
```

```python
import functools
import jax
import jax.numpy as jnp
from jax import lax
from jax.experimental import pallas as pl
from jax.experimental.pallas import tpu as pltpu
from jax.sharding import PartitionSpec as P

BETA_ONE = 0.9
BETA_TWO = 0.95
EPSILON = 1e-08
CHUNKS = 4
EXTRA = 16
F32 = jnp.float32
BF16 = jnp.bfloat16
MIB = 2**20


def params(mib):
    return pltpu.CompilerParams(vmem_limit_bytes=mib * MIB)


def cost(flops, moved):
    return pl.CostEstimate(flops=int(flops) // 100, bytes_accessed=int(moved) // 100, transcendentals=0)


def split(value):
    high = lax.reduce_precision(value, exponent_bits=8, mantissa_bits=7)
    return high.astype(BF16), (value - high).astype(BF16)


def kernel_split(value):
    high = value.astype(BF16)
    return high, (value - high.astype(F32)).astype(BF16)


def dot(a, b, dims):
    return lax.dot_general(a, b, (dims, ((), ())), preferred_element_type=F32)


TOP = 7.5


def encode(value, inverse):
    code = jnp.abs(value) * (inverse * 2.0**TOP)
    for _ in range(4):
        code = code * code
    return jnp.where(value < 0, -code, code).astype(BF16)


def decode(code, scale):
    code = code.astype(F32)
    size = jnp.abs(code)
    root = jnp.exp2(jnp.log2(size) * 0.0625 - TOP) * scale
    root = jnp.where(size > 0, root, 0.0)
    return jnp.where(code < 0, -root, root)


def scale_of(message, depth):
    return jnp.max(message[depth : depth + EXTRA, :].astype(F32), axis=(0, 1), keepdims=True)


def fill(message, total, value_at, tile, again=None):
    depth, piece = message.shape[0] - EXTRA, message.shape[1]

    def add(i, top):
        rows = pl.ds(pl.multiple_of(i * tile, tile), tile)
        value = value_at(rows)
        if again is None:
            total[rows, :] = value
        return jnp.maximum(top, jnp.abs(value))

    top = lax.fori_loop(0, depth // tile, add, jnp.zeros((tile, piece), F32))
    top = jnp.maximum(jnp.max(top, axis=(0, 1), keepdims=True), 1e-30)
    scale = jnp.broadcast_to(top, (EXTRA, piece)).astype(BF16)
    message[depth : depth + EXTRA, :] = scale
    inverse = 1.0 / jnp.max(scale.astype(F32), axis=(0, 1), keepdims=True)

    def put(i, carry):
        rows = pl.ds(pl.multiple_of(i * tile, tile), tile)
        value = total[rows, :] if again is None else again(rows)
        message[rows, :] = encode(value, inverse)
        return carry

    lax.fori_loop(0, depth // tile, put, 0)


def halfway_kernel(place_ref, left, *refs, offsets, lines, first):
    pieces, refs = refs[: len(offsets)], refs[len(offsets) :]
    total = refs[-1]
    depth = pieces[0].shape[0]
    total[...] = jnp.zeros_like(total) if first else refs[0][...]
    place = place_ref[0]
    for offset, piece in zip(offsets, pieces):

        @pl.when((place + offset >= 0) & (place + offset < lines))
        def _(offset=offset, piece=piece):
            rows = left[pl.ds(pl.multiple_of((place + offset) * depth, depth), depth), :]
            total[...] += dot(rows, piece[...], ((0,), (0,)))

    refs[-2][...] = total[...]


def halfway(place, left, held, offsets, lines, before):
    pieces = [held[offset] for offset in offsets]
    depth, width = pieces[0].shape
    inner = left.shape[1]
    tile = min(256, inner)
    whole = pl.BlockSpec((depth, width), lambda i, s: (0, 0))
    block = pl.BlockSpec((tile, width), lambda i, s: (i, 0))
    extra = [] if before is None else [before]
    return pl.pallas_call(
        functools.partial(halfway_kernel, offsets=offsets, lines=lines, first=before is None),
        grid_spec=pltpu.PrefetchScalarGridSpec(
            num_scalar_prefetch=1,
            grid=(inner // tile,),
            in_specs=[pl.BlockSpec((left.shape[0], tile), lambda i, s: (0, i))]
            + [whole] * len(pieces)
            + [block] * len(extra),
            out_specs=block,
            scratch_shapes=[pltpu.VMEM((tile, width), F32)],
        ),
        out_shape=jax.ShapeDtypeStruct((inner, width), F32),
        compiler_params=params(48),
        cost_estimate=cost(8 * depth * inner * width, 8 * depth * inner),
        name="halfway",
    )(place, left, *pieces, *extra)


def pack_kernel(value, pair, message, *, tile):
    depth, _ = value.shape

    def value_at(rows):
        now = value[rows, :]
        high, low = kernel_split(now)
        pair[0, rows, :] = high
        pair[1, rows, :] = low
        return now

    fill(message, None, value_at, tile, lambda rows: value[rows, :])


def pack(value):
    depth, width = value.shape
    return pl.pallas_call(
        functools.partial(pack_kernel, tile=min(16, depth)),
        out_shape=[
            jax.ShapeDtypeStruct((2, depth, width), BF16),
            jax.ShapeDtypeStruct((depth + EXTRA, width), BF16),
        ],
        compiler_params=params(32),
        cost_estimate=cost(400 * depth * width, 10 * depth * width),
        name="pack",
    )(value)


def unpack_kernel(message, pair, *, tile):
    _, depth, _ = pair.shape
    scale = scale_of(message, depth)

    def put(i, carry):
        rows = pl.ds(pl.multiple_of(i * tile, tile), tile)
        high, low = kernel_split(decode(message[rows, :], scale))
        pair[0, rows, :] = high
        pair[1, rows, :] = low
        return carry

    lax.fori_loop(0, depth // tile, put, 0)


def unpack(message):
    depth, width = message.shape[0] - EXTRA, message.shape[1]
    return pl.pallas_call(
        functools.partial(unpack_kernel, tile=min(16, depth)),
        out_shape=jax.ShapeDtypeStruct((2, depth, width), BF16),
        compiler_params=params(32),
        cost_estimate=cost(400 * depth * width, 6 * depth * width),
        name="unpack",
    )(message)


def rotate_part_kernel(me_ref, *refs, cols, width):
    pieces, (right, out) = refs[:cols], refs[cols:]
    tile = out.shape[0]
    total = None
    for distance in range(cols):
        rows = right[pl.ds(pl.multiple_of((me_ref[0] ^ distance) * width, width), width), :]
        term = dot(pieces[distance][...].reshape(2 * tile, width), rows, ((1,), (0,)))
        total = term if total is None else total + term
    out[...] = total[:tile] + total[tile:]


def rotate_part(at, pieces, right):
    cols = len(pieces)
    _, depth, width = pieces[0].shape
    tile = min(256, depth)
    return pl.pallas_call(
        functools.partial(rotate_part_kernel, cols=cols, width=width),
        grid_spec=pltpu.PrefetchScalarGridSpec(
            num_scalar_prefetch=1,
            grid=(depth // tile,),
            in_specs=[pl.BlockSpec((2, tile, width), lambda i, s: (0, i, 0))] * cols
            + [pl.BlockSpec(right.shape, lambda i, s: (0, 0), pipeline_mode=pl.Buffered(1))],
            out_specs=pl.BlockSpec((tile, width), lambda i, s: (i, 0)),
        ),
        out_shape=jax.ShapeDtypeStruct((depth, width), F32),
        compiler_params=params(48),
        cost_estimate=cost(4 * depth * width * width * cols, 20 * depth * width),
        name="rotate_part",
    )(at, *pieces, right)


def rotate_kernel(at_ref, part, above, below, first, second, *refs, cols, lines):
    pieces, (new_first, new_second, normed, held, last, arrived) = refs[:cols], refs[cols:]
    tile, width = first.shape
    depth = last.shape[0]
    me, place = at_ref[0], at_ref[1]
    step, steps = pl.program_id(0), held.shape[1] // tile
    start = (lines - 1 - place) * depth
    distance_now = me ^ (start // width)

    def copy(distance, at):
        rows = pl.ds(at * tile, tile)
        if depth == width:
            source = pieces[distance].at[:, rows, :]
        else:
            columns = pl.ds(pl.multiple_of(lax.rem(start, width), depth), depth)
            source = pieces[distance].at[:, rows, columns]
        return pltpu.make_async_copy(source, held.at[:, rows, :], arrived.at[at])

    @pl.when(step == 0)
    def _():
        for distance in range(cols):

            @pl.when(distance_now == distance)
            def _(distance=distance):
                for at in range(steps):
                    copy(distance, at).start()

        last[...] = jnp.where(place == 0, above[...], below[...])

    for at in range(steps):

        @pl.when(step == at)
        def _(at=at):
            copy(0, at).wait()

    rows = pl.ds(pl.multiple_of(step * tile, tile), tile)
    both = dot(held[:, rows, :].reshape(2 * tile, depth), last[...], ((1,), (0,)))
    rotated = part[...] + both[:tile] + both[tile:]
    one = BETA_ONE * first[...] + (1.0 - BETA_ONE) * rotated
    two = BETA_TWO * second[...] + (1.0 - BETA_TWO) * rotated * rotated
    new_first[...] = one
    new_second[...] = two
    high, low = kernel_split(one / (jnp.sqrt(two) + EPSILON))
    normed[0] = high
    normed[1] = low


def rotate(at, part, pieces, above, below, first, second, lines):
    cols = len(pieces)
    rows, width = first.shape
    depth = above.shape[0]
    tile = min(256, rows)
    block = pl.BlockSpec((tile, width), lambda i, s: (i, 0))
    pair = pl.BlockSpec((2, tile, width), lambda i, s: (0, i, 0))
    whole = pl.BlockSpec(above.shape, lambda i, s: (0, 0), pipeline_mode=pl.Buffered(1))
    return pl.pallas_call(
        functools.partial(rotate_kernel, cols=cols, lines=lines),
        grid_spec=pltpu.PrefetchScalarGridSpec(
            num_scalar_prefetch=1,
            grid=(rows // tile,),
            in_specs=[block, whole, whole, block, block]
            + [pl.BlockSpec(memory_space=pl.ANY)] * cols,
            out_specs=[block, block, pair],
            scratch_shapes=[
                pltpu.VMEM((2, rows, depth), BF16),
                pltpu.VMEM((depth, width), BF16),
                pltpu.SemaphoreType.DMA((rows // tile,)),
            ],
        ),
        out_shape=[
            jax.ShapeDtypeStruct((rows, width), F32),
            jax.ShapeDtypeStruct((rows, width), F32),
            jax.ShapeDtypeStruct((2, rows, width), BF16),
        ],
        compiler_params=params(40),
        cost_estimate=cost(4 * rows * width * depth, 30 * rows * width),
        name="rotate",
    )(at, part, above, below, first, second, *pieces)


def restore_kernel(at_ref, normed, *refs, cols, far):
    rows, (above, below, keep, mate, flipped) = refs[:cols], refs[cols:]
    tile, piece = normed.shape[1], keep.shape[2]
    me, place = at_ref[0], at_ref[1]

    @pl.when(pl.program_id(0) == 0)
    def _():
        for distance in range(cols):
            here = pl.ds(distance * piece, piece)
            late = (me ^ distance) == far - place

            @pl.when(jnp.logical_not(late & ((place == 0) | (place == far))))
            def _(distance=distance, here=here):
                flipped[:, here] = rows[distance][...].T

            @pl.when(late & (place == 0))
            def _(here=here):
                flipped[:, here] = above[...].T

            @pl.when(late & (place == far))
            def _(here=here):
                flipped[:, here] = below[...].T

    both = dot(normed[...].reshape(2 * tile, normed.shape[2]), flipped[...], ((1,), (0,)))
    term = both[:tile] + both[tile:]
    for distance in range(cols):
        out = mate if distance % 2 else keep
        out[distance // 2] = term[:, distance * piece : (distance + 1) * piece]


def restore(at, normed, right, above, below, cols, lines, chunk, piece):
    _, depth, inner = normed.shape
    tile = min(256, depth)
    aligned = above.shape[0] == inner
    far = lines - 1 if aligned else -cols
    out = pl.BlockSpec((cols // 2, tile, piece), lambda i, s: (0, i, 0))

    def rows(distance):
        return pl.BlockSpec((piece, inner), lambda i, s: ((s[0] ^ distance) * CHUNKS + chunk, 0))

    last = pl.BlockSpec((piece, inner), lambda i, s: (chunk if aligned else 0, 0))
    return pl.pallas_call(
        functools.partial(restore_kernel, cols=cols, far=far),
        grid_spec=pltpu.PrefetchScalarGridSpec(
            num_scalar_prefetch=1,
            grid=(depth // tile,),
            in_specs=[pl.BlockSpec((2, tile, inner), lambda i, s: (0, i, 0))]
            + [rows(distance) for distance in range(cols)]
            + [last, last],
            out_specs=[out, out],
            scratch_shapes=[pltpu.VMEM((inner, cols * piece), BF16)],
        ),
        out_shape=[jax.ShapeDtypeStruct((cols // 2, depth, piece), F32)] * 2,
        compiler_params=params(40),
        cost_estimate=cost(4 * depth * inner * piece * cols, 8 * depth * piece * cols),
        name="restore",
    )(at, normed, *([right] * cols), above, below)


def summed(keep, mate, codes):
    depth = keep.shape[1]
    scales = [scale_of(code, depth) for code in codes]

    def value_at(rows):
        value = keep[0, rows, :] + mate[0, rows, :]
        for code, scale in zip(codes, scales):
            value = value + decode(code[rows, :], scale)
        return value

    return value_at


def send_kernel(keep, mate, *refs, tile):
    codes, (message, total) = refs[:-2], refs[-2:]
    fill(message, total, summed(keep, mate, codes), tile)


def send(keep, mate, distance, codes):
    _, depth, piece = keep.shape
    tile = min(64, depth)
    pair = pl.BlockSpec((1, depth, piece), lambda i: (distance // 2, 0, 0))
    message = pl.BlockSpec((depth + EXTRA, piece), lambda i: (0, 0))
    return pl.pallas_call(
        functools.partial(send_kernel, tile=tile),
        grid=(1,),
        in_specs=[pair, pair] + [message] * len(codes),
        out_specs=message,
        out_shape=jax.ShapeDtypeStruct((depth + EXTRA, piece), BF16),
        scratch_shapes=[pltpu.VMEM((depth, piece), F32)],
        compiler_params=params(16),
        cost_estimate=cost(400 * depth * piece, 18 * depth * piece),
        name="send",
    )(keep, mate, *codes)


def expand_kernel(keep, mate, *refs, tile):
    codes, (left, out, both) = refs[:-3], refs[-3:]
    depth, piece = both.shape[0], out.shape[1]

    @pl.when(pl.program_id(0) == 0)
    def _():
        value_at = summed(keep, mate, codes)

        def put(i, carry):
            rows = pl.ds(pl.multiple_of(i * tile, tile), tile)
            high, low = kernel_split(value_at(rows))
            both[rows, :piece] = high
            both[rows, piece:] = low
            return carry

        lax.fori_loop(0, depth // tile, put, 0)

    product = dot(left[...], both[...], ((1,), (0,)))
    out[...] = product[:, :piece] + product[:, piece:]


def expand(keep, mate, codes, left):
    rows, inner = left.shape
    _, depth, piece = keep.shape
    step = min(1024, rows)
    pair = pl.BlockSpec((1, depth, piece), lambda i: (0, 0, 0))
    message = pl.BlockSpec((depth + EXTRA, piece), lambda i: (0, 0))
    return pl.pallas_call(
        functools.partial(expand_kernel, tile=min(64, depth)),
        grid=(rows // step,),
        in_specs=[pair, pair]
        + [message] * len(codes)
        + [pl.BlockSpec((step, inner), lambda i: (i, 0))],
        out_specs=pl.BlockSpec((step, piece), lambda i: (i, 0)),
        out_shape=jax.ShapeDtypeStruct((rows, piece), F32),
        scratch_shapes=[pltpu.VMEM((depth, 2 * piece), BF16)],
        compiler_params=params(48),
        cost_estimate=cost(4 * rows * inner * piece, 4 * rows * piece + 2 * rows * inner),
        name="expand",
    )(keep, mate, *codes, left)


def hop_kernel(place_ref, *refs, lines, step, tile):
    blocks, refs = refs[:2], refs[2:]
    arrived, outs, total = refs[:-3], refs[-3:-1], refs[-1]
    depth = total.shape[0]
    sends = (place_ref[0] < step, place_ref[0] >= lines - step)
    for way in range(2):

        @pl.when(sends[way])
        def _(way=way):
            scale = scale_of(arrived[way], depth) if arrived else None

            def value_at(rows):
                value = blocks[way][rows, :]
                if arrived:
                    value = value + decode(arrived[way][rows, :], scale)
                return value

            fill(outs[way], total, value_at, tile)


def hop(place, product, arrived, lines, step):
    depth, piece = product.shape[0] // lines, product.shape[1]
    ahead = lines - step
    message = pl.BlockSpec((depth + EXTRA, piece), lambda i, s: (0, 0))
    return pl.pallas_call(
        functools.partial(hop_kernel, lines=lines, step=step, tile=min(64, depth)),
        grid_spec=pltpu.PrefetchScalarGridSpec(
            num_scalar_prefetch=1,
            grid=(1,),
            in_specs=[
                pl.BlockSpec(
                    (depth, piece), lambda i, s: (jnp.minimum(s[0] + ahead, lines - 1), 0)
                ),
                pl.BlockSpec((depth, piece), lambda i, s: (jnp.maximum(s[0] - ahead, 0), 0)),
            ]
            + [message] * len(arrived),
            out_specs=[message] * 2,
            scratch_shapes=[pltpu.VMEM((depth, piece), F32)],
        ),
        out_shape=[jax.ShapeDtypeStruct((depth + EXTRA, piece), BF16)] * 2,
        compiler_params=params(48),
        cost_estimate=cost(400 * depth * piece, 12 * depth * piece),
        name="hop",
    )(place, product, product, *arrived)


def finish_kernel(at_ref, block, up, down, *refs, tile):
    out = refs[-1]
    depth = out.shape[0]
    scales = [scale_of(message, depth) for message in (up, down)]

    def add(i, carry):
        rows = pl.ds(pl.multiple_of(i * tile, tile), tile)
        out[rows, :] = (
            block[rows, :] + decode(up[rows, :], scales[0]) + decode(down[rows, :], scales[1])
        )
        return carry

    lax.fori_loop(0, depth // tile, add, 0)


def finish(at, product, arrived, update, chunk, depth, width):
    piece = product.shape[1]
    tile = min(64, depth)
    message = pl.BlockSpec((depth + EXTRA, piece), lambda i, s: (0, 0))
    extra = [] if update is None else [update]
    return pl.pallas_call(
        functools.partial(finish_kernel, tile=tile),
        grid_spec=pltpu.PrefetchScalarGridSpec(
            num_scalar_prefetch=1,
            grid=(1,),
            in_specs=[pl.BlockSpec((depth, piece), lambda i, s: (s[0], 0)), message, message]
            + [pl.BlockSpec(memory_space=pl.ANY)] * len(extra),
            out_specs=pl.BlockSpec((depth, piece), lambda i, s: (0, chunk)),
        ),
        out_shape=jax.ShapeDtypeStruct((depth, width), F32),
        input_output_aliases={4: 0} if extra else {},
        compiler_params=params(48),
        cost_estimate=cost(400 * depth * piece, 12 * depth * piece),
        name="finish",
    )(at, product, *arrived, *extra)


def build(lines, cols):
    def swap(value, distance):
        return lax.ppermute(value, "col", [(i, i ^ distance) for i in range(cols)])

    def by_distance(block):
        held = {0: block}
        for distance in range(2, cols, 2):
            held[distance] = swap(block, distance)
        for distance in range(0, cols, 2):
            held[distance + 1] = swap(held[distance], 1)
        return held

    def place_by_distance(block, me):
        out = jnp.zeros((cols,) + block.shape, block.dtype)
        for distance, value in by_distance(block).items():
            out = lax.dynamic_update_index_in_dim(out, value, me ^ distance, 0)
        return out

    def up(value, senders):
        return lax.ppermute(value, "row", [(i, i + 1) for i in senders])

    def down(value, senders):
        return lax.ppermute(value, "row", [(i, i - 1) for i in senders])

    def walk(held, step):
        held[-step] = up(held[1 - step], range(step - 1, lines - 1))
        held[step] = down(held[step - 1], range(1, lines - step + 1))

    def local(gradient, first_moment, second_moment, left_basis, right_basis):
        me, place = lax.axis_index("col"), lax.axis_index("row")
        depth, width = gradient.shape
        piece = width // CHUNKS
        far = lines - 1
        spot, at = jnp.reshape(place, (1,)), jnp.stack([me, place])
        barrier = lax.optimization_barrier
        near = [offset for offset in range(-far, far + 1) if abs(offset) < far]

        left = place_by_distance(left_basis, me).reshape(-1, left_basis.shape[1])
        grads = {0: gradient}
        for step in range(1, lines):
            if step == far:
                left, grads[1 - step], grads[step - 1] = barrier(
                    (left, grads[1 - step], grads[step - 1])
                )
            walk(grads, step)
        before = halfway(spot, left, grads, near, lines, None)

        own, before, grads[-far], grads[far] = barrier(
            (right_basis, before, grads[-far], grads[far])
        )
        rights = {0: own}
        right = jnp.zeros(((lines + 1) * depth, width), BF16)

        def put(right, offset):
            there = place + offset
            there = jnp.where((there >= 0) & (there < lines), there, lines)
            return lax.dynamic_update_slice_in_dim(right, rights[offset], there * depth, 0)

        right = put(right, 0)
        for step in range(1, lines):
            walk(rights, step)
            if step < far or depth != width:
                right = put(put(right, -step), step)
        above, below = rights[far], rights[-far]

        pair, message = pack(halfway(spot, left, grads, [-far, far], lines, before))
        message, rights[-1], rights[1] = barrier((message, rights[-1], rights[1]))
        pieces = by_distance(message)
        pieces = [pair] + [unpack(pieces[distance]) for distance in range(1, cols)]
        part = rotate_part(at, pieces, right)
        part, above, below = barrier((part, above, below))
        if depth != width:
            above_now, below_now = jnp.zeros_like(above), jnp.zeros_like(below)
        else:
            above_now, below_now = above, below
        new_first, new_second, normed = rotate(
            at, part, pieces, above_now, below_now, first_moment, second_moment, lines
        )

        products, hops = [], []
        for chunk in range(CHUNKS):
            if chunk >= 2:
                normed, hops[chunk - 2] = barrier((normed, hops[chunk - 2]))
            keep, mate = restore(at, normed, right, above, below, cols, lines, chunk, piece)
            mate = swap(mate, 1)
            crossed = [
                swap(send(keep, mate, distance, []), distance) for distance in range(2, cols, 2)
            ]
            products.append(expand(keep, mate, crossed, left))
            hops.append(hop(spot, products[chunk], (), lines, 1))
        arrived = [()] * CHUNKS
        for step in range(1, lines):
            for chunk, product in enumerate(products):
                if step > 1:
                    hops[chunk] = hop(spot, product, arrived[chunk], lines, step)
                upward, downward = hops[chunk]
                arrived[chunk] = (
                    up(upward, range(0, step)),
                    down(downward, range(lines - step, lines)),
                )
        update = None
        for chunk, product in enumerate(products):
            update = finish(spot, product, arrived[chunk], update, chunk, depth, width)
        return (new_first, new_second, update)

    return local


def solution(mesh):
    return jax.shard_map(
        build(mesh.shape["row"], mesh.shape["col"]),
        mesh=mesh,
        in_specs=(
            P(("groups", "row"), "col"),
            P(("groups", "row"), "col"),
            P(("groups", "row"), "col"),
            P(("groups", "col"), "row"),
            P(("groups", "row"), "col"),
        ),
        out_specs=(
            P(("groups", "row"), "col"),
            P(("groups", "row"), "col"),
            P(("groups", "row"), "col"),
        ),
        check_vma=False,
    )
```

```python
import functools
import jax
import jax.numpy as jnp
from jax import lax
from jax.experimental import pallas as pl
from jax.experimental.pallas import tpu as pltpu
from jax.sharding import PartitionSpec as P

BETA_ONE = 0.9
BETA_TWO = 0.95
EPSILON = 1e-08
CHUNKS = 4
EXTRA = 16
F32 = jnp.float32
BF16 = jnp.bfloat16
MIB = 2**20


def params(mib):
    return pltpu.CompilerParams(vmem_limit_bytes=mib * MIB)


def cost(flops, moved):
    return pl.CostEstimate(flops=int(flops) // 100, bytes_accessed=int(moved) // 100, transcendentals=0)


def split(value):
    high = lax.reduce_precision(value, exponent_bits=8, mantissa_bits=7)
    return high.astype(BF16), (value - high).astype(BF16)


def kernel_split(value):
    high = value.astype(BF16)
    return high, (value - high.astype(F32)).astype(BF16)


def dot(a, b, dims):
    return lax.dot_general(a, b, (dims, ((), ())), preferred_element_type=F32)


TOP = 7.5


def encode(value, inverse):
    code = jnp.abs(value) * (inverse * 2.0**TOP)
    for _ in range(4):
        code = code * code
    return jnp.where(value < 0, -code, code).astype(BF16)


def decode(code, scale):
    code = code.astype(F32)
    size = jnp.abs(code)
    root = jnp.exp2(jnp.log2(size) * 0.0625 - TOP) * scale
    root = jnp.where(size > 0, root, 0.0)
    return jnp.where(code < 0, -root, root)


def scale_of(message, depth):
    return jnp.max(message[depth : depth + EXTRA, :].astype(F32), axis=(0, 1), keepdims=True)


def fill(message, total, value_at, tile, again=None):
    depth, piece = message.shape[0] - EXTRA, message.shape[1]

    def add(i, top):
        rows = pl.ds(pl.multiple_of(i * tile, tile), tile)
        value = value_at(rows)
        if again is None:
            total[rows, :] = value
        return jnp.maximum(top, jnp.abs(value))

    top = lax.fori_loop(0, depth // tile, add, jnp.zeros((tile, piece), F32))
    top = jnp.maximum(jnp.max(top, axis=(0, 1), keepdims=True), 1e-30)
    scale = jnp.broadcast_to(top, (EXTRA, piece)).astype(BF16)
    message[depth : depth + EXTRA, :] = scale
    inverse = 1.0 / jnp.max(scale.astype(F32), axis=(0, 1), keepdims=True)

    def put(i, carry):
        rows = pl.ds(pl.multiple_of(i * tile, tile), tile)
        value = total[rows, :] if again is None else again(rows)
        message[rows, :] = encode(value, inverse)
        return carry

    lax.fori_loop(0, depth // tile, put, 0)


def halfway_kernel(place_ref, left, *refs, offsets, lines, first):
    pieces, refs = refs[: len(offsets)], refs[len(offsets) :]
    total = refs[-1]
    depth = pieces[0].shape[0]
    total[...] = jnp.zeros_like(total) if first else refs[0][...]
    place = place_ref[0]
    for offset, piece in zip(offsets, pieces):

        @pl.when((place + offset >= 0) & (place + offset < lines))
        def _(offset=offset, piece=piece):
            rows = left[pl.ds(pl.multiple_of((place + offset) * depth, depth), depth), :]
            total[...] += dot(rows, piece[...], ((0,), (0,)))

    refs[-2][...] = total[...]


def halfway(place, left, held, offsets, lines, before):
    pieces = [held[offset] for offset in offsets]
    depth, width = pieces[0].shape
    inner = left.shape[1]
    tile = min(256, inner)
    whole = pl.BlockSpec((depth, width), lambda i, s: (0, 0))
    block = pl.BlockSpec((tile, width), lambda i, s: (i, 0))
    extra = [] if before is None else [before]
    return pl.pallas_call(
        functools.partial(halfway_kernel, offsets=offsets, lines=lines, first=before is None),
        grid_spec=pltpu.PrefetchScalarGridSpec(
            num_scalar_prefetch=1,
            grid=(inner // tile,),
            in_specs=[pl.BlockSpec((left.shape[0], tile), lambda i, s: (0, i))]
            + [whole] * len(pieces)
            + [block] * len(extra),
            out_specs=block,
            scratch_shapes=[pltpu.VMEM((tile, width), F32)],
        ),
        out_shape=jax.ShapeDtypeStruct((inner, width), F32),
        compiler_params=params(48),
        cost_estimate=cost(8 * depth * inner * width, 8 * depth * inner),
        name="halfway",
    )(place, left, *pieces, *extra)


def pack_kernel(value, pair, message, *, tile):
    depth, _ = value.shape

    def value_at(rows):
        now = value[rows, :]
        high, low = kernel_split(now)
        pair[0, rows, :] = high
        pair[1, rows, :] = low
        return now

    fill(message, None, value_at, tile, lambda rows: value[rows, :])


def pack(value):
    depth, width = value.shape
    return pl.pallas_call(
        functools.partial(pack_kernel, tile=min(16, depth)),
        out_shape=[
            jax.ShapeDtypeStruct((2, depth, width), BF16),
            jax.ShapeDtypeStruct((depth + EXTRA, width), BF16),
        ],
        compiler_params=params(32),
        cost_estimate=cost(400 * depth * width, 10 * depth * width),
        name="pack",
    )(value)


def unpack_kernel(message, scales, pair, *, tile):
    _, depth, _ = pair.shape
    scale = scale_of(scales, 0)

    def put(i, carry):
        rows = pl.ds(pl.multiple_of(i * tile, tile), tile)
        high, low = kernel_split(decode(message[rows, :], scale))
        pair[0, rows, :] = high
        pair[1, rows, :] = low
        return carry

    lax.fori_loop(0, depth // tile, put, 0)


def unpack(message):
    depth, width = message.shape[0] - EXTRA, message.shape[1]
    step = min(256, depth)
    return pl.pallas_call(
        functools.partial(unpack_kernel, tile=min(16, step)),
        grid=(depth // step,),
        in_specs=[
            pl.BlockSpec((step, width), lambda i: (i, 0)),
            pl.BlockSpec((EXTRA, width), lambda i: (depth // EXTRA, 0)),
        ],
        out_specs=pl.BlockSpec((2, step, width), lambda i: (0, i, 0)),
        out_shape=jax.ShapeDtypeStruct((2, depth, width), BF16),
        compiler_params=params(60),
        cost_estimate=cost(400 * depth * width, 6 * depth * width),
        name="unpack",
    )(message, message)


def rotate_part_kernel(me_ref, *refs, cols, width):
    pieces, (right, out) = refs[:cols], refs[cols:]
    tile = out.shape[0]
    total = None
    for distance in range(cols):
        rows = right[pl.ds(pl.multiple_of((me_ref[0] ^ distance) * width, width), width), :]
        term = dot(pieces[distance][...].reshape(2 * tile, width), rows, ((1,), (0,)))
        total = term if total is None else total + term
    out[...] = total[:tile] + total[tile:]


def rotate_part(at, pieces, right):
    cols = len(pieces)
    _, depth, width = pieces[0].shape
    tile = min(256, depth)
    return pl.pallas_call(
        functools.partial(rotate_part_kernel, cols=cols, width=width),
        grid_spec=pltpu.PrefetchScalarGridSpec(
            num_scalar_prefetch=1,
            grid=(depth // tile,),
            in_specs=[pl.BlockSpec((2, tile, width), lambda i, s: (0, i, 0))] * cols
            + [pl.BlockSpec(right.shape, lambda i, s: (0, 0), pipeline_mode=pl.Buffered(1))],
            out_specs=pl.BlockSpec((tile, width), lambda i, s: (i, 0)),
        ),
        out_shape=jax.ShapeDtypeStruct((depth, width), F32),
        compiler_params=params(48),
        cost_estimate=cost(4 * depth * width * width * cols, 20 * depth * width),
        name="rotate_part",
    )(at, *pieces, right)


def rotate_kernel(at_ref, part, above, below, first, second, *refs, cols, lines):
    pieces, (new_first, new_second, normed, held, last, arrived) = refs[:cols], refs[cols:]
    tile, width = first.shape
    depth = last.shape[0]
    me, place = at_ref[0], at_ref[1]
    step, steps = pl.program_id(0), held.shape[1] // tile
    start = (lines - 1 - place) * depth
    distance_now = me ^ (start // width)

    def copy(distance, at):
        rows = pl.ds(at * tile, tile)
        if depth == width:
            source = pieces[distance].at[:, rows, :]
        else:
            columns = pl.ds(pl.multiple_of(lax.rem(start, width), depth), depth)
            source = pieces[distance].at[:, rows, columns]
        return pltpu.make_async_copy(source, held.at[:, rows, :], arrived.at[at])

    @pl.when(step == 0)
    def _():
        for distance in range(cols):

            @pl.when(distance_now == distance)
            def _(distance=distance):
                for at in range(steps):
                    copy(distance, at).start()

        last[...] = jnp.where(place == 0, above[...], below[...])

    for at in range(steps):

        @pl.when(step == at)
        def _(at=at):
            copy(0, at).wait()

    rows = pl.ds(pl.multiple_of(step * tile, tile), tile)
    both = dot(held[:, rows, :].reshape(2 * tile, depth), last[...], ((1,), (0,)))
    rotated = part[...] + both[:tile] + both[tile:]
    one = BETA_ONE * first[...] + (1.0 - BETA_ONE) * rotated
    two = BETA_TWO * second[...] + (1.0 - BETA_TWO) * rotated * rotated
    new_first[...] = one
    new_second[...] = two
    high, low = kernel_split(one / (jnp.sqrt(two) + EPSILON))
    normed[0] = high
    normed[1] = low


def rotate(at, part, pieces, above, below, first, second, lines):
    cols = len(pieces)
    rows, width = first.shape
    depth = above.shape[0]
    tile = min(256, rows)
    block = pl.BlockSpec((tile, width), lambda i, s: (i, 0))
    pair = pl.BlockSpec((2, tile, width), lambda i, s: (0, i, 0))
    whole = pl.BlockSpec(above.shape, lambda i, s: (0, 0), pipeline_mode=pl.Buffered(1))
    return pl.pallas_call(
        functools.partial(rotate_kernel, cols=cols, lines=lines),
        grid_spec=pltpu.PrefetchScalarGridSpec(
            num_scalar_prefetch=1,
            grid=(rows // tile,),
            in_specs=[block, whole, whole, block, block]
            + [pl.BlockSpec(memory_space=pl.ANY)] * cols,
            out_specs=[block, block, pair],
            scratch_shapes=[
                pltpu.VMEM((2, rows, depth), BF16),
                pltpu.VMEM((depth, width), BF16),
                pltpu.SemaphoreType.DMA((rows // tile,)),
            ],
        ),
        out_shape=[
            jax.ShapeDtypeStruct((rows, width), F32),
            jax.ShapeDtypeStruct((rows, width), F32),
            jax.ShapeDtypeStruct((2, rows, width), BF16),
        ],
        compiler_params=params(40),
        cost_estimate=cost(4 * rows * width * depth, 30 * rows * width),
        name="rotate",
    )(at, part, above, below, first, second, *pieces)


def restore_kernel(at_ref, normed, *refs, cols, far):
    rows, (above, below, keep, mate, flipped) = refs[:cols], refs[cols:]
    tile, piece = normed.shape[1], keep.shape[2]
    me, place = at_ref[0], at_ref[1]

    @pl.when(pl.program_id(0) == 0)
    def _():
        for distance in range(cols):
            here = pl.ds(distance * piece, piece)
            late = (me ^ distance) == far - place

            @pl.when(jnp.logical_not(late & ((place == 0) | (place == far))))
            def _(distance=distance, here=here):
                flipped[:, here] = rows[distance][...].T

            @pl.when(late & (place == 0))
            def _(here=here):
                flipped[:, here] = above[...].T

            @pl.when(late & (place == far))
            def _(here=here):
                flipped[:, here] = below[...].T

    both = dot(normed[...].reshape(2 * tile, normed.shape[2]), flipped[...], ((1,), (0,)))
    term = both[:tile] + both[tile:]
    for distance in range(cols):
        out = mate if distance % 2 else keep
        out[distance // 2] = term[:, distance * piece : (distance + 1) * piece]


def restore(at, normed, right, above, below, cols, lines, chunk, piece):
    _, depth, inner = normed.shape
    tile = min(256, depth)
    aligned = above.shape[0] == inner
    far = lines - 1 if aligned else -cols
    out = pl.BlockSpec((cols // 2, tile, piece), lambda i, s: (0, i, 0))

    def rows(distance):
        return pl.BlockSpec((piece, inner), lambda i, s: ((s[0] ^ distance) * CHUNKS + chunk, 0))

    last = pl.BlockSpec((piece, inner), lambda i, s: (chunk if aligned else 0, 0))
    return pl.pallas_call(
        functools.partial(restore_kernel, cols=cols, far=far),
        grid_spec=pltpu.PrefetchScalarGridSpec(
            num_scalar_prefetch=1,
            grid=(depth // tile,),
            in_specs=[pl.BlockSpec((2, tile, inner), lambda i, s: (0, i, 0))]
            + [rows(distance) for distance in range(cols)]
            + [last, last],
            out_specs=[out, out],
            scratch_shapes=[pltpu.VMEM((inner, cols * piece), BF16)],
        ),
        out_shape=[jax.ShapeDtypeStruct((cols // 2, depth, piece), F32)] * 2,
        compiler_params=params(40),
        cost_estimate=cost(4 * depth * inner * piece * cols, 8 * depth * piece * cols),
        name="restore",
    )(at, normed, *([right] * cols), above, below)


def summed(keep, mate, codes):
    depth = keep.shape[1]
    scales = [scale_of(code, depth) for code in codes]

    def value_at(rows):
        value = keep[0, rows, :] + mate[0, rows, :]
        for code, scale in zip(codes, scales):
            value = value + decode(code[rows, :], scale)
        return value

    return value_at


def send_kernel(keep, mate, *refs, tile):
    codes, (message, total) = refs[:-2], refs[-2:]
    fill(message, total, summed(keep, mate, codes), tile)


def send(keep, mate, distance, codes):
    _, depth, piece = keep.shape
    tile = min(64, depth)
    pair = pl.BlockSpec((1, depth, piece), lambda i: (distance // 2, 0, 0))
    message = pl.BlockSpec((depth + EXTRA, piece), lambda i: (0, 0))
    return pl.pallas_call(
        functools.partial(send_kernel, tile=tile),
        grid=(1,),
        in_specs=[pair, pair] + [message] * len(codes),
        out_specs=message,
        out_shape=jax.ShapeDtypeStruct((depth + EXTRA, piece), BF16),
        scratch_shapes=[pltpu.VMEM((depth, piece), F32)],
        compiler_params=params(16),
        cost_estimate=cost(400 * depth * piece, 18 * depth * piece),
        name="send",
    )(keep, mate, *codes)


def expand_kernel(keep, mate, *refs, tile):
    codes, (left, out, both) = refs[:-3], refs[-3:]
    depth, piece = both.shape[0], out.shape[1]

    @pl.when(pl.program_id(0) == 0)
    def _():
        value_at = summed(keep, mate, codes)

        def put(i, carry):
            rows = pl.ds(pl.multiple_of(i * tile, tile), tile)
            high, low = kernel_split(value_at(rows))
            both[rows, :piece] = high
            both[rows, piece:] = low
            return carry

        lax.fori_loop(0, depth // tile, put, 0)

    product = dot(left[...], both[...], ((1,), (0,)))
    out[...] = product[:, :piece] + product[:, piece:]


def expand(keep, mate, codes, left):
    rows, inner = left.shape
    _, depth, piece = keep.shape
    step = min(1024, rows)
    pair = pl.BlockSpec((1, depth, piece), lambda i: (0, 0, 0))
    message = pl.BlockSpec((depth + EXTRA, piece), lambda i: (0, 0))
    return pl.pallas_call(
        functools.partial(expand_kernel, tile=min(64, depth)),
        grid=(rows // step,),
        in_specs=[pair, pair]
        + [message] * len(codes)
        + [pl.BlockSpec((step, inner), lambda i: (i, 0))],
        out_specs=pl.BlockSpec((step, piece), lambda i: (i, 0)),
        out_shape=jax.ShapeDtypeStruct((rows, piece), F32),
        scratch_shapes=[pltpu.VMEM((depth, 2 * piece), BF16)],
        compiler_params=params(48),
        cost_estimate=cost(4 * rows * inner * piece, 4 * rows * piece + 2 * rows * inner),
        name="expand",
    )(keep, mate, *codes, left)


def hop_kernel(place_ref, *refs, lines, step, tile):
    blocks, refs = refs[:2], refs[2:]
    arrived, outs, total = refs[:-3], refs[-3:-1], refs[-1]
    depth = total.shape[0]
    sends = (place_ref[0] < step, place_ref[0] >= lines - step)
    for way in range(2):

        @pl.when(sends[way])
        def _(way=way):
            scale = scale_of(arrived[way], depth) if arrived else None

            def value_at(rows):
                value = blocks[way][rows, :]
                if arrived:
                    value = value + decode(arrived[way][rows, :], scale)
                return value

            fill(outs[way], total, value_at, tile)


def hop(place, product, arrived, lines, step):
    depth, piece = product.shape[0] // lines, product.shape[1]
    ahead = lines - step
    message = pl.BlockSpec((depth + EXTRA, piece), lambda i, s: (0, 0))
    return pl.pallas_call(
        functools.partial(hop_kernel, lines=lines, step=step, tile=min(64, depth)),
        grid_spec=pltpu.PrefetchScalarGridSpec(
            num_scalar_prefetch=1,
            grid=(1,),
            in_specs=[
                pl.BlockSpec(
                    (depth, piece), lambda i, s: (jnp.minimum(s[0] + ahead, lines - 1), 0)
                ),
                pl.BlockSpec((depth, piece), lambda i, s: (jnp.maximum(s[0] - ahead, 0), 0)),
            ]
            + [message] * len(arrived),
            out_specs=[message] * 2,
            scratch_shapes=[pltpu.VMEM((depth, piece), F32)],
        ),
        out_shape=[jax.ShapeDtypeStruct((depth + EXTRA, piece), BF16)] * 2,
        compiler_params=params(48),
        cost_estimate=cost(400 * depth * piece, 12 * depth * piece),
        name="hop",
    )(place, product, product, *arrived)


def finish_kernel(at_ref, block, up, down, *refs, tile):
    out = refs[-1]
    depth = out.shape[0]
    scales = [scale_of(message, depth) for message in (up, down)]

    def add(i, carry):
        rows = pl.ds(pl.multiple_of(i * tile, tile), tile)
        out[rows, :] = (
            block[rows, :] + decode(up[rows, :], scales[0]) + decode(down[rows, :], scales[1])
        )
        return carry

    lax.fori_loop(0, depth // tile, add, 0)


def finish(at, product, arrived, update, chunk, depth, width):
    piece = product.shape[1]
    tile = min(64, depth)
    message = pl.BlockSpec((depth + EXTRA, piece), lambda i, s: (0, 0))
    extra = [] if update is None else [update]
    return pl.pallas_call(
        functools.partial(finish_kernel, tile=tile),
        grid_spec=pltpu.PrefetchScalarGridSpec(
            num_scalar_prefetch=1,
            grid=(1,),
            in_specs=[pl.BlockSpec((depth, piece), lambda i, s: (s[0], 0)), message, message]
            + [pl.BlockSpec(memory_space=pl.ANY)] * len(extra),
            out_specs=pl.BlockSpec((depth, piece), lambda i, s: (0, chunk)),
        ),
        out_shape=jax.ShapeDtypeStruct((depth, width), F32),
        input_output_aliases={4: 0} if extra else {},
        compiler_params=params(48),
        cost_estimate=cost(400 * depth * piece, 12 * depth * piece),
        name="finish",
    )(at, product, *arrived, *extra)


def build(lines, cols):
    def swap(value, distance):
        return lax.ppermute(value, "col", [(i, i ^ distance) for i in range(cols)])

    def by_distance(block):
        held = {0: block}
        for distance in range(2, cols, 2):
            held[distance] = swap(block, distance)
        for distance in range(0, cols, 2):
            held[distance + 1] = swap(held[distance], 1)
        return held

    def place_by_distance(block, me):
        out = jnp.zeros((cols,) + block.shape, block.dtype)
        for distance, value in by_distance(block).items():
            out = lax.dynamic_update_index_in_dim(out, value, me ^ distance, 0)
        return out

    def up(value, senders):
        return lax.ppermute(value, "row", [(i, i + 1) for i in senders])

    def down(value, senders):
        return lax.ppermute(value, "row", [(i, i - 1) for i in senders])

    def walk(held, step):
        held[-step] = up(held[1 - step], range(step - 1, lines - 1))
        held[step] = down(held[step - 1], range(1, lines - step + 1))

    def local(gradient, first_moment, second_moment, left_basis, right_basis):
        me, place = lax.axis_index("col"), lax.axis_index("row")
        depth, width = gradient.shape
        piece = width // CHUNKS
        far = lines - 1
        spot, at = jnp.reshape(place, (1,)), jnp.stack([me, place])
        barrier = lax.optimization_barrier
        near = [offset for offset in range(-far, far + 1) if abs(offset) < far]

        left = place_by_distance(left_basis, me).reshape(-1, left_basis.shape[1])
        grads = {0: gradient}
        for step in range(1, lines):
            if step == far:
                left, grads[1 - step], grads[step - 1] = barrier(
                    (left, grads[1 - step], grads[step - 1])
                )
            walk(grads, step)
        before = halfway(spot, left, grads, near, lines, None)

        own, before, grads[-far], grads[far] = barrier(
            (right_basis, before, grads[-far], grads[far])
        )
        rights = {0: own}
        right = jnp.zeros(((lines + 1) * depth, width), BF16)

        def put(right, offset):
            there = place + offset
            there = jnp.where((there >= 0) & (there < lines), there, lines)
            return lax.dynamic_update_slice_in_dim(right, rights[offset], there * depth, 0)

        for step in range(1, lines):
            walk(rights, step)
        above, below = rights[far], rights[-far]

        pair, message = pack(halfway(spot, left, grads, [-far, far], lines, before))
        message, rights[-1], rights[1] = barrier((message, rights[-1], rights[1]))
        pieces = by_distance(message)
        right = put(put(put(right, 0), -1), 1)
        right, pieces[cols - 2] = barrier((right, pieces[cols - 2]))
        for step in range(2, far if depth == width else lines):
            right = put(put(right, -step), step)
        pieces = [pair] + [unpack(pieces[distance]) for distance in range(1, cols)]
        part = rotate_part(at, pieces, right)
        part, above, below = barrier((part, above, below))
        if depth != width:
            above_now, below_now = jnp.zeros_like(above), jnp.zeros_like(below)
        else:
            above_now, below_now = above, below
        new_first, new_second, normed = rotate(
            at, part, pieces, above_now, below_now, first_moment, second_moment, lines
        )

        def pass_on(product, arrived, step):
            upward, downward = hop(spot, product, arrived, lines, step)
            return up(upward, range(0, step)), down(downward, range(lines - step, lines))

        products, arrived = [], []
        for chunk in range(CHUNKS):
            if chunk >= 2:
                step = chunk - 1
                if step > 1 and step < lines:
                    arrived[0] = pass_on(products[0], arrived[0], step)
                normed, arrived[0] = barrier((normed, arrived[0]))
            keep, mate = restore(at, normed, right, above, below, cols, lines, chunk, piece)
            mate = swap(mate, 1)
            crossed = [
                swap(send(keep, mate, distance, []), distance) for distance in range(2, cols, 2)
            ]
            products.append(expand(keep, mate, crossed, left))
            arrived.append(pass_on(products[chunk], (), 1))
        for step in range(2, lines):
            for chunk, product in enumerate(products):
                if chunk == 0 and step < CHUNKS - 1:
                    continue
                arrived[chunk] = pass_on(product, arrived[chunk], step)
        update = None
        for chunk, product in enumerate(products):
            update = finish(spot, product, arrived[chunk], update, chunk, depth, width)
        return (new_first, new_second, update)

    return local


def solution(mesh):
    return jax.shard_map(
        build(mesh.shape["row"], mesh.shape["col"]),
        mesh=mesh,
        in_specs=(
            P(("groups", "row"), "col"),
            P(("groups", "row"), "col"),
            P(("groups", "row"), "col"),
            P(("groups", "col"), "row"),
            P(("groups", "row"), "col"),
        ),
        out_specs=(
            P(("groups", "row"), "col"),
            P(("groups", "row"), "col"),
            P(("groups", "row"), "col"),
        ),
        check_vma=False,
    )
```

```python
import functools
import jax
import jax.numpy as jnp
from jax import lax
from jax.experimental import pallas as pl
from jax.experimental.pallas import tpu as pltpu
from jax.sharding import PartitionSpec as P

BETA_ONE = 0.9
BETA_TWO = 0.95
EPSILON = 1e-08
CHUNKS = 4
EXTRA = 16
F32 = jnp.float32
BF16 = jnp.bfloat16
MIB = 2**20


def params(mib):
    return pltpu.CompilerParams(vmem_limit_bytes=mib * MIB)


def cost(flops, moved, weight=4):
    return pl.CostEstimate(
        flops=int(flops * weight), bytes_accessed=int(moved * weight), transcendentals=0
    )


def split(value):
    high = lax.reduce_precision(value, exponent_bits=8, mantissa_bits=7)
    return high.astype(BF16), (value - high).astype(BF16)


def kernel_split(value):
    high = value.astype(BF16)
    return high, (value - high.astype(F32)).astype(BF16)


def dot(a, b, dims):
    return lax.dot_general(a, b, (dims, ((), ())), preferred_element_type=F32)


TOP = 7.5


def encode(value, inverse):
    code = jnp.abs(value) * (inverse * 2.0**TOP)
    for _ in range(4):
        code = code * code
    return jnp.where(value < 0, -code, code).astype(BF16)


def decode(code, scale):
    code = code.astype(F32)
    size = jnp.abs(code)
    root = jnp.exp2(jnp.log2(size) * 0.0625 - TOP) * scale
    root = jnp.where(size > 0, root, 0.0)
    return jnp.where(code < 0, -root, root)


def scale_of(message, depth):
    return jnp.max(message[depth : depth + EXTRA, :].astype(F32), axis=(0, 1), keepdims=True)


def fill(message, total, value_at, tile, again=None):
    depth, piece = message.shape[0] - EXTRA, message.shape[1]

    def add(i, top):
        rows = pl.ds(pl.multiple_of(i * tile, tile), tile)
        value = value_at(rows)
        if again is None:
            total[rows, :] = value
        return jnp.maximum(top, jnp.abs(value))

    top = lax.fori_loop(0, depth // tile, add, jnp.zeros((tile, piece), F32))
    top = jnp.maximum(jnp.max(top, axis=(0, 1), keepdims=True), 1e-30)
    scale = jnp.broadcast_to(top, (EXTRA, piece)).astype(BF16)
    message[depth : depth + EXTRA, :] = scale
    inverse = 1.0 / jnp.max(scale.astype(F32), axis=(0, 1), keepdims=True)

    def put(i, carry):
        rows = pl.ds(pl.multiple_of(i * tile, tile), tile)
        value = total[rows, :] if again is None else again(rows)
        message[rows, :] = encode(value, inverse)
        return carry

    lax.fori_loop(0, depth // tile, put, 0)


def halfway_kernel(place_ref, left, *refs, offsets, lines, first):
    pieces, refs = refs[: len(offsets)], refs[len(offsets) :]
    total = refs[-1]
    depth = pieces[0].shape[0]
    total[...] = jnp.zeros_like(total) if first else refs[0][...]
    place = place_ref[0]
    for offset, piece in zip(offsets, pieces):

        @pl.when((place + offset >= 0) & (place + offset < lines))
        def _(offset=offset, piece=piece):
            rows = left[pl.ds(pl.multiple_of((place + offset) * depth, depth), depth), :]
            total[...] += dot(rows, piece[...], ((0,), (0,)))

    refs[-2][...] = total[...]


def halfway(place, left, held, offsets, lines, before):
    pieces = [held[offset] for offset in offsets]
    depth, width = pieces[0].shape
    inner = left.shape[1]
    tile = min(256, inner)
    whole = pl.BlockSpec((depth, width), lambda i, s: (0, 0))
    block = pl.BlockSpec((tile, width), lambda i, s: (i, 0))
    extra = [] if before is None else [before]
    return pl.pallas_call(
        functools.partial(halfway_kernel, offsets=offsets, lines=lines, first=before is None),
        grid_spec=pltpu.PrefetchScalarGridSpec(
            num_scalar_prefetch=1,
            grid=(inner // tile,),
            in_specs=[pl.BlockSpec((left.shape[0], tile), lambda i, s: (0, i))]
            + [whole] * len(pieces)
            + [block] * len(extra),
            out_specs=block,
            scratch_shapes=[pltpu.VMEM((tile, width), F32)],
        ),
        out_shape=jax.ShapeDtypeStruct((inner, width), F32),
        compiler_params=params(48),
        cost_estimate=cost(8 * depth * inner * width, 8 * depth * inner, 0.3),
        name="halfway",
    )(place, left, *pieces, *extra)


def pack_kernel(value, pair, message, *, tile):
    depth, _ = value.shape

    def value_at(rows):
        now = value[rows, :]
        high, low = kernel_split(now)
        pair[0, rows, :] = high
        pair[1, rows, :] = low
        return now

    fill(message, None, value_at, tile, lambda rows: value[rows, :])


def pack(value):
    depth, width = value.shape
    return pl.pallas_call(
        functools.partial(pack_kernel, tile=min(16, depth)),
        out_shape=[
            jax.ShapeDtypeStruct((2, depth, width), BF16),
            jax.ShapeDtypeStruct((depth + EXTRA, width), BF16),
        ],
        compiler_params=params(60),
        cost_estimate=cost(400 * depth * width, 10 * depth * width, 0.3),
        name="pack",
    )(value)


def unpack_kernel(message, scales, pair, *, tile):
    _, depth, _ = pair.shape
    scale = scale_of(scales, 0)

    def put(i, carry):
        rows = pl.ds(pl.multiple_of(i * tile, tile), tile)
        high, low = kernel_split(decode(message[rows, :], scale))
        pair[0, rows, :] = high
        pair[1, rows, :] = low
        return carry

    lax.fori_loop(0, depth // tile, put, 0)


def unpack(message):
    depth, width = message.shape[0] - EXTRA, message.shape[1]
    step = min(256, depth)
    return pl.pallas_call(
        functools.partial(unpack_kernel, tile=min(16, step)),
        grid=(depth // step,),
        in_specs=[
            pl.BlockSpec((step, width), lambda i: (i, 0)),
            pl.BlockSpec((EXTRA, width), lambda i: (depth // EXTRA, 0)),
        ],
        out_specs=pl.BlockSpec((2, step, width), lambda i: (0, i, 0)),
        out_shape=jax.ShapeDtypeStruct((2, depth, width), BF16),
        compiler_params=params(60),
        cost_estimate=cost(400 * depth * width, 6 * depth * width, 0.3),
        name="unpack",
    )(message, message)


def put_kernel(there_ref, piece, *refs):
    right, flipped = refs[-2:]
    right[...] = piece[...]
    flipped[0] = piece[...].T


def put(there, piece, held, blocks):
    depth, width = piece.shape
    extra = [] if held is None else list(held)
    return pl.pallas_call(
        put_kernel,
        grid_spec=pltpu.PrefetchScalarGridSpec(
            num_scalar_prefetch=1,
            grid=(1,),
            in_specs=[pl.BlockSpec((depth, width), lambda i, s: (0, 0))]
            + [pl.BlockSpec(memory_space=pl.ANY)] * len(extra),
            out_specs=[
                pl.BlockSpec((depth, width), lambda i, s: (s[0], 0)),
                pl.BlockSpec((1, width, depth), lambda i, s: (s[0], 0, 0)),
            ],
        ),
        out_shape=[
            jax.ShapeDtypeStruct((blocks * depth, width), BF16),
            jax.ShapeDtypeStruct((blocks, width, depth), BF16),
        ],
        input_output_aliases={2: 0, 3: 1} if extra else {},
        compiler_params=params(60),
        cost_estimate=cost(0, 6 * depth * width, 0.3),
        name="put",
    )(there, piece, *extra)


def rotate_part_kernel(at_ref, *refs, cols, width, far):
    pieces, (right, out, total) = refs[:cols], refs[cols:]
    tile = out.shape[0]
    me, place = at_ref[0], at_ref[1]
    total[...] = jnp.zeros_like(total)
    for distance in range(cols):
        block = me ^ distance
        late = (block == far - place) & ((place == 0) | (place == far))

        @pl.when(jnp.logical_not(late))
        def _(distance=distance, block=block):
            rows = right[pl.ds(pl.multiple_of(block * width, width), width), :]
            total[...] += dot(pieces[distance][...].reshape(2 * tile, width), rows, ((1,), (0,)))

    out[...] = total[:tile, :] + total[tile:, :]


def rotate_part(at, pieces, right, far):
    cols = len(pieces)
    _, depth, width = pieces[0].shape
    tile = min(256, depth)
    return pl.pallas_call(
        functools.partial(rotate_part_kernel, cols=cols, width=width, far=far),
        grid_spec=pltpu.PrefetchScalarGridSpec(
            num_scalar_prefetch=1,
            grid=(depth // tile,),
            in_specs=[pl.BlockSpec((2, tile, width), lambda i, s: (0, i, 0))] * cols
            + [
                pl.BlockSpec(
                    (cols * width, width), lambda i, s: (0, 0), pipeline_mode=pl.Buffered(1)
                )
            ],
            out_specs=pl.BlockSpec((tile, width), lambda i, s: (i, 0)),
            scratch_shapes=[pltpu.VMEM((2 * tile, width), F32)],
        ),
        out_shape=jax.ShapeDtypeStruct((depth, width), F32),
        compiler_params=params(48),
        cost_estimate=cost(4 * depth * width * width * cols, 20 * depth * width, 0.3),
        name="rotate_part",
    )(at, *pieces, right)


def rotate_kernel(at_ref, part, above, below, first, second, *refs, cols, lines):
    pieces, (new_first, new_second, normed, held, last, arrived) = refs[:cols], refs[cols:]
    tile, width = first.shape
    depth = last.shape[0]
    me, place = at_ref[0], at_ref[1]
    step, steps = pl.program_id(0), held.shape[1] // tile
    start = (lines - 1 - place) * depth
    distance_now = me ^ (start // width)

    def copy(distance, at):
        rows = pl.ds(at * tile, tile)
        if depth == width:
            source = pieces[distance].at[:, rows, :]
        else:
            columns = pl.ds(pl.multiple_of(lax.rem(start, width), depth), depth)
            source = pieces[distance].at[:, rows, columns]
        return pltpu.make_async_copy(source, held.at[:, rows, :], arrived.at[at])

    @pl.when(step == 0)
    def _():
        for distance in range(cols):

            @pl.when(distance_now == distance)
            def _(distance=distance):
                for at in range(steps):
                    copy(distance, at).start()

        last[...] = jnp.where(place == 0, above[...], below[...])

    for at in range(steps):

        @pl.when(step == at)
        def _(at=at):
            copy(0, at).wait()

    rows = pl.ds(pl.multiple_of(step * tile, tile), tile)
    both = dot(held[:, rows, :].reshape(2 * tile, depth), last[...], ((1,), (0,)))
    rotated = part[...] + both[:tile] + both[tile:]
    one = BETA_ONE * first[...] + (1.0 - BETA_ONE) * rotated
    two = BETA_TWO * second[...] + (1.0 - BETA_TWO) * rotated * rotated
    new_first[...] = one
    new_second[...] = two
    high, low = kernel_split(one / (jnp.sqrt(two) + EPSILON))
    normed[0] = high
    normed[1] = low


def rotate(at, part, pieces, above, below, first, second, lines):
    cols = len(pieces)
    rows, width = first.shape
    depth = above.shape[0]
    tile = min(256, rows)
    block = pl.BlockSpec((tile, width), lambda i, s: (i, 0))
    pair = pl.BlockSpec((2, tile, width), lambda i, s: (0, i, 0))
    whole = pl.BlockSpec(above.shape, lambda i, s: (0, 0), pipeline_mode=pl.Buffered(1))
    return pl.pallas_call(
        functools.partial(rotate_kernel, cols=cols, lines=lines),
        grid_spec=pltpu.PrefetchScalarGridSpec(
            num_scalar_prefetch=1,
            grid=(rows // tile,),
            in_specs=[block, whole, whole, block, block]
            + [pl.BlockSpec(memory_space=pl.ANY)] * cols,
            out_specs=[block, block, pair],
            scratch_shapes=[
                pltpu.VMEM((2, rows, depth), BF16),
                pltpu.VMEM((depth, width), BF16),
                pltpu.SemaphoreType.DMA((rows // tile,)),
            ],
        ),
        out_shape=[
            jax.ShapeDtypeStruct((rows, width), F32),
            jax.ShapeDtypeStruct((rows, width), F32),
            jax.ShapeDtypeStruct((2, rows, width), BF16),
        ],
        compiler_params=params(40),
        cost_estimate=cost(4 * rows * width * depth, 30 * rows * width),
        name="rotate",
    )(at, part, above, below, first, second, *pieces)


def restore_kernel(me_ref, normed, *refs, cols):
    flipped, (keep, mate) = refs[:cols], refs[cols:]
    tile = normed.shape[1]
    both = normed[...].reshape(2 * tile, normed.shape[2])
    for distance in range(cols):
        term = dot(both, flipped[distance][0], ((1,), (0,)))
        (mate if distance % 2 else keep)[distance // 2] = term[:tile] + term[tile:]


def restore(me, normed, flipped, cols, chunk, piece):
    _, depth, inner = normed.shape
    wide = flipped.shape[2]
    tile = min(256, depth)
    out = pl.BlockSpec((cols // 2, tile, piece), lambda i, s: (0, i, 0))

    def columns(distance):
        def at(i, s):
            start = (s[0] ^ distance) * inner + chunk * piece
            return start // wide, 0, lax.rem(start, wide) // piece

        return pl.BlockSpec((1, inner, piece), at)

    return pl.pallas_call(
        functools.partial(restore_kernel, cols=cols),
        grid_spec=pltpu.PrefetchScalarGridSpec(
            num_scalar_prefetch=1,
            grid=(depth // tile,),
            in_specs=[pl.BlockSpec((2, tile, inner), lambda i, s: (0, i, 0))]
            + [columns(distance) for distance in range(cols)],
            out_specs=[out, out],
        ),
        out_shape=[jax.ShapeDtypeStruct((cols // 2, depth, piece), F32)] * 2,
        compiler_params=params(60),
        cost_estimate=cost(4 * depth * inner * piece * cols, 8 * depth * piece * cols),
        name="restore",
    )(me, normed, *([flipped] * cols))


def summed(keep, mate, codes):
    depth = keep.shape[1]
    scales = [scale_of(code, depth) for code in codes]

    def value_at(rows):
        value = keep[0, rows, :] + mate[0, rows, :]
        for code, scale in zip(codes, scales):
            value = value + decode(code[rows, :], scale)
        return value

    return value_at


def send_kernel(keep, mate, *refs, tile):
    codes, (message, total) = refs[:-2], refs[-2:]
    fill(message, total, summed(keep, mate, codes), tile)


def send(keep, mate, distance, codes):
    _, depth, piece = keep.shape
    tile = min(64, depth)
    pair = pl.BlockSpec((1, depth, piece), lambda i: (distance // 2, 0, 0))
    message = pl.BlockSpec((depth + EXTRA, piece), lambda i: (0, 0))
    return pl.pallas_call(
        functools.partial(send_kernel, tile=tile),
        grid=(1,),
        in_specs=[pair, pair] + [message] * len(codes),
        out_specs=message,
        out_shape=jax.ShapeDtypeStruct((depth + EXTRA, piece), BF16),
        scratch_shapes=[pltpu.VMEM((depth, piece), F32)],
        compiler_params=params(16),
        cost_estimate=cost(400 * depth * piece, 18 * depth * piece),
        name="send",
    )(keep, mate, *codes)


def expand_kernel(keep, mate, *refs, tile):
    codes, (left, out, both) = refs[:-3], refs[-3:]
    depth, piece = both.shape[0], out.shape[1]

    @pl.when(pl.program_id(0) == 0)
    def _():
        value_at = summed(keep, mate, codes)

        def put(i, carry):
            rows = pl.ds(pl.multiple_of(i * tile, tile), tile)
            high, low = kernel_split(value_at(rows))
            both[rows, :piece] = high
            both[rows, piece:] = low
            return carry

        lax.fori_loop(0, depth // tile, put, 0)

    product = dot(left[...], both[...], ((1,), (0,)))
    out[...] = product[:, :piece] + product[:, piece:]


def expand(keep, mate, codes, left):
    rows, inner = left.shape
    _, depth, piece = keep.shape
    step = min(1024, rows)
    pair = pl.BlockSpec((1, depth, piece), lambda i: (0, 0, 0))
    message = pl.BlockSpec((depth + EXTRA, piece), lambda i: (0, 0))
    return pl.pallas_call(
        functools.partial(expand_kernel, tile=min(64, depth)),
        grid=(rows // step,),
        in_specs=[pair, pair]
        + [message] * len(codes)
        + [pl.BlockSpec((step, inner), lambda i: (i, 0))],
        out_specs=pl.BlockSpec((step, piece), lambda i: (i, 0)),
        out_shape=jax.ShapeDtypeStruct((rows, piece), F32),
        scratch_shapes=[pltpu.VMEM((depth, 2 * piece), BF16)],
        compiler_params=params(48),
        cost_estimate=cost(4 * rows * inner * piece, 4 * rows * piece + 2 * rows * inner),
        name="expand",
    )(keep, mate, *codes, left)


def hop_kernel(place_ref, *refs, lines, step, tile):
    blocks, refs = refs[:2], refs[2:]
    arrived, outs, total = refs[:-3], refs[-3:-1], refs[-1]
    depth = total.shape[0]
    sends = (place_ref[0] < step, place_ref[0] >= lines - step)
    for way in range(2):

        @pl.when(sends[way])
        def _(way=way):
            scale = scale_of(arrived[way], depth) if arrived else None

            def value_at(rows):
                value = blocks[way][rows, :]
                if arrived:
                    value = value + decode(arrived[way][rows, :], scale)
                return value

            fill(outs[way], total, value_at, tile)


def hop(place, product, arrived, lines, step):
    depth, piece = product.shape[0] // lines, product.shape[1]
    ahead = lines - step
    message = pl.BlockSpec((depth + EXTRA, piece), lambda i, s: (0, 0))
    return pl.pallas_call(
        functools.partial(hop_kernel, lines=lines, step=step, tile=min(64, depth)),
        grid_spec=pltpu.PrefetchScalarGridSpec(
            num_scalar_prefetch=1,
            grid=(1,),
            in_specs=[
                pl.BlockSpec(
                    (depth, piece), lambda i, s: (jnp.minimum(s[0] + ahead, lines - 1), 0)
                ),
                pl.BlockSpec((depth, piece), lambda i, s: (jnp.maximum(s[0] - ahead, 0), 0)),
            ]
            + [message] * len(arrived),
            out_specs=[message] * 2,
            scratch_shapes=[pltpu.VMEM((depth, piece), F32)],
        ),
        out_shape=[jax.ShapeDtypeStruct((depth + EXTRA, piece), BF16)] * 2,
        compiler_params=params(48),
        cost_estimate=cost(400 * depth * piece, 12 * depth * piece),
        name="hop",
    )(place, product, product, *arrived)


def finish_kernel(at_ref, block, up, down, *refs, tile):
    out = refs[-1]
    depth = out.shape[0]
    scales = [scale_of(message, depth) for message in (up, down)]

    def add(i, carry):
        rows = pl.ds(pl.multiple_of(i * tile, tile), tile)
        out[rows, :] = (
            block[rows, :] + decode(up[rows, :], scales[0]) + decode(down[rows, :], scales[1])
        )
        return carry

    lax.fori_loop(0, depth // tile, add, 0)


def finish(at, product, arrived, update, chunk, depth, width):
    piece = product.shape[1]
    tile = min(64, depth)
    message = pl.BlockSpec((depth + EXTRA, piece), lambda i, s: (0, 0))
    extra = [] if update is None else [update]
    return pl.pallas_call(
        functools.partial(finish_kernel, tile=tile),
        grid_spec=pltpu.PrefetchScalarGridSpec(
            num_scalar_prefetch=1,
            grid=(1,),
            in_specs=[pl.BlockSpec((depth, piece), lambda i, s: (s[0], 0)), message, message]
            + [pl.BlockSpec(memory_space=pl.ANY)] * len(extra),
            out_specs=pl.BlockSpec((depth, piece), lambda i, s: (0, chunk)),
        ),
        out_shape=jax.ShapeDtypeStruct((depth, width), F32),
        input_output_aliases={4: 0} if extra else {},
        compiler_params=params(48),
        cost_estimate=cost(400 * depth * piece, 12 * depth * piece),
        name="finish",
    )(at, product, *arrived, *extra)


def build(lines, cols):
    def swap(value, distance):
        return lax.ppermute(value, "col", [(i, i ^ distance) for i in range(cols)])

    def by_distance(block):
        held = {0: block}
        for distance in range(2, cols, 2):
            held[distance] = swap(block, distance)
        for distance in range(0, cols, 2):
            held[distance + 1] = swap(held[distance], 1)
        return held

    def place_by_distance(block, me):
        out = jnp.zeros((cols,) + block.shape, block.dtype)
        for distance, value in by_distance(block).items():
            out = lax.dynamic_update_index_in_dim(out, value, me ^ distance, 0)
        return out

    def up(value, senders):
        return lax.ppermute(value, "row", [(i, i + 1) for i in senders])

    def down(value, senders):
        return lax.ppermute(value, "row", [(i, i - 1) for i in senders])

    def after(value, *others):
        return lax.optimization_barrier((value,) + others)[0]

    def walk(held, step):
        held[-step] = up(held[1 - step], range(step - 1, lines - 1))
        held[step] = down(held[step - 1], range(1, lines - step + 1))

    def local(gradient, first_moment, second_moment, left_basis, right_basis):
        me, place = lax.axis_index("col"), lax.axis_index("row")
        depth, width = gradient.shape
        piece = width // CHUNKS
        far = lines - 1
        spot, at = jnp.reshape(place, (1,)), jnp.stack([me, place])
        me_now = jnp.reshape(me, (1,))
        barrier = lax.optimization_barrier
        near = [offset for offset in range(-far, far + 1) if abs(offset) < far]

        left = place_by_distance(left_basis, me).reshape(-1, left_basis.shape[1])
        grads = {0: gradient}
        for step in range(1, lines):
            if step == far:
                left, grads[1 - step], grads[step - 1] = barrier(
                    (left, grads[1 - step], grads[step - 1])
                )
            walk(grads, step)
        before = halfway(spot, left, grads, near, lines, None)

        own, before, grads[-far], grads[far] = barrier(
            (right_basis, before, grads[-far], grads[far])
        )
        rights = {0: own}
        for step in range(1, lines):
            walk(rights, step)
        above, below = rights[far], rights[-far]

        pair, message = pack(halfway(spot, left, grads, [-far, far], lines, before))
        message, rights[-1], rights[1] = barrier((message, rights[-1], rights[1]))
        aligned = depth == width

        def put_block(held, offset):
            there = place + offset
            there = jnp.where((there >= 0) & (there < lines), there, lines)
            return put(jnp.reshape(there, (1,)), rights[offset], held, lines + 1)

        held = None
        for offset in (0, -1, 1):
            held = put_block(held, offset)
        pieces = {1: swap(message, 1)}
        mate_pair = unpack(pieces[1])
        for distance in range(2, cols, 2):
            pieces[distance] = after(swap(message, distance), held[1], mate_pair)
            pieces[distance + 1] = swap(pieces[distance], 1)
        for step in range(2, far if aligned else lines):
            held = put_block(put_block(held, -step), step)
        pieces = [pair, mate_pair] + [unpack(pieces[distance]) for distance in range(2, cols)]
        part = rotate_part(at, pieces, held[0], far if aligned else -1)
        part, above, below = barrier((part, above, below))
        if not aligned:
            above, below = jnp.zeros_like(above), jnp.zeros_like(below)
        new_first, new_second, normed = rotate(
            at, part, pieces, above, below, first_moment, second_moment, lines
        )
        if aligned:
            last = jnp.where(place == 0, above, below)
            there = jnp.where((place == 0) | (place == far), far - place, lines)
            held = put(jnp.reshape(there, (1,)), last, held, lines + 1)
        flipped = held[1]

        keeps, products, sent, hops = [], [], [], {}

        def running(chunk, step):
            if step > 1:
                upward, downward = running(chunk, step - 1)
                before = (
                    up(upward, range(0, step - 1)),
                    down(downward, range(lines - step + 1, lines)),
                )
            if (chunk, step) not in hops:
                arrived = () if step == 1 else before
                hops[chunk, step] = hop(spot, products[chunk], arrived, lines, step)
            return hops[chunk, step]

        for chunk in range(CHUNKS):
            ready = after(normed, *sent[-1]) if chunk else normed
            keep, mate = restore(me_now, ready, flipped, cols, chunk, piece)
            mate = swap(mate, 1)
            if chunk:
                mate = after(mate, *running(chunk - 1, 1))
            sent.append([send(keep, mate, distance, []) for distance in range(2, cols, 2)])
            crossed = [swap(code, 2 * index + 2) for index, code in enumerate(sent[-1])]
            due = [
                message
                for earlier in range(max(0, chunk - 2), chunk)
                if chunk - earlier + 1 < lines
                for message in running(earlier, chunk - earlier + 1)
            ]
            if due and crossed:
                crossed[0] = after(crossed[0], *due)
            products.append(expand(keep, mate, crossed, left))
        arrived = []
        for chunk in range(CHUNKS):
            upward, downward = running(chunk, far)
            arrived.append((up(upward, range(0, far)), down(downward, range(1, lines))))
        update = None
        for chunk, product in enumerate(products):
            update = finish(spot, product, arrived[chunk], update, chunk, depth, width)
        return (new_first, new_second, update)

    return local


def solution(mesh):
    return jax.shard_map(
        build(mesh.shape["row"], mesh.shape["col"]),
        mesh=mesh,
        in_specs=(
            P(("groups", "row"), "col"),
            P(("groups", "row"), "col"),
            P(("groups", "row"), "col"),
            P(("groups", "col"), "row"),
            P(("groups", "row"), "col"),
        ),
        out_specs=(
            P(("groups", "row"), "col"),
            P(("groups", "row"), "col"),
            P(("groups", "row"), "col"),
        ),
        check_vma=False,
    )
```

```python
import functools
import jax
import jax.numpy as jnp
from jax import lax
from jax.experimental import pallas as pl
from jax.experimental.pallas import tpu as pltpu
from jax.sharding import PartitionSpec as P

BETA_ONE = 0.9
BETA_TWO = 0.95
EPSILON = 1e-08
CHUNKS = 4
EXTRA = 16
F32 = jnp.float32
BF16 = jnp.bfloat16
MIB = 2**20


def params(mib):
    return pltpu.CompilerParams(vmem_limit_bytes=mib * MIB)


def cost(flops, moved, weight=4):
    return pl.CostEstimate(
        flops=int(flops * weight), bytes_accessed=int(moved * weight), transcendentals=0
    )


def split(value):
    high = lax.reduce_precision(value, exponent_bits=8, mantissa_bits=7)
    return high.astype(BF16), (value - high).astype(BF16)


def kernel_split(value):
    high = value.astype(BF16)
    return high, (value - high.astype(F32)).astype(BF16)


def dot(a, b, dims):
    return lax.dot_general(a, b, (dims, ((), ())), preferred_element_type=F32)


TOP = 7.5


def encode(value, inverse):
    code = jnp.abs(value) * (inverse * 2.0**TOP)
    for _ in range(4):
        code = code * code
    return jnp.where(value < 0, -code, code).astype(BF16)


def decode(code, scale):
    code = code.astype(F32)
    size = jnp.abs(code)
    root = jnp.exp2(jnp.log2(size) * 0.0625 - TOP) * scale
    root = jnp.where(size > 0, root, 0.0)
    return jnp.where(code < 0, -root, root)


def scale_of(message, depth):
    return jnp.max(message[depth : depth + EXTRA, :].astype(F32), axis=(0, 1), keepdims=True)


def fill(message, total, value_at, tile, again=None):
    depth, piece = message.shape[0] - EXTRA, message.shape[1]

    def add(i, top):
        rows = pl.ds(pl.multiple_of(i * tile, tile), tile)
        value = value_at(rows)
        if again is None:
            total[rows, :] = value
        return jnp.maximum(top, jnp.abs(value))

    top = lax.fori_loop(0, depth // tile, add, jnp.zeros((tile, piece), F32))
    top = jnp.maximum(jnp.max(top, axis=(0, 1), keepdims=True), 1e-30)
    scale = jnp.broadcast_to(top, (EXTRA, piece)).astype(BF16)
    message[depth : depth + EXTRA, :] = scale
    inverse = 1.0 / jnp.max(scale.astype(F32), axis=(0, 1), keepdims=True)

    def put(i, carry):
        rows = pl.ds(pl.multiple_of(i * tile, tile), tile)
        value = total[rows, :] if again is None else again(rows)
        message[rows, :] = encode(value, inverse)
        return carry

    lax.fori_loop(0, depth // tile, put, 0)


def halfway_kernel(place_ref, left, *refs, offsets, lines, first):
    pieces, refs = refs[: len(offsets)], refs[len(offsets) :]
    total = refs[-1]
    depth = pieces[0].shape[0]
    total[...] = jnp.zeros_like(total) if first else refs[0][...]
    place = place_ref[0]
    for offset, piece in zip(offsets, pieces):

        @pl.when((place + offset >= 0) & (place + offset < lines))
        def _(offset=offset, piece=piece):
            rows = left[pl.ds(pl.multiple_of((place + offset) * depth, depth), depth), :]
            total[...] += dot(rows, piece[...], ((0,), (0,)))

    refs[-2][...] = total[...]


def halfway(place, left, held, offsets, lines, before):
    pieces = [held[offset] for offset in offsets]
    depth, width = pieces[0].shape
    inner = left.shape[1]
    tile = min(256, inner)
    whole = pl.BlockSpec((depth, width), lambda i, s: (0, 0))
    block = pl.BlockSpec((tile, width), lambda i, s: (i, 0))
    extra = [] if before is None else [before]
    return pl.pallas_call(
        functools.partial(halfway_kernel, offsets=offsets, lines=lines, first=before is None),
        grid_spec=pltpu.PrefetchScalarGridSpec(
            num_scalar_prefetch=1,
            grid=(inner // tile,),
            in_specs=[pl.BlockSpec((left.shape[0], tile), lambda i, s: (0, i))]
            + [whole] * len(pieces)
            + [block] * len(extra),
            out_specs=block,
            scratch_shapes=[pltpu.VMEM((tile, width), F32)],
        ),
        out_shape=jax.ShapeDtypeStruct((inner, width), F32),
        compiler_params=params(48),
        cost_estimate=cost(8 * depth * inner * width, 8 * depth * inner, 0.3),
        name="halfway",
    )(place, left, *pieces, *extra)


def pack_kernel(value, pair, message, *, tile):
    depth, _ = value.shape

    def value_at(rows):
        now = value[rows, :]
        high, low = kernel_split(now)
        pair[0, rows, :] = high
        pair[1, rows, :] = low
        return now

    fill(message, None, value_at, tile, lambda rows: value[rows, :])


def pack(value):
    depth, width = value.shape
    return pl.pallas_call(
        functools.partial(pack_kernel, tile=min(16, depth)),
        out_shape=[
            jax.ShapeDtypeStruct((2, depth, width), BF16),
            jax.ShapeDtypeStruct((depth + EXTRA, width), BF16),
        ],
        compiler_params=params(60),
        cost_estimate=cost(400 * depth * width, 10 * depth * width, 0.3),
        name="pack",
    )(value)


def unpack_kernel(message, scales, pair, *, tile):
    _, depth, _ = pair.shape
    scale = scale_of(scales, 0)

    def put(i, carry):
        rows = pl.ds(pl.multiple_of(i * tile, tile), tile)
        high, low = kernel_split(decode(message[rows, :], scale))
        pair[0, rows, :] = high
        pair[1, rows, :] = low
        return carry

    lax.fori_loop(0, depth // tile, put, 0)


def unpack(message):
    depth, width = message.shape[0] - EXTRA, message.shape[1]
    step = min(256, depth)
    return pl.pallas_call(
        functools.partial(unpack_kernel, tile=min(16, step)),
        grid=(depth // step,),
        in_specs=[
            pl.BlockSpec((step, width), lambda i: (i, 0)),
            pl.BlockSpec((EXTRA, width), lambda i: (depth // EXTRA, 0)),
        ],
        out_specs=pl.BlockSpec((2, step, width), lambda i: (0, i, 0)),
        out_shape=jax.ShapeDtypeStruct((2, depth, width), BF16),
        compiler_params=params(60),
        cost_estimate=cost(400 * depth * width, 6 * depth * width, 0.3),
        name="unpack",
    )(message, message)


def put_kernel(there_ref, piece, *refs):
    right, flipped = refs[-2:]
    right[...] = piece[...]
    flipped[0] = piece[...].T


def put(there, piece, held, blocks):
    depth, width = piece.shape
    extra = [] if held is None else list(held)
    return pl.pallas_call(
        put_kernel,
        grid_spec=pltpu.PrefetchScalarGridSpec(
            num_scalar_prefetch=1,
            grid=(1,),
            in_specs=[pl.BlockSpec((depth, width), lambda i, s: (0, 0))]
            + [pl.BlockSpec(memory_space=pl.ANY)] * len(extra),
            out_specs=[
                pl.BlockSpec((depth, width), lambda i, s: (s[0], 0)),
                pl.BlockSpec((1, width, depth), lambda i, s: (s[0], 0, 0)),
            ],
        ),
        out_shape=[
            jax.ShapeDtypeStruct((blocks * depth, width), BF16),
            jax.ShapeDtypeStruct((blocks, width, depth), BF16),
        ],
        input_output_aliases={2: 0, 3: 1} if extra else {},
        compiler_params=params(60),
        cost_estimate=cost(0, 6 * depth * width, 0.3),
        name="put",
    )(there, piece, *extra)


def rotate_part_kernel(at_ref, *refs, cols, width, far):
    pieces, (right, out, total) = refs[:cols], refs[cols:]
    tile = out.shape[0]
    me, place = at_ref[0], at_ref[1]
    total[...] = jnp.zeros_like(total)
    for distance in range(cols):
        block = me ^ distance
        late = (block == far - place) & ((place == 0) | (place == far))

        @pl.when(jnp.logical_not(late))
        def _(distance=distance, block=block):
            rows = right[pl.ds(pl.multiple_of(block * width, width), width), :]
            total[...] += dot(pieces[distance][...].reshape(2 * tile, width), rows, ((1,), (0,)))

    out[...] = total[:tile, :] + total[tile:, :]


def rotate_part(at, pieces, right, far):
    cols = len(pieces)
    _, depth, width = pieces[0].shape
    tile = min(256, depth)
    return pl.pallas_call(
        functools.partial(rotate_part_kernel, cols=cols, width=width, far=far),
        grid_spec=pltpu.PrefetchScalarGridSpec(
            num_scalar_prefetch=1,
            grid=(depth // tile,),
            in_specs=[pl.BlockSpec((2, tile, width), lambda i, s: (0, i, 0))] * cols
            + [
                pl.BlockSpec(
                    (cols * width, width), lambda i, s: (0, 0), pipeline_mode=pl.Buffered(1)
                )
            ],
            out_specs=pl.BlockSpec((tile, width), lambda i, s: (i, 0)),
            scratch_shapes=[pltpu.VMEM((2 * tile, width), F32)],
        ),
        out_shape=jax.ShapeDtypeStruct((depth, width), F32),
        compiler_params=params(48),
        cost_estimate=cost(4 * depth * width * width * cols, 20 * depth * width, 0.3),
        name="rotate_part",
    )(at, *pieces, right)


def rotate_kernel(at_ref, part, above, below, first, second, *refs, cols, lines):
    pieces, (new_first, new_second, normed, held, last, arrived) = refs[:cols], refs[cols:]
    tile, width = first.shape
    depth = last.shape[0]
    me, place = at_ref[0], at_ref[1]
    step, steps = pl.program_id(0), held.shape[1] // tile
    start = (lines - 1 - place) * depth
    distance_now = me ^ (start // width)

    def copy(distance, at):
        rows = pl.ds(at * tile, tile)
        if depth == width:
            source = pieces[distance].at[:, rows, :]
        else:
            columns = pl.ds(pl.multiple_of(lax.rem(start, width), depth), depth)
            source = pieces[distance].at[:, rows, columns]
        return pltpu.make_async_copy(source, held.at[:, rows, :], arrived.at[at])

    @pl.when(step == 0)
    def _():
        for distance in range(cols):

            @pl.when(distance_now == distance)
            def _(distance=distance):
                for at in range(steps):
                    copy(distance, at).start()

        last[...] = jnp.where(place == 0, above[...], below[...])

    for at in range(steps):

        @pl.when(step == at)
        def _(at=at):
            copy(0, at).wait()

    rows = pl.ds(pl.multiple_of(step * tile, tile), tile)
    both = dot(held[:, rows, :].reshape(2 * tile, depth), last[...], ((1,), (0,)))
    rotated = part[...] + both[:tile] + both[tile:]
    one = BETA_ONE * first[...] + (1.0 - BETA_ONE) * rotated
    two = BETA_TWO * second[...] + (1.0 - BETA_TWO) * rotated * rotated
    new_first[...] = one
    new_second[...] = two
    high, low = kernel_split(one / (jnp.sqrt(two) + EPSILON))
    normed[0] = high
    normed[1] = low


def rotate(at, part, pieces, above, below, first, second, lines):
    cols = len(pieces)
    rows, width = first.shape
    depth = above.shape[0]
    tile = min(256, rows)
    block = pl.BlockSpec((tile, width), lambda i, s: (i, 0))
    pair = pl.BlockSpec((2, tile, width), lambda i, s: (0, i, 0))
    whole = pl.BlockSpec(above.shape, lambda i, s: (0, 0), pipeline_mode=pl.Buffered(1))
    return pl.pallas_call(
        functools.partial(rotate_kernel, cols=cols, lines=lines),
        grid_spec=pltpu.PrefetchScalarGridSpec(
            num_scalar_prefetch=1,
            grid=(rows // tile,),
            in_specs=[block, whole, whole, block, block]
            + [pl.BlockSpec(memory_space=pl.ANY)] * cols,
            out_specs=[block, block, pair],
            scratch_shapes=[
                pltpu.VMEM((2, rows, depth), BF16),
                pltpu.VMEM((depth, width), BF16),
                pltpu.SemaphoreType.DMA((rows // tile,)),
            ],
        ),
        out_shape=[
            jax.ShapeDtypeStruct((rows, width), F32),
            jax.ShapeDtypeStruct((rows, width), F32),
            jax.ShapeDtypeStruct((2, rows, width), BF16),
        ],
        compiler_params=params(60),
        cost_estimate=cost(4 * rows * width * depth, 30 * rows * width),
        name="rotate",
    )(at, part, above, below, first, second, *pieces)


def restore_kernel(me_ref, normed, *refs, cols):
    flipped, (keep, mate) = refs[:cols], refs[cols:]
    tile = normed.shape[1]
    both = normed[...].reshape(2 * tile, normed.shape[2])
    for distance in range(cols):
        term = dot(both, flipped[distance][0], ((1,), (0,)))
        (mate if distance % 2 else keep)[distance // 2] = term[:tile] + term[tile:]


def restore(me, normed, flipped, cols, chunk, piece):
    _, depth, inner = normed.shape
    wide = flipped.shape[2]
    tile = min(256, depth)
    out = pl.BlockSpec((cols // 2, tile, piece), lambda i, s: (0, i, 0))

    def columns(distance):
        def at(i, s):
            start = (s[0] ^ distance) * inner + chunk * piece
            return start // wide, 0, lax.rem(start, wide) // piece

        return pl.BlockSpec((1, inner, piece), at)

    return pl.pallas_call(
        functools.partial(restore_kernel, cols=cols),
        grid_spec=pltpu.PrefetchScalarGridSpec(
            num_scalar_prefetch=1,
            grid=(depth // tile,),
            in_specs=[pl.BlockSpec((2, tile, inner), lambda i, s: (0, i, 0))]
            + [columns(distance) for distance in range(cols)],
            out_specs=[out, out],
        ),
        out_shape=[jax.ShapeDtypeStruct((cols // 2, depth, piece), F32)] * 2,
        compiler_params=params(60),
        cost_estimate=cost(4 * depth * inner * piece * cols, 8 * depth * piece * cols, 4),
        name="restore",
    )(me, normed, *([flipped] * cols))


def summed(keep, mate, codes):
    depth = keep.shape[1]
    scales = [scale_of(code, depth) for code in codes]

    def value_at(rows):
        value = keep[0, rows, :] + mate[0, rows, :]
        for code, scale in zip(codes, scales):
            value = value + decode(code[rows, :], scale)
        return value

    return value_at


def send_kernel(keep, mate, *refs, tile):
    codes, (message, total) = refs[:-2], refs[-2:]
    fill(message, total, summed(keep, mate, codes), tile)


def send(keep, mate, distance, codes):
    _, depth, piece = keep.shape
    tile = min(64, depth)
    pair = pl.BlockSpec((1, depth, piece), lambda i: (distance // 2, 0, 0))
    message = pl.BlockSpec((depth + EXTRA, piece), lambda i: (0, 0))
    return pl.pallas_call(
        functools.partial(send_kernel, tile=tile),
        grid=(1,),
        in_specs=[pair, pair] + [message] * len(codes),
        out_specs=message,
        out_shape=jax.ShapeDtypeStruct((depth + EXTRA, piece), BF16),
        scratch_shapes=[pltpu.VMEM((depth, piece), F32)],
        compiler_params=params(16),
        cost_estimate=cost(400 * depth * piece, 18 * depth * piece, 4),
        name="send",
    )(keep, mate, *codes)


def expand_send_kernel(place_ref, keep, mate, *refs, tile):
    codes, (left, message, both, total) = refs[:-4], refs[-4:]
    depth, piece = total.shape

    @pl.when(pl.program_id(0) == 0)
    def _():
        value_at = summed(keep, mate, codes)

        def put(i, carry):
            rows = pl.ds(pl.multiple_of(i * tile, tile), tile)
            high, low = kernel_split(value_at(rows))
            both[rows, :piece] = high
            both[rows, piece:] = low
            return carry

        lax.fori_loop(0, both.shape[0] // tile, put, 0)

    product = dot(left[...], both[...], ((1,), (0,)))
    total[...] = product[:, :piece] + product[:, piece:]
    fill(message, None, lambda rows: total[rows, :], tile, lambda rows: total[rows, :])


def expand_send(place, keep, mate, codes, left, depth):
    inner, piece = keep.shape[1:]
    count = left.shape[0] // depth // 2
    pair = pl.BlockSpec((1, inner, piece), lambda i, s: (0, 0, 0))
    code = pl.BlockSpec((inner + EXTRA, piece), lambda i, s: (0, 0))
    return pl.pallas_call(
        functools.partial(expand_send_kernel, tile=min(64, depth)),
        grid_spec=pltpu.PrefetchScalarGridSpec(
            num_scalar_prefetch=1,
            grid=(count,),
            in_specs=[pair, pair]
            + [code] * len(codes)
            + [pl.BlockSpec((depth, inner), lambda i, s: (s[0] ^ (2 * i + 1), 0))],
            out_specs=[
                pl.BlockSpec((None, depth + EXTRA, piece), lambda i, s: (i, 0, 0)),
                pl.BlockSpec((inner, 2 * piece), lambda i, s: (0, 0)),
            ],
            scratch_shapes=[pltpu.VMEM((depth, piece), F32)],
        ),
        out_shape=[
            jax.ShapeDtypeStruct((count, depth + EXTRA, piece), BF16),
            jax.ShapeDtypeStruct((inner, 2 * piece), BF16),
        ],
        compiler_params=params(40),
        cost_estimate=cost(4 * count * depth * inner * piece, 4 * depth * inner, 4),
        name="expand_send",
    )(place, keep, mate, *codes, left)


def expand_keep_kernel(place_ref, both, left, out):
    piece = out.shape[1]
    product = dot(left[...], both[...], ((1,), (0,)))
    out[...] = product[:, :piece] + product[:, piece:]


def expand_keep(place, both, left, depth):
    inner, piece = both.shape[0], both.shape[1] // 2
    count = left.shape[0] // depth // 2
    return pl.pallas_call(
        expand_keep_kernel,
        grid_spec=pltpu.PrefetchScalarGridSpec(
            num_scalar_prefetch=1,
            grid=(count,),
            in_specs=[
                pl.BlockSpec((inner, 2 * piece), lambda i, s: (0, 0)),
                pl.BlockSpec((depth, inner), lambda i, s: (s[0] ^ (2 * i), 0)),
            ],
            out_specs=pl.BlockSpec((None, depth, piece), lambda i, s: (i, 0, 0)),
        ),
        out_shape=jax.ShapeDtypeStruct((count, depth, piece), F32),
        compiler_params=params(60),
        cost_estimate=cost(4 * count * depth * inner * piece, 4 * depth * inner, 4),
        name="expand_keep",
    )(place, both, left)


def hop_kernel(kept, *refs, tile):
    arrived, (message, total) = refs[:-2], refs[-2:]
    depth = total.shape[0]
    scales = [scale_of(code, depth) for code in arrived]

    def value_at(rows):
        value = kept[rows, :]
        for code, scale in zip(arrived, scales):
            value = value + decode(code[rows, :], scale)
        return value

    fill(message, total, value_at, tile)


def hop(kept, arrived, step):
    _, depth, piece = kept.shape
    count = arrived[-1].shape[0] // 2

    def at(shift):
        return lambda i: ((2 * i + 1) * 2**shift, 0, 0)

    return pl.pallas_call(
        functools.partial(hop_kernel, tile=min(64, depth)),
        grid=(count,),
        in_specs=[pl.BlockSpec((None, depth, piece), at(step - 1))]
        + [
            pl.BlockSpec((None, depth + EXTRA, piece), at(step - 1 - index))
            for index in range(len(arrived))
        ],
        out_specs=pl.BlockSpec((None, depth + EXTRA, piece), lambda i: (i, 0, 0)),
        out_shape=jax.ShapeDtypeStruct((count, depth + EXTRA, piece), BF16),
        scratch_shapes=[pltpu.VMEM((depth, piece), F32)],
        compiler_params=params(40),
        cost_estimate=cost(400 * count * depth * piece, 12 * count * depth * piece, 4),
        name="hop",
    )(kept, *arrived)


def finish_kernel(kept, *refs, tile, terms):
    arrived, out = refs[:terms], refs[-1]
    depth = out.shape[0]
    scales = [scale_of(code, depth) for code in arrived]

    def add(i, carry):
        rows = pl.ds(pl.multiple_of(i * tile, tile), tile)
        value = kept[rows, :]
        for code, scale in zip(arrived, scales):
            value = value + decode(code[rows, :], scale)
        out[rows, :] = value
        return carry

    lax.fori_loop(0, depth // tile, add, 0)


def finish(kept, arrived, update, chunk, width):
    _, depth, piece = kept.shape
    extra = [] if update is None else [update]
    first = lambda i: (0, 0, 0)
    return pl.pallas_call(
        functools.partial(finish_kernel, tile=min(64, depth), terms=len(arrived)),
        grid=(1,),
        in_specs=[pl.BlockSpec((None, depth, piece), first)]
        + [pl.BlockSpec((None, depth + EXTRA, piece), first)] * len(arrived)
        + [pl.BlockSpec(memory_space=pl.ANY)] * len(extra),
        out_specs=pl.BlockSpec((depth, piece), lambda i: (0, chunk)),
        out_shape=jax.ShapeDtypeStruct((depth, width), F32),
        input_output_aliases={1 + len(arrived): 0} if extra else {},
        compiler_params=params(40),
        cost_estimate=cost(400 * depth * piece, 12 * depth * piece, 0.1),
        name="finish",
    )(kept, *arrived, *extra)


def build(lines, cols):
    def swap(value, distance):
        return lax.ppermute(value, "col", [(i, i ^ distance) for i in range(cols)])

    def by_distance(block):
        held = {0: block}
        for distance in range(2, cols, 2):
            held[distance] = swap(block, distance)
        for distance in range(0, cols, 2):
            held[distance + 1] = swap(held[distance], 1)
        return held

    def place_by_distance(block, me):
        out = jnp.zeros((cols,) + block.shape, block.dtype)
        for distance, value in by_distance(block).items():
            out = lax.dynamic_update_index_in_dim(out, value, me ^ distance, 0)
        return out

    def up(value, senders):
        return lax.ppermute(value, "row", [(i, i + 1) for i in senders])

    def down(value, senders):
        return lax.ppermute(value, "row", [(i, i - 1) for i in senders])

    def after(value, *others):
        return lax.optimization_barrier((value,) + others)[0]

    def walk(held, step):
        held[-step] = up(held[1 - step], range(step - 1, lines - 1))
        held[step] = down(held[step - 1], range(1, lines - step + 1))

    def local(gradient, first_moment, second_moment, left_basis, right_basis):
        me, place = lax.axis_index("col"), lax.axis_index("row")
        depth, width = gradient.shape
        piece = width // CHUNKS
        far = lines - 1
        spot, at = jnp.reshape(place, (1,)), jnp.stack([me, place])
        me_now = jnp.reshape(me, (1,))
        barrier = lax.optimization_barrier
        near = [offset for offset in range(-far, far + 1) if abs(offset) < far]

        left = place_by_distance(left_basis, me).reshape(-1, left_basis.shape[1])
        grads = {0: gradient}
        for step in range(1, lines):
            if step == far:
                left, grads[1 - step], grads[step - 1] = barrier(
                    (left, grads[1 - step], grads[step - 1])
                )
            walk(grads, step)
        before = halfway(spot, left, grads, near, lines, None)

        own, before, grads[-far], grads[far] = barrier(
            (right_basis, before, grads[-far], grads[far])
        )
        rights = {0: own}
        for step in range(1, lines):
            walk(rights, step)
        above, below = rights[far], rights[-far]

        pair, message = pack(halfway(spot, left, grads, [-far, far], lines, before))
        message, rights[-1], rights[1] = barrier((message, rights[-1], rights[1]))
        aligned = depth == width

        def put_block(held, offset):
            there = place + offset
            there = jnp.where((there >= 0) & (there < lines), there, lines)
            return put(jnp.reshape(there, (1,)), rights[offset], held, lines + 1)

        held = None
        for offset in (0, -1, 1):
            held = put_block(held, offset)
        pieces = {1: swap(message, 1)}
        mate_pair = unpack(pieces[1])
        for distance in range(2, cols, 2):
            pieces[distance] = after(swap(message, distance), held[1], mate_pair)
            pieces[distance + 1] = swap(pieces[distance], 1)
        for step in range(2, far if aligned else lines):
            held = put_block(put_block(held, -step), step)
        pieces = [pair, mate_pair] + [unpack(pieces[distance]) for distance in range(2, cols)]
        part = rotate_part(at, pieces, held[0], far if aligned else -1)
        part, above, below = barrier((part, above, below))
        if not aligned:
            above, below = jnp.zeros_like(above), jnp.zeros_like(below)
        new_first, new_second, normed = rotate(
            at, part, pieces, above, below, first_moment, second_moment, lines
        )
        if aligned:
            last = jnp.where(place == 0, above, below)
            there = jnp.where((place == 0) | (place == far), far - place, lines)
            held = put(jnp.reshape(there, (1,)), last, held, lines + 1)
        flipped = held[1]

        def cross(value, distance):
            return lax.ppermute(value, "row", [(i, i ^ distance) for i in range(lines)])

        def later_hops(chunk):
            kept, arrived = products[chunk]
            step = 1
            while 2**step < lines:
                message = hop(kept, arrived, step)
                if step == 1:
                    second[chunk] = message
                arrived = arrived + [cross(message, 2**step)]
                step += 1
            products[chunk] = kept, arrived

        products, sent, outgoing, second = [], [], [], {}
        for chunk in range(CHUNKS):
            ready = after(normed, *products[0][1], outgoing[1]) if chunk >= 2 else normed
            keep, mate = restore(me_now, ready, flipped, cols, chunk, piece)
            mate = swap(mate, 1)
            sent.append([send(keep, mate, distance, []) for distance in range(2, cols, 2)])
            crossed = [swap(code, 2 * index + 2) for index, code in enumerate(sent[-1])]
            message, both = expand_send(spot, keep, mate, crossed, left, depth)
            outgoing.append(message)
            products.append((expand_keep(spot, both, left, depth), [cross(message, 1)]))
            if chunk == 1:
                later_hops(0)
            if chunk == CHUNKS - 1:
                later_hops(1)
        update = None
        for chunk in range(CHUNKS):
            if chunk >= CHUNKS - 2:
                later_hops(chunk)
            update = finish(*products[chunk], update, chunk, width)
        return (new_first, new_second, update)

    return local


def solution(mesh):
    return jax.shard_map(
        build(mesh.shape["row"], mesh.shape["col"]),
        mesh=mesh,
        in_specs=(
            P(("groups", "row"), "col"),
            P(("groups", "row"), "col"),
            P(("groups", "row"), "col"),
            P(("groups", "col"), "row"),
            P(("groups", "row"), "col"),
        ),
        out_specs=(
            P(("groups", "row"), "col"),
            P(("groups", "row"), "col"),
            P(("groups", "row"), "col"),
        ),
        check_vma=False,
    )
```

```python
import functools
import jax
import jax.numpy as jnp
from jax import lax
from jax.experimental import pallas as pl
from jax.experimental.pallas import tpu as pltpu
from jax.sharding import PartitionSpec as P

BETA_ONE = 0.9
BETA_TWO = 0.95
EPSILON = 1e-08
CHUNKS = 4
EXTRA = 16
F32 = jnp.float32
BF16 = jnp.bfloat16
MIB = 2**20


def params(mib):
    return pltpu.CompilerParams(vmem_limit_bytes=mib * MIB)


def cost(flops, moved, weight=4):
    return pl.CostEstimate(
        flops=int(flops * weight), bytes_accessed=int(moved * weight), transcendentals=0
    )


def split(value):
    high = lax.reduce_precision(value, exponent_bits=8, mantissa_bits=7)
    return high.astype(BF16), (value - high).astype(BF16)


def kernel_split(value):
    high = value.astype(BF16)
    return high, (value - high.astype(F32)).astype(BF16)


def dot(a, b, dims):
    return lax.dot_general(a, b, (dims, ((), ())), preferred_element_type=F32)


TOP = 7.5


def encode(value, inverse):
    code = jnp.abs(value) * (inverse * 2.0**TOP)
    for _ in range(4):
        code = code * code
    return jnp.where(value < 0, -code, code).astype(BF16)


def decode(code, scale):
    code = code.astype(F32)
    size = jnp.abs(code)
    root = jnp.exp2(jnp.log2(size) * 0.0625 - TOP) * scale
    root = jnp.where(size > 0, root, 0.0)
    return jnp.where(code < 0, -root, root)


def scale_of(message, depth):
    return jnp.max(message[depth : depth + EXTRA, :].astype(F32), axis=(0, 1), keepdims=True)


def fill(message, total, value_at, tile, again=None):
    depth, piece = message.shape[0] - EXTRA, message.shape[1]

    def add(i, top):
        rows = pl.ds(pl.multiple_of(i * tile, tile), tile)
        value = value_at(rows)
        if again is None:
            total[rows, :] = value
        return jnp.maximum(top, jnp.abs(value))

    top = lax.fori_loop(0, depth // tile, add, jnp.zeros((tile, piece), F32))
    top = jnp.maximum(jnp.max(top, axis=(0, 1), keepdims=True), 1e-30)
    scale = jnp.broadcast_to(top, (EXTRA, piece)).astype(BF16)
    message[depth : depth + EXTRA, :] = scale
    inverse = 1.0 / jnp.max(scale.astype(F32), axis=(0, 1), keepdims=True)

    def put(i, carry):
        rows = pl.ds(pl.multiple_of(i * tile, tile), tile)
        value = total[rows, :] if again is None else again(rows)
        message[rows, :] = encode(value, inverse)
        return carry

    lax.fori_loop(0, depth // tile, put, 0)


def halfway_kernel(place_ref, left, *refs, offsets, lines, first):
    pieces, refs = refs[: len(offsets)], refs[len(offsets) :]
    total = refs[-1]
    depth = pieces[0].shape[0]
    total[...] = jnp.zeros_like(total) if first else refs[0][...]
    place = place_ref[0]
    for offset, piece in zip(offsets, pieces):

        @pl.when((place + offset >= 0) & (place + offset < lines))
        def _(offset=offset, piece=piece):
            rows = left[pl.ds(pl.multiple_of((place + offset) * depth, depth), depth), :]
            total[...] += dot(rows, piece[...], ((0,), (0,)))

    refs[-2][...] = total[...]


def halfway(place, left, held, offsets, lines, before):
    pieces = [held[offset] for offset in offsets]
    depth, width = pieces[0].shape
    inner = left.shape[1]
    tile = min(256, inner)
    whole = pl.BlockSpec((depth, width), lambda i, s: (0, 0))
    block = pl.BlockSpec((tile, width), lambda i, s: (i, 0))
    extra = [] if before is None else [before]
    return pl.pallas_call(
        functools.partial(halfway_kernel, offsets=offsets, lines=lines, first=before is None),
        grid_spec=pltpu.PrefetchScalarGridSpec(
            num_scalar_prefetch=1,
            grid=(inner // tile,),
            in_specs=[pl.BlockSpec((left.shape[0], tile), lambda i, s: (0, i))]
            + [whole] * len(pieces)
            + [block] * len(extra),
            out_specs=block,
            scratch_shapes=[pltpu.VMEM((tile, width), F32)],
        ),
        out_shape=jax.ShapeDtypeStruct((inner, width), F32),
        compiler_params=params(48),
        cost_estimate=cost(8 * depth * inner * width, 8 * depth * inner, 0.3),
        name="halfway",
    )(place, left, *pieces, *extra)


def pack_kernel(value, pair, message, *, tile):
    depth, _ = value.shape

    def value_at(rows):
        now = value[rows, :]
        high, low = kernel_split(now)
        pair[0, rows, :] = high
        pair[1, rows, :] = low
        return now

    fill(message, None, value_at, tile, lambda rows: value[rows, :])


def pack(value):
    depth, width = value.shape
    return pl.pallas_call(
        functools.partial(pack_kernel, tile=min(16, depth)),
        out_shape=[
            jax.ShapeDtypeStruct((2, depth, width), BF16),
            jax.ShapeDtypeStruct((depth + EXTRA, width), BF16),
        ],
        compiler_params=params(60),
        cost_estimate=cost(400 * depth * width, 10 * depth * width, 0.3),
        name="pack",
    )(value)


def unpack_kernel(message, scales, pair, *, tile):
    _, depth, _ = pair.shape
    scale = scale_of(scales, 0)

    def put(i, carry):
        rows = pl.ds(pl.multiple_of(i * tile, tile), tile)
        high, low = kernel_split(decode(message[rows, :], scale))
        pair[0, rows, :] = high
        pair[1, rows, :] = low
        return carry

    lax.fori_loop(0, depth // tile, put, 0)


def unpack(message):
    depth, width = message.shape[0] - EXTRA, message.shape[1]
    step = min(256, depth)
    return pl.pallas_call(
        functools.partial(unpack_kernel, tile=min(16, step)),
        grid=(depth // step,),
        in_specs=[
            pl.BlockSpec((step, width), lambda i: (i, 0)),
            pl.BlockSpec((EXTRA, width), lambda i: (depth // EXTRA, 0)),
        ],
        out_specs=pl.BlockSpec((2, step, width), lambda i: (0, i, 0)),
        out_shape=jax.ShapeDtypeStruct((2, depth, width), BF16),
        compiler_params=params(60),
        cost_estimate=cost(400 * depth * width, 6 * depth * width, 0.3),
        name="unpack",
    )(message, message)


def put_kernel(there_ref, piece, *refs):
    right, flipped = refs[-2:]
    right[...] = piece[...]
    flipped[0] = piece[...].T


def put(there, piece, held, blocks):
    depth, width = piece.shape
    extra = [] if held is None else list(held)
    return pl.pallas_call(
        put_kernel,
        grid_spec=pltpu.PrefetchScalarGridSpec(
            num_scalar_prefetch=1,
            grid=(1,),
            in_specs=[pl.BlockSpec((depth, width), lambda i, s: (0, 0))]
            + [pl.BlockSpec(memory_space=pl.ANY)] * len(extra),
            out_specs=[
                pl.BlockSpec((depth, width), lambda i, s: (s[0], 0)),
                pl.BlockSpec((1, width, depth), lambda i, s: (s[0], 0, 0)),
            ],
        ),
        out_shape=[
            jax.ShapeDtypeStruct((blocks * depth, width), BF16),
            jax.ShapeDtypeStruct((blocks, width, depth), BF16),
        ],
        input_output_aliases={2: 0, 3: 1} if extra else {},
        compiler_params=params(60),
        cost_estimate=cost(0, 6 * depth * width, 0.3),
        name="put",
    )(there, piece, *extra)


def rotate_part_kernel(at_ref, *refs, cols, width, far):
    pieces, (right, out, total) = refs[:cols], refs[cols:]
    tile = out.shape[0]
    me, place = at_ref[0], at_ref[1]
    total[...] = jnp.zeros_like(total)
    for distance in range(cols):
        block = me ^ distance
        late = (block == far - place) & ((place == 0) | (place == far))

        @pl.when(jnp.logical_not(late))
        def _(distance=distance, block=block):
            rows = right[pl.ds(pl.multiple_of(block * width, width), width), :]
            total[...] += dot(pieces[distance][...].reshape(2 * tile, width), rows, ((1,), (0,)))

    out[...] = total[:tile, :] + total[tile:, :]


def rotate_part(at, pieces, right, far):
    cols = len(pieces)
    _, depth, width = pieces[0].shape
    tile = min(256, depth)
    return pl.pallas_call(
        functools.partial(rotate_part_kernel, cols=cols, width=width, far=far),
        grid_spec=pltpu.PrefetchScalarGridSpec(
            num_scalar_prefetch=1,
            grid=(depth // tile,),
            in_specs=[pl.BlockSpec((2, tile, width), lambda i, s: (0, i, 0))] * cols
            + [
                pl.BlockSpec(
                    (cols * width, width), lambda i, s: (0, 0), pipeline_mode=pl.Buffered(1)
                )
            ],
            out_specs=pl.BlockSpec((tile, width), lambda i, s: (i, 0)),
            scratch_shapes=[pltpu.VMEM((2 * tile, width), F32)],
        ),
        out_shape=jax.ShapeDtypeStruct((depth, width), F32),
        compiler_params=params(48),
        cost_estimate=cost(4 * depth * width * width * cols, 20 * depth * width, 0.3),
        name="rotate_part",
    )(at, *pieces, right)


def rotate_kernel(at_ref, part, above, below, first, second, *refs, cols, lines):
    pieces, (new_first, new_second, normed, held, last, arrived) = refs[:cols], refs[cols:]
    tile, width = first.shape
    depth = last.shape[0]
    me, place = at_ref[0], at_ref[1]
    step, steps = pl.program_id(0), held.shape[1] // tile
    start = (lines - 1 - place) * depth
    distance_now = me ^ (start // width)

    def copy(distance, at):
        rows = pl.ds(at * tile, tile)
        if depth == width:
            source = pieces[distance].at[:, rows, :]
        else:
            columns = pl.ds(pl.multiple_of(lax.rem(start, width), depth), depth)
            source = pieces[distance].at[:, rows, columns]
        return pltpu.make_async_copy(source, held.at[:, rows, :], arrived.at[at])

    @pl.when(step == 0)
    def _():
        for distance in range(cols):

            @pl.when(distance_now == distance)
            def _(distance=distance):
                for at in range(steps):
                    copy(distance, at).start()

        last[...] = jnp.where(place == 0, above[...], below[...])

    for at in range(steps):

        @pl.when(step == at)
        def _(at=at):
            copy(0, at).wait()

    rows = pl.ds(pl.multiple_of(step * tile, tile), tile)
    both = dot(held[:, rows, :].reshape(2 * tile, depth), last[...], ((1,), (0,)))
    rotated = part[...] + both[:tile] + both[tile:]
    one = BETA_ONE * first[...] + (1.0 - BETA_ONE) * rotated
    two = BETA_TWO * second[...] + (1.0 - BETA_TWO) * rotated * rotated
    new_first[...] = one
    new_second[...] = two
    high, low = kernel_split(one / (jnp.sqrt(two) + EPSILON))
    normed[0] = high
    normed[1] = low


def rotate(at, part, pieces, above, below, first, second, lines):
    cols = len(pieces)
    rows, width = first.shape
    depth = above.shape[0]
    tile = min(256, rows)
    block = pl.BlockSpec((tile, width), lambda i, s: (i, 0))
    pair = pl.BlockSpec((2, tile, width), lambda i, s: (0, i, 0))
    whole = pl.BlockSpec(above.shape, lambda i, s: (0, 0), pipeline_mode=pl.Buffered(1))
    return pl.pallas_call(
        functools.partial(rotate_kernel, cols=cols, lines=lines),
        grid_spec=pltpu.PrefetchScalarGridSpec(
            num_scalar_prefetch=1,
            grid=(rows // tile,),
            in_specs=[block, whole, whole, block, block]
            + [pl.BlockSpec(memory_space=pl.ANY)] * cols,
            out_specs=[block, block, pair],
            scratch_shapes=[
                pltpu.VMEM((2, rows, depth), BF16),
                pltpu.VMEM((depth, width), BF16),
                pltpu.SemaphoreType.DMA((rows // tile,)),
            ],
        ),
        out_shape=[
            jax.ShapeDtypeStruct((rows, width), F32),
            jax.ShapeDtypeStruct((rows, width), F32),
            jax.ShapeDtypeStruct((2, rows, width), BF16),
        ],
        compiler_params=params(60),
        cost_estimate=cost(4 * rows * width * depth, 30 * rows * width),
        name="rotate",
    )(at, part, above, below, first, second, *pieces)


def restore_kernel(me_ref, normed, *refs, cols):
    flipped, (keep, mate) = refs[:cols], refs[cols:]
    tile = normed.shape[1]
    both = normed[...].reshape(2 * tile, normed.shape[2])
    for distance in range(cols):
        term = dot(both, flipped[distance][0], ((1,), (0,)))
        (mate if distance % 2 else keep)[distance // 2] = term[:tile] + term[tile:]


def restore(me, normed, flipped, cols, chunk, piece):
    _, depth, inner = normed.shape
    wide = flipped.shape[2]
    tile = min(256, depth)
    out = pl.BlockSpec((cols // 2, tile, piece), lambda i, s: (0, i, 0))

    def columns(distance):
        def at(i, s):
            start = (s[0] ^ distance) * inner + chunk * piece
            return start // wide, 0, lax.rem(start, wide) // piece

        return pl.BlockSpec((1, inner, piece), at)

    return pl.pallas_call(
        functools.partial(restore_kernel, cols=cols),
        grid_spec=pltpu.PrefetchScalarGridSpec(
            num_scalar_prefetch=1,
            grid=(depth // tile,),
            in_specs=[pl.BlockSpec((2, tile, inner), lambda i, s: (0, i, 0))]
            + [columns(distance) for distance in range(cols)],
            out_specs=[out, out],
        ),
        out_shape=[jax.ShapeDtypeStruct((cols // 2, depth, piece), F32)] * 2,
        compiler_params=params(60),
        cost_estimate=cost(4 * depth * inner * piece * cols, 8 * depth * piece * cols, 4),
        name="restore",
    )(me, normed, *([flipped] * cols))


def summed(keep, mate, codes):
    depth = keep.shape[1]
    scales = [scale_of(code, depth) for code in codes]

    def value_at(rows):
        value = keep[0, rows, :] + mate[0, rows, :]
        for code, scale in zip(codes, scales):
            value = value + decode(code[rows, :], scale)
        return value

    return value_at


def send_kernel(keep, mate, *refs, tile):
    codes, (message, total) = refs[:-2], refs[-2:]
    fill(message, total, summed(keep, mate, codes), tile)


def send(keep, mate, distance, codes):
    _, depth, piece = keep.shape
    tile = min(64, depth)
    pair = pl.BlockSpec((1, depth, piece), lambda i: (distance // 2, 0, 0))
    message = pl.BlockSpec((depth + EXTRA, piece), lambda i: (0, 0))
    return pl.pallas_call(
        functools.partial(send_kernel, tile=tile),
        grid=(1,),
        in_specs=[pair, pair] + [message] * len(codes),
        out_specs=message,
        out_shape=jax.ShapeDtypeStruct((depth + EXTRA, piece), BF16),
        scratch_shapes=[pltpu.VMEM((depth, piece), F32)],
        compiler_params=params(16),
        cost_estimate=cost(400 * depth * piece, 18 * depth * piece, 4),
        name="send",
    )(keep, mate, *codes)


def expand_send_kernel(place_ref, keep, mate, *refs, tile):
    codes, (left, message, both, total) = refs[:-4], refs[-4:]
    depth, piece = total.shape

    @pl.when(pl.program_id(0) == 0)
    def _():
        value_at = summed(keep, mate, codes)

        def put(i, carry):
            rows = pl.ds(pl.multiple_of(i * tile, tile), tile)
            high, low = kernel_split(value_at(rows))
            both[rows, :piece] = high
            both[rows, piece:] = low
            return carry

        lax.fori_loop(0, both.shape[0] // tile, put, 0)

    product = dot(left[...], both[...], ((1,), (0,)))
    total[...] = product[:, :piece] + product[:, piece:]
    fill(message, None, lambda rows: total[rows, :], tile, lambda rows: total[rows, :])


def expand_send(place, keep, mate, codes, left, depth):
    inner, piece = keep.shape[1:]
    count = left.shape[0] // depth // 2
    pair = pl.BlockSpec((1, inner, piece), lambda i, s: (0, 0, 0))
    code = pl.BlockSpec((inner + EXTRA, piece), lambda i, s: (0, 0))
    return pl.pallas_call(
        functools.partial(expand_send_kernel, tile=min(64, depth)),
        grid_spec=pltpu.PrefetchScalarGridSpec(
            num_scalar_prefetch=1,
            grid=(count,),
            in_specs=[pair, pair]
            + [code] * len(codes)
            + [pl.BlockSpec((depth, inner), lambda i, s: (s[0] ^ (2 * i + 1), 0))],
            out_specs=[
                pl.BlockSpec((None, depth + EXTRA, piece), lambda i, s: (i, 0, 0)),
                pl.BlockSpec((inner, 2 * piece), lambda i, s: (0, 0)),
            ],
            scratch_shapes=[pltpu.VMEM((depth, piece), F32)],
        ),
        out_shape=[
            jax.ShapeDtypeStruct((count, depth + EXTRA, piece), BF16),
            jax.ShapeDtypeStruct((inner, 2 * piece), BF16),
        ],
        compiler_params=params(40),
        cost_estimate=cost(4 * count * depth * inner * piece, 4 * depth * inner, 4),
        name="expand_send",
    )(place, keep, mate, *codes, left)


def expand_keep_kernel(place_ref, both, left, out):
    piece = out.shape[1]
    product = dot(left[...], both[...], ((1,), (0,)))
    out[...] = product[:, :piece] + product[:, piece:]


def expand_keep(place, both, left, depth):
    inner, piece = both.shape[0], both.shape[1] // 2
    count = left.shape[0] // depth // 2
    return pl.pallas_call(
        expand_keep_kernel,
        grid_spec=pltpu.PrefetchScalarGridSpec(
            num_scalar_prefetch=1,
            grid=(count,),
            in_specs=[
                pl.BlockSpec((inner, 2 * piece), lambda i, s: (0, 0)),
                pl.BlockSpec((depth, inner), lambda i, s: (s[0] ^ (2 * i), 0)),
            ],
            out_specs=pl.BlockSpec((None, depth, piece), lambda i, s: (i, 0, 0)),
        ),
        out_shape=jax.ShapeDtypeStruct((count, depth, piece), F32),
        compiler_params=params(60),
        cost_estimate=cost(4 * count * depth * inner * piece, 4 * depth * inner, 4),
        name="expand_keep",
    )(place, both, left)


def hop_kernel(kept, *refs, tile):
    arrived, (message, total) = refs[:-2], refs[-2:]
    depth = total.shape[0]
    scales = [scale_of(code, depth) for code in arrived]

    def value_at(rows):
        value = kept[rows, :]
        for code, scale in zip(arrived, scales):
            value = value + decode(code[rows, :], scale)
        return value

    fill(message, total, value_at, tile)


def hop(kept, arrived, step):
    _, depth, piece = kept.shape
    count = arrived[-1].shape[0] // 2

    def at(shift):
        return lambda i: ((2 * i + 1) * 2**shift, 0, 0)

    return pl.pallas_call(
        functools.partial(hop_kernel, tile=min(64, depth)),
        grid=(count,),
        in_specs=[pl.BlockSpec((None, depth, piece), at(step - 1))]
        + [
            pl.BlockSpec((None, depth + EXTRA, piece), at(step - 1 - index))
            for index in range(len(arrived))
        ],
        out_specs=pl.BlockSpec((None, depth + EXTRA, piece), lambda i: (i, 0, 0)),
        out_shape=jax.ShapeDtypeStruct((count, depth + EXTRA, piece), BF16),
        scratch_shapes=[pltpu.VMEM((depth, piece), F32)],
        compiler_params=params(40),
        cost_estimate=cost(400 * count * depth * piece, 12 * count * depth * piece, 4),
        name="hop",
    )(kept, *arrived)


def finish_kernel(kept, *refs, tile, terms):
    arrived, out = refs[:terms], refs[-1]
    depth = out.shape[0]
    scales = [scale_of(code, depth) for code in arrived]

    def add(i, carry):
        rows = pl.ds(pl.multiple_of(i * tile, tile), tile)
        value = kept[rows, :]
        for code, scale in zip(arrived, scales):
            value = value + decode(code[rows, :], scale)
        out[rows, :] = value
        return carry

    lax.fori_loop(0, depth // tile, add, 0)


def finish(kept, arrived, update, chunk, width):
    _, depth, piece = kept.shape
    extra = [] if update is None else [update]
    first = lambda i: (0, 0, 0)
    return pl.pallas_call(
        functools.partial(finish_kernel, tile=min(64, depth), terms=len(arrived)),
        grid=(1,),
        in_specs=[pl.BlockSpec((None, depth, piece), first)]
        + [pl.BlockSpec((None, depth + EXTRA, piece), first)] * len(arrived)
        + [pl.BlockSpec(memory_space=pl.ANY)] * len(extra),
        out_specs=pl.BlockSpec((depth, piece), lambda i: (0, chunk)),
        out_shape=jax.ShapeDtypeStruct((depth, width), F32),
        input_output_aliases={1 + len(arrived): 0} if extra else {},
        compiler_params=params(40),
        cost_estimate=cost(400 * depth * piece, 12 * depth * piece, 0.1),
        name="finish",
    )(kept, *arrived, *extra)


def build(lines, cols):
    def swap(value, distance):
        return lax.ppermute(value, "col", [(i, i ^ distance) for i in range(cols)])

    def by_distance(block):
        held = {0: block}
        for distance in range(2, cols, 2):
            held[distance] = swap(block, distance)
        for distance in range(0, cols, 2):
            held[distance + 1] = swap(held[distance], 1)
        return held

    def place_by_distance(block, me):
        out = jnp.zeros((cols,) + block.shape, block.dtype)
        for distance, value in by_distance(block).items():
            out = lax.dynamic_update_index_in_dim(out, value, me ^ distance, 0)
        return out

    def up(value, senders):
        return lax.ppermute(value, "row", [(i, i + 1) for i in senders])

    def down(value, senders):
        return lax.ppermute(value, "row", [(i, i - 1) for i in senders])

    def after(value, *others):
        return lax.optimization_barrier((value,) + others)[0]

    def walk(held, step):
        held[-step] = up(held[1 - step], range(step - 1, lines - 1))
        held[step] = down(held[step - 1], range(1, lines - step + 1))

    def local(gradient, first_moment, second_moment, left_basis, right_basis):
        me, place = lax.axis_index("col"), lax.axis_index("row")
        depth, width = gradient.shape
        piece = width // CHUNKS
        far = lines - 1
        spot, at = jnp.reshape(place, (1,)), jnp.stack([me, place])
        me_now = jnp.reshape(me, (1,))
        barrier = lax.optimization_barrier
        near = [offset for offset in range(-far, far + 1) if abs(offset) < far]

        left = place_by_distance(left_basis, me).reshape(-1, left_basis.shape[1])
        grads = {0: gradient}
        for step in range(1, lines):
            if step == far:
                left, grads[1 - step], grads[step - 1] = barrier(
                    (left, grads[1 - step], grads[step - 1])
                )
            walk(grads, step)
        before = halfway(spot, left, grads, near, lines, None)

        own, before, grads[-far], grads[far] = barrier(
            (right_basis, before, grads[-far], grads[far])
        )
        rights = {0: own}
        for step in range(1, lines):
            walk(rights, step)
        above, below = rights[far], rights[-far]

        pair, message = pack(halfway(spot, left, grads, [-far, far], lines, before))
        message, rights[-1], rights[1] = barrier((message, rights[-1], rights[1]))
        aligned = depth == width

        def put_block(held, offset):
            there = place + offset
            there = jnp.where((there >= 0) & (there < lines), there, lines)
            return put(jnp.reshape(there, (1,)), rights[offset], held, lines + 1)

        held = None
        for offset in (0, -1, 1):
            held = put_block(held, offset)
        pieces = {1: swap(message, 1)}
        mate_pair = unpack(pieces[1])
        for distance in range(2, cols, 2):
            pieces[distance] = after(swap(message, distance), held[1], mate_pair)
            pieces[distance + 1] = swap(pieces[distance], 1)
        for step in range(2, far if aligned else lines):
            held = put_block(put_block(held, -step), step)
        pieces = [pair, mate_pair] + [unpack(pieces[distance]) for distance in range(2, cols)]
        part = rotate_part(at, pieces, held[0], far if aligned else -1)
        part, above, below = barrier((part, above, below))
        if not aligned:
            above, below = jnp.zeros_like(above), jnp.zeros_like(below)
        new_first, new_second, normed = rotate(
            at, part, pieces, above, below, first_moment, second_moment, lines
        )
        if aligned:
            last = jnp.where(place == 0, above, below)
            there = jnp.where((place == 0) | (place == far), far - place, lines)
            held = put(jnp.reshape(there, (1,)), last, held, lines + 1)
        flipped = held[1]

        def cross(value, distance):
            return lax.ppermute(value, "row", [(i, i ^ distance) for i in range(lines)])

        def later_hops(chunk):
            kept, arrived = products[chunk]
            if chunk - 1 in second:
                kept = after(kept, second[chunk - 1])
            step = 1
            while 2**step < lines:
                message = hop(kept, arrived, step)
                if step == 1:
                    second[chunk] = message
                arrived = arrived + [cross(message, 2**step)]
                step += 1
            products[chunk] = kept, arrived

        products, halves, sent, outgoing, second = [], [], [], [], {}

        def sums(chunk, ready):
            keep, mate = restore(me_now, ready, flipped, cols, chunk, piece)
            mate = swap(mate, 1)
            halves.append((keep, mate))
            sent.append([send(keep, mate, distance, []) for distance in range(2, cols, 2)])

        def multiply(chunk, *before):
            codes = [swap(code, 2 * index + 2) for index, code in enumerate(sent[chunk])]
            if codes and before:
                codes[0] = after(codes[0], *before)
            message, both = expand_send(spot, *halves[chunk], codes, left, depth)
            outgoing.append(message)
            products.append((expand_keep(spot, both, left, depth), [cross(message, 1)]))

        sums(0, normed)
        sums(1, normed)
        multiply(0, *sent[1])
        multiply(1)
        firsts = [product[1][0] for product in products]
        later_hops(0)
        later_hops(1)
        for chunk in range(2, CHUNKS):
            sums(chunk, after(normed, second.get(chunk % 2, firsts[chunk % 2]), outgoing[1]))
        for chunk in range(2, CHUNKS):
            multiply(chunk)
        update = None
        for chunk in range(CHUNKS):
            if chunk >= CHUNKS - 2:
                later_hops(chunk)
            update = finish(*products[chunk], update, chunk, width)
        return (new_first, new_second, update)

    return local


def solution(mesh):
    return jax.shard_map(
        build(mesh.shape["row"], mesh.shape["col"]),
        mesh=mesh,
        in_specs=(
            P(("groups", "row"), "col"),
            P(("groups", "row"), "col"),
            P(("groups", "row"), "col"),
            P(("groups", "col"), "row"),
            P(("groups", "row"), "col"),
        ),
        out_specs=(
            P(("groups", "row"), "col"),
            P(("groups", "row"), "col"),
            P(("groups", "row"), "col"),
        ),
        check_vma=False,
    )
```

```python
import functools
import jax
import jax.numpy as jnp
from jax import lax
from jax.experimental import pallas as pl
from jax.experimental.pallas import tpu as pltpu
from jax.sharding import PartitionSpec as P

BETA_ONE = 0.9
BETA_TWO = 0.95
EPSILON = 1e-08
CHUNKS = 4
EXTRA = 16
F32 = jnp.float32
BF16 = jnp.bfloat16
MIB = 2**20


def params(mib):
    return pltpu.CompilerParams(vmem_limit_bytes=mib * MIB)


def cost(flops, moved, weight=4):
    return pl.CostEstimate(
        flops=int(flops * weight), bytes_accessed=int(moved * weight), transcendentals=0
    )


def split(value):
    high = lax.reduce_precision(value, exponent_bits=8, mantissa_bits=7)
    return high.astype(BF16), (value - high).astype(BF16)


def kernel_split(value):
    high = value.astype(BF16)
    return high, (value - high.astype(F32)).astype(BF16)


def dot(a, b, dims):
    return lax.dot_general(a, b, (dims, ((), ())), preferred_element_type=F32)


TOP = 7.5


def encode(value, inverse):
    code = jnp.abs(value) * (inverse * 2.0**TOP)
    for _ in range(4):
        code = code * code
    return jnp.where(value < 0, -code, code).astype(BF16)


def decode(code, scale):
    code = code.astype(F32)
    size = jnp.abs(code)
    root = jnp.exp2(jnp.log2(size) * 0.0625 - TOP) * scale
    root = jnp.where(size > 0, root, 0.0)
    return jnp.where(code < 0, -root, root)


def scale_of(message, depth):
    return jnp.max(message[depth : depth + EXTRA, :].astype(F32), axis=(0, 1), keepdims=True)


def fill(message, total, value_at, tile, again=None):
    depth, piece = message.shape[0] - EXTRA, message.shape[1]

    def add(i, top):
        rows = pl.ds(pl.multiple_of(i * tile, tile), tile)
        value = value_at(rows)
        if again is None:
            total[rows, :] = value
        return jnp.maximum(top, jnp.abs(value))

    top = lax.fori_loop(0, depth // tile, add, jnp.zeros((tile, piece), F32))
    top = jnp.maximum(jnp.max(top, axis=(0, 1), keepdims=True), 1e-30)
    scale = jnp.broadcast_to(top, (EXTRA, piece)).astype(BF16)
    message[depth : depth + EXTRA, :] = scale
    inverse = 1.0 / jnp.max(scale.astype(F32), axis=(0, 1), keepdims=True)

    def put(i, carry):
        rows = pl.ds(pl.multiple_of(i * tile, tile), tile)
        value = total[rows, :] if again is None else again(rows)
        message[rows, :] = encode(value, inverse)
        return carry

    lax.fori_loop(0, depth // tile, put, 0)


def halfway_kernel(place_ref, left, *refs, offsets, lines, first):
    pieces, refs = refs[: len(offsets)], refs[len(offsets) :]
    total = refs[-1]
    depth = pieces[0].shape[0]
    total[...] = jnp.zeros_like(total) if first else refs[0][...]
    place = place_ref[0]
    for offset, piece in zip(offsets, pieces):

        @pl.when((place + offset >= 0) & (place + offset < lines))
        def _(offset=offset, piece=piece):
            rows = left[pl.ds(pl.multiple_of((place + offset) * depth, depth), depth), :]
            total[...] += dot(rows, piece[...], ((0,), (0,)))

    refs[-2][...] = total[...]


def halfway(place, left, held, offsets, lines, before):
    pieces = [held[offset] for offset in offsets]
    depth, width = pieces[0].shape
    inner = left.shape[1]
    tile = min(256, inner)
    whole = pl.BlockSpec((depth, width), lambda i, s: (0, 0))
    block = pl.BlockSpec((tile, width), lambda i, s: (i, 0))
    extra = [] if before is None else [before]
    return pl.pallas_call(
        functools.partial(halfway_kernel, offsets=offsets, lines=lines, first=before is None),
        grid_spec=pltpu.PrefetchScalarGridSpec(
            num_scalar_prefetch=1,
            grid=(inner // tile,),
            in_specs=[pl.BlockSpec((left.shape[0], tile), lambda i, s: (0, i))]
            + [whole] * len(pieces)
            + [block] * len(extra),
            out_specs=block,
            scratch_shapes=[pltpu.VMEM((tile, width), F32)],
        ),
        out_shape=jax.ShapeDtypeStruct((inner, width), F32),
        compiler_params=params(48),
        cost_estimate=cost(8 * depth * inner * width, 8 * depth * inner, 0.3),
        name="halfway",
    )(place, left, *pieces, *extra)


def pack_kernel(value, pair, message, *, tile):
    depth, _ = value.shape

    def value_at(rows):
        now = value[rows, :]
        high, low = kernel_split(now)
        pair[0, rows, :] = high
        pair[1, rows, :] = low
        return now

    fill(message, None, value_at, tile, lambda rows: value[rows, :])


def pack(value):
    depth, width = value.shape
    return pl.pallas_call(
        functools.partial(pack_kernel, tile=min(16, depth)),
        out_shape=[
            jax.ShapeDtypeStruct((2, depth, width), BF16),
            jax.ShapeDtypeStruct((depth + EXTRA, width), BF16),
        ],
        compiler_params=params(60),
        cost_estimate=cost(400 * depth * width, 10 * depth * width, 0.3),
        name="pack",
    )(value)


def unpack_kernel(message, scales, pair, *, tile):
    _, depth, _ = pair.shape
    scale = scale_of(scales, 0)

    def put(i, carry):
        rows = pl.ds(pl.multiple_of(i * tile, tile), tile)
        high, low = kernel_split(decode(message[rows, :], scale))
        pair[0, rows, :] = high
        pair[1, rows, :] = low
        return carry

    lax.fori_loop(0, depth // tile, put, 0)


def unpack(message):
    depth, width = message.shape[0] - EXTRA, message.shape[1]
    step = min(256, depth)
    return pl.pallas_call(
        functools.partial(unpack_kernel, tile=min(16, step)),
        grid=(depth // step,),
        in_specs=[
            pl.BlockSpec((step, width), lambda i: (i, 0)),
            pl.BlockSpec((EXTRA, width), lambda i: (depth // EXTRA, 0)),
        ],
        out_specs=pl.BlockSpec((2, step, width), lambda i: (0, i, 0)),
        out_shape=jax.ShapeDtypeStruct((2, depth, width), BF16),
        compiler_params=params(60),
        cost_estimate=cost(400 * depth * width, 6 * depth * width, 0.3),
        name="unpack",
    )(message, message)


def put_kernel(there_ref, piece, *refs):
    right, flipped = refs[-2:]
    right[...] = piece[...]
    flipped[0] = piece[...].T


def put(there, piece, held, blocks):
    depth, width = piece.shape
    extra = [] if held is None else list(held)
    return pl.pallas_call(
        put_kernel,
        grid_spec=pltpu.PrefetchScalarGridSpec(
            num_scalar_prefetch=1,
            grid=(1,),
            in_specs=[pl.BlockSpec((depth, width), lambda i, s: (0, 0))]
            + [pl.BlockSpec(memory_space=pl.ANY)] * len(extra),
            out_specs=[
                pl.BlockSpec((depth, width), lambda i, s: (s[0], 0)),
                pl.BlockSpec((1, width, depth), lambda i, s: (s[0], 0, 0)),
            ],
        ),
        out_shape=[
            jax.ShapeDtypeStruct((blocks * depth, width), BF16),
            jax.ShapeDtypeStruct((blocks, width, depth), BF16),
        ],
        input_output_aliases={2: 0, 3: 1} if extra else {},
        compiler_params=params(60),
        cost_estimate=cost(0, 6 * depth * width, 0.3),
        name="put",
    )(there, piece, *extra)


def rotate_part_kernel(at_ref, *refs, cols, width, far):
    pieces, (right, out, total) = refs[:cols], refs[cols:]
    tile = out.shape[0]
    me, place = at_ref[0], at_ref[1]
    total[...] = jnp.zeros_like(total)
    for distance in range(cols):
        block = me ^ distance
        late = (block == far - place) & ((place == 0) | (place == far))

        @pl.when(jnp.logical_not(late))
        def _(distance=distance, block=block):
            rows = right[pl.ds(pl.multiple_of(block * width, width), width), :]
            total[...] += dot(pieces[distance][...].reshape(2 * tile, width), rows, ((1,), (0,)))

    out[...] = total[:tile, :] + total[tile:, :]


def rotate_part(at, pieces, right, far):
    cols = len(pieces)
    _, depth, width = pieces[0].shape
    tile = min(256, depth)
    return pl.pallas_call(
        functools.partial(rotate_part_kernel, cols=cols, width=width, far=far),
        grid_spec=pltpu.PrefetchScalarGridSpec(
            num_scalar_prefetch=1,
            grid=(depth // tile,),
            in_specs=[pl.BlockSpec((2, tile, width), lambda i, s: (0, i, 0))] * cols
            + [
                pl.BlockSpec(
                    (cols * width, width), lambda i, s: (0, 0), pipeline_mode=pl.Buffered(1)
                )
            ],
            out_specs=pl.BlockSpec((tile, width), lambda i, s: (i, 0)),
            scratch_shapes=[pltpu.VMEM((2 * tile, width), F32)],
        ),
        out_shape=jax.ShapeDtypeStruct((depth, width), F32),
        compiler_params=params(48),
        cost_estimate=cost(4 * depth * width * width * cols, 20 * depth * width, 0.3),
        name="rotate_part",
    )(at, *pieces, right)


def rotate_kernel(at_ref, part, above, below, first, second, *refs, cols, lines):
    pieces, (new_first, new_second, normed, held, last, arrived) = refs[:cols], refs[cols:]
    tile, width = first.shape
    depth = last.shape[0]
    me, place = at_ref[0], at_ref[1]
    step, steps = pl.program_id(0), held.shape[1] // tile
    start = (lines - 1 - place) * depth
    distance_now = me ^ (start // width)

    def copy(distance, at):
        rows = pl.ds(at * tile, tile)
        if depth == width:
            source = pieces[distance].at[:, rows, :]
        else:
            columns = pl.ds(pl.multiple_of(lax.rem(start, width), depth), depth)
            source = pieces[distance].at[:, rows, columns]
        return pltpu.make_async_copy(source, held.at[:, rows, :], arrived.at[at])

    @pl.when(step == 0)
    def _():
        for distance in range(cols):

            @pl.when(distance_now == distance)
            def _(distance=distance):
                for at in range(steps):
                    copy(distance, at).start()

        last[...] = jnp.where(place == 0, above[...], below[...])

    for at in range(steps):

        @pl.when(step == at)
        def _(at=at):
            copy(0, at).wait()

    rows = pl.ds(pl.multiple_of(step * tile, tile), tile)
    both = dot(held[:, rows, :].reshape(2 * tile, depth), last[...], ((1,), (0,)))
    rotated = part[...] + both[:tile] + both[tile:]
    one = BETA_ONE * first[...] + (1.0 - BETA_ONE) * rotated
    two = BETA_TWO * second[...] + (1.0 - BETA_TWO) * rotated * rotated
    new_first[...] = one
    new_second[...] = two
    high, low = kernel_split(one / (jnp.sqrt(two) + EPSILON))
    normed[0] = high
    normed[1] = low


def rotate(at, part, pieces, above, below, first, second, lines):
    cols = len(pieces)
    rows, width = first.shape
    depth = above.shape[0]
    tile = min(256, rows)
    block = pl.BlockSpec((tile, width), lambda i, s: (i, 0))
    pair = pl.BlockSpec((2, tile, width), lambda i, s: (0, i, 0))
    whole = pl.BlockSpec(above.shape, lambda i, s: (0, 0), pipeline_mode=pl.Buffered(1))
    return pl.pallas_call(
        functools.partial(rotate_kernel, cols=cols, lines=lines),
        grid_spec=pltpu.PrefetchScalarGridSpec(
            num_scalar_prefetch=1,
            grid=(rows // tile,),
            in_specs=[block, whole, whole, block, block]
            + [pl.BlockSpec(memory_space=pl.ANY)] * cols,
            out_specs=[block, block, pair],
            scratch_shapes=[
                pltpu.VMEM((2, rows, depth), BF16),
                pltpu.VMEM((depth, width), BF16),
                pltpu.SemaphoreType.DMA((rows // tile,)),
            ],
        ),
        out_shape=[
            jax.ShapeDtypeStruct((rows, width), F32),
            jax.ShapeDtypeStruct((rows, width), F32),
            jax.ShapeDtypeStruct((2, rows, width), BF16),
        ],
        compiler_params=params(40),
        cost_estimate=cost(4 * rows * width * depth, 30 * rows * width),
        name="rotate",
    )(at, part, above, below, first, second, *pieces)


def restore_kernel(me_ref, normed, *refs, cols, spans):
    flipped, outs = refs[: cols * spans], refs[cols * spans :]
    tile = normed.shape[1]
    wide = flipped[0].shape[2]
    piece = outs[0].shape[2]
    both = normed[...].reshape(2 * tile, normed.shape[2])
    for distance in range(cols):
        for span in range(spans):
            term = dot(both, flipped[distance * spans + span][0], ((1,), (0,)))
            term = term[:tile] + term[tile:]
            for at in range(wide // piece):
                chunk = span * (wide // piece) + at
                out = outs[2 * chunk + distance % 2]
                out[distance // 2] = term[:, at * piece : (at + 1) * piece]


def restore(me, normed, flipped, cols, piece):
    _, depth, inner = normed.shape
    wide = flipped.shape[2]
    spans = inner // wide
    tile = min(256, depth)
    out = pl.BlockSpec((cols // 2, tile, piece), lambda i, s: (0, i, 0))

    def columns(distance, span):
        return pl.BlockSpec(
            (1, inner, wide),
            lambda i, s: ((s[0] ^ distance) * spans + span, 0, 0),
            pipeline_mode=pl.Buffered(1),
        )

    outs = pl.pallas_call(
        functools.partial(restore_kernel, cols=cols, spans=spans),
        grid_spec=pltpu.PrefetchScalarGridSpec(
            num_scalar_prefetch=1,
            grid=(depth // tile,),
            in_specs=[pl.BlockSpec((2, tile, inner), lambda i, s: (0, i, 0))]
            + [columns(distance, span) for distance in range(cols) for span in range(spans)],
            out_specs=[out] * (2 * CHUNKS),
        ),
        out_shape=[jax.ShapeDtypeStruct((cols // 2, depth, piece), F32)] * (2 * CHUNKS),
        compiler_params=params(44),
        cost_estimate=cost(4 * depth * inner * inner * cols, 8 * depth * inner * cols),
        name="restore",
    )(me, normed, *([flipped] * (cols * spans)))
    return [(outs[2 * chunk], outs[2 * chunk + 1]) for chunk in range(CHUNKS)]


def summed(keep, mate, codes):
    depth = keep.shape[1]
    scales = [scale_of(code, depth) for code in codes]

    def value_at(rows):
        value = keep[0, rows, :] + mate[0, rows, :]
        for code, scale in zip(codes, scales):
            value = value + decode(code[rows, :], scale)
        return value

    return value_at


def send_kernel(keep, mate, *refs, tile):
    codes, (message, total) = refs[:-2], refs[-2:]
    fill(message, total, summed(keep, mate, codes), tile)


def send(keep, mate, distance, codes):
    _, depth, piece = keep.shape
    tile = min(64, depth)
    pair = pl.BlockSpec((1, depth, piece), lambda i: (distance // 2, 0, 0))
    message = pl.BlockSpec((depth + EXTRA, piece), lambda i: (0, 0))
    return pl.pallas_call(
        functools.partial(send_kernel, tile=tile),
        grid=(1,),
        in_specs=[pair, pair] + [message] * len(codes),
        out_specs=message,
        out_shape=jax.ShapeDtypeStruct((depth + EXTRA, piece), BF16),
        scratch_shapes=[pltpu.VMEM((depth, piece), F32)],
        compiler_params=params(16),
        cost_estimate=cost(400 * depth * piece, 18 * depth * piece, 4),
        name="send",
    )(keep, mate, *codes)


def expand_send_kernel(place_ref, keep, mate, *refs, tile):
    codes, (left, message, both, total) = refs[:-4], refs[-4:]
    depth, piece = total.shape

    @pl.when(pl.program_id(0) == 0)
    def _():
        value_at = summed(keep, mate, codes)

        def put(i, carry):
            rows = pl.ds(pl.multiple_of(i * tile, tile), tile)
            high, low = kernel_split(value_at(rows))
            both[rows, :piece] = high
            both[rows, piece:] = low
            return carry

        lax.fori_loop(0, both.shape[0] // tile, put, 0)

    product = dot(left[...], both[...], ((1,), (0,)))
    total[...] = product[:, :piece] + product[:, piece:]
    fill(message, None, lambda rows: total[rows, :], tile, lambda rows: total[rows, :])


def expand_send(place, keep, mate, codes, left, depth):
    inner, piece = keep.shape[1:]
    count = left.shape[0] // depth // 2
    pair = pl.BlockSpec((1, inner, piece), lambda i, s: (0, 0, 0))
    code = pl.BlockSpec((inner + EXTRA, piece), lambda i, s: (0, 0))
    return pl.pallas_call(
        functools.partial(expand_send_kernel, tile=min(64, depth)),
        grid_spec=pltpu.PrefetchScalarGridSpec(
            num_scalar_prefetch=1,
            grid=(count,),
            in_specs=[pair, pair]
            + [code] * len(codes)
            + [pl.BlockSpec((depth, inner), lambda i, s: (s[0] ^ (2 * i + 1), 0))],
            out_specs=[
                pl.BlockSpec((None, depth + EXTRA, piece), lambda i, s: (i, 0, 0)),
                pl.BlockSpec((inner, 2 * piece), lambda i, s: (0, 0)),
            ],
            scratch_shapes=[pltpu.VMEM((depth, piece), F32)],
        ),
        out_shape=[
            jax.ShapeDtypeStruct((count, depth + EXTRA, piece), BF16),
            jax.ShapeDtypeStruct((inner, 2 * piece), BF16),
        ],
        compiler_params=params(40),
        cost_estimate=cost(4 * count * depth * inner * piece, 4 * depth * inner, 4),
        name="expand_send",
    )(place, keep, mate, *codes, left)


def expand_keep_kernel(place_ref, both, left, out):
    piece = out.shape[1]
    product = dot(left[...], both[...], ((1,), (0,)))
    out[...] = product[:, :piece] + product[:, piece:]


def expand_keep(place, both, left, depth):
    inner, piece = both.shape[0], both.shape[1] // 2
    count = left.shape[0] // depth // 2
    return pl.pallas_call(
        expand_keep_kernel,
        grid_spec=pltpu.PrefetchScalarGridSpec(
            num_scalar_prefetch=1,
            grid=(count,),
            in_specs=[
                pl.BlockSpec((inner, 2 * piece), lambda i, s: (0, 0)),
                pl.BlockSpec((depth, inner), lambda i, s: (s[0] ^ (2 * i), 0)),
            ],
            out_specs=pl.BlockSpec((None, depth, piece), lambda i, s: (i, 0, 0)),
        ),
        out_shape=jax.ShapeDtypeStruct((count, depth, piece), F32),
        compiler_params=params(60),
        cost_estimate=cost(4 * count * depth * inner * piece, 4 * depth * inner, 4),
        name="expand_keep",
    )(place, both, left)


def hop_kernel(kept, *refs, tile):
    arrived, (message, total) = refs[:-2], refs[-2:]
    depth = total.shape[0]
    scales = [scale_of(code, depth) for code in arrived]

    def value_at(rows):
        value = kept[rows, :]
        for code, scale in zip(arrived, scales):
            value = value + decode(code[rows, :], scale)
        return value

    fill(message, total, value_at, tile)


def hop(kept, arrived, step):
    _, depth, piece = kept.shape
    count = arrived[-1].shape[0] // 2

    def at(shift):
        return lambda i: ((2 * i + 1) * 2**shift, 0, 0)

    return pl.pallas_call(
        functools.partial(hop_kernel, tile=min(64, depth)),
        grid=(count,),
        in_specs=[pl.BlockSpec((None, depth, piece), at(step - 1))]
        + [
            pl.BlockSpec((None, depth + EXTRA, piece), at(step - 1 - index))
            for index in range(len(arrived))
        ],
        out_specs=pl.BlockSpec((None, depth + EXTRA, piece), lambda i: (i, 0, 0)),
        out_shape=jax.ShapeDtypeStruct((count, depth + EXTRA, piece), BF16),
        scratch_shapes=[pltpu.VMEM((depth, piece), F32)],
        compiler_params=params(40),
        cost_estimate=cost(400 * count * depth * piece, 12 * count * depth * piece, 4),
        name="hop",
    )(kept, *arrived)


def finish_kernel(kept, *refs, tile, terms):
    arrived, out = refs[:terms], refs[-1]
    depth = out.shape[0]
    scales = [scale_of(code, depth) for code in arrived]

    def add(i, carry):
        rows = pl.ds(pl.multiple_of(i * tile, tile), tile)
        value = kept[rows, :]
        for code, scale in zip(arrived, scales):
            value = value + decode(code[rows, :], scale)
        out[rows, :] = value
        return carry

    lax.fori_loop(0, depth // tile, add, 0)


def finish(kept, arrived, update, chunk, width):
    _, depth, piece = kept.shape
    extra = [] if update is None else [update]
    first = lambda i: (0, 0, 0)
    return pl.pallas_call(
        functools.partial(finish_kernel, tile=min(64, depth), terms=len(arrived)),
        grid=(1,),
        in_specs=[pl.BlockSpec((None, depth, piece), first)]
        + [pl.BlockSpec((None, depth + EXTRA, piece), first)] * len(arrived)
        + [pl.BlockSpec(memory_space=pl.ANY)] * len(extra),
        out_specs=pl.BlockSpec((depth, piece), lambda i: (0, chunk)),
        out_shape=jax.ShapeDtypeStruct((depth, width), F32),
        input_output_aliases={1 + len(arrived): 0} if extra else {},
        compiler_params=params(40),
        cost_estimate=cost(400 * depth * piece, 12 * depth * piece, 0.1),
        name="finish",
    )(kept, *arrived, *extra)


def build(lines, cols):
    def swap(value, distance):
        return lax.ppermute(value, "col", [(i, i ^ distance) for i in range(cols)])

    def by_distance(block):
        held = {0: block}
        for distance in range(2, cols, 2):
            held[distance] = swap(block, distance)
        for distance in range(0, cols, 2):
            held[distance + 1] = swap(held[distance], 1)
        return held

    def place_by_distance(block, me):
        out = jnp.zeros((cols,) + block.shape, block.dtype)
        for distance, value in by_distance(block).items():
            out = lax.dynamic_update_index_in_dim(out, value, me ^ distance, 0)
        return out

    def up(value, senders):
        return lax.ppermute(value, "row", [(i, i + 1) for i in senders])

    def down(value, senders):
        return lax.ppermute(value, "row", [(i, i - 1) for i in senders])

    def after(value, *others):
        return lax.optimization_barrier((value,) + others)[0]

    def walk(held, step):
        held[-step] = up(held[1 - step], range(step - 1, lines - 1))
        held[step] = down(held[step - 1], range(1, lines - step + 1))

    def local(gradient, first_moment, second_moment, left_basis, right_basis):
        me, place = lax.axis_index("col"), lax.axis_index("row")
        depth, width = gradient.shape
        piece = width // CHUNKS
        far = lines - 1
        spot, at = jnp.reshape(place, (1,)), jnp.stack([me, place])
        me_now = jnp.reshape(me, (1,))
        barrier = lax.optimization_barrier
        near = [offset for offset in range(-far, far + 1) if abs(offset) < far]

        left = place_by_distance(left_basis, me).reshape(-1, left_basis.shape[1])
        grads = {0: gradient}
        for step in range(1, lines):
            if step == far:
                left, grads[1 - step], grads[step - 1] = barrier(
                    (left, grads[1 - step], grads[step - 1])
                )
            walk(grads, step)
        before = halfway(spot, left, grads, near, lines, None)

        own, before, grads[-far], grads[far] = barrier(
            (right_basis, before, grads[-far], grads[far])
        )
        rights = {0: own}
        for step in range(1, lines):
            walk(rights, step)
        above, below = rights[far], rights[-far]

        pair, message = pack(halfway(spot, left, grads, [-far, far], lines, before))
        message, rights[-1], rights[1] = barrier((message, rights[-1], rights[1]))
        aligned = depth == width

        def put_block(held, offset):
            there = place + offset
            there = jnp.where((there >= 0) & (there < lines), there, lines)
            return put(jnp.reshape(there, (1,)), rights[offset], held, lines + 1)

        held = None
        for offset in (0, -1, 1):
            held = put_block(held, offset)
        pieces = {1: swap(message, 1)}
        mate_pair = unpack(pieces[1])
        for distance in range(2, cols, 2):
            pieces[distance] = after(swap(message, distance), held[1], mate_pair)
            pieces[distance + 1] = swap(pieces[distance], 1)
        for step in range(2, far if aligned else lines):
            held = put_block(put_block(held, -step), step)
        pieces = [pair, mate_pair] + [unpack(pieces[distance]) for distance in range(2, cols)]
        part = rotate_part(at, pieces, held[0], far if aligned else -1)
        part, above, below = barrier((part, above, below))
        if not aligned:
            above, below = jnp.zeros_like(above), jnp.zeros_like(below)
        new_first, new_second, normed = rotate(
            at, part, pieces, above, below, first_moment, second_moment, lines
        )
        if aligned:
            last = jnp.where(place == 0, after(above, normed), below)
            there = jnp.where((place == 0) | (place == far), far - place, lines)
            held = put(jnp.reshape(there, (1,)), last, held, lines + 1)
        flipped = held[1]

        def cross(value, distance):
            return lax.ppermute(value, "row", [(i, i ^ distance) for i in range(lines)])

        def later_hops(chunk):
            kept, arrived = products[chunk]
            if chunk - 1 in second:
                kept = after(kept, second[chunk - 1])
            step = 1
            while 2**step < lines:
                message = hop(kept, arrived, step)
                if step == 1:
                    second[chunk] = message
                arrived = arrived + [cross(message, 2**step)]
                step += 1
            products[chunk] = kept, arrived

        products, halves, sent, outgoing, second = [], [], [], [], {}

        def multiply(chunk, *before):
            codes = [swap(code, 2 * index + 2) for index, code in enumerate(sent[chunk])]
            if codes and before:
                codes[0] = after(codes[0], *before)
            message, both = expand_send(spot, *halves[chunk], codes, left, depth)
            outgoing.append(message)
            products.append((expand_keep(spot, both, left, depth), [cross(message, 1)]))

        for keep, mate in restore(me_now, normed, flipped, cols, piece):
            mate = swap(mate, 1)
            halves.append((keep, mate))
            sent.append([send(keep, mate, distance, []) for distance in range(2, cols, 2)])
        for chunk in range(CHUNKS):
            multiply(chunk, *(outgoing[-1:]))
        update = None
        for chunk in range(CHUNKS):
            later_hops(chunk)
            update = finish(*products[chunk], update, chunk, width)
        return (new_first, new_second, update)

    return local


def solution(mesh):
    return jax.shard_map(
        build(mesh.shape["row"], mesh.shape["col"]),
        mesh=mesh,
        in_specs=(
            P(("groups", "row"), "col"),
            P(("groups", "row"), "col"),
            P(("groups", "row"), "col"),
            P(("groups", "col"), "row"),
            P(("groups", "row"), "col"),
        ),
        out_specs=(
            P(("groups", "row"), "col"),
            P(("groups", "row"), "col"),
            P(("groups", "row"), "col"),
        ),
        check_vma=False,
    )
```

```python
import functools
import jax
import jax.numpy as jnp
from jax import lax
from jax.experimental import pallas as pl
from jax.experimental.pallas import tpu as pltpu
from jax.sharding import PartitionSpec as P

BETA_ONE = 0.9
BETA_TWO = 0.95
EPSILON = 1e-08
CHUNKS = 4
EXTRA = 16
F32 = jnp.float32
BF16 = jnp.bfloat16
MIB = 2**20


def params(mib):
    return pltpu.CompilerParams(vmem_limit_bytes=mib * MIB)


def cost(flops, moved, weight=4):
    return pl.CostEstimate(
        flops=int(flops * weight), bytes_accessed=int(moved * weight), transcendentals=0
    )


def split(value):
    high = lax.reduce_precision(value, exponent_bits=8, mantissa_bits=7)
    return high.astype(BF16), (value - high).astype(BF16)


def kernel_split(value):
    high = value.astype(BF16)
    return high, (value - high.astype(F32)).astype(BF16)


def dot(a, b, dims):
    return lax.dot_general(a, b, (dims, ((), ())), preferred_element_type=F32)


TOP = 7.5


def encode(value, inverse):
    code = jnp.abs(value) * (inverse * 2.0**TOP)
    for _ in range(4):
        code = code * code
    return jnp.where(value < 0, -code, code).astype(BF16)


def decode(code, scale):
    code = code.astype(F32)
    size = jnp.abs(code)
    root = jnp.exp2(jnp.log2(size) * 0.0625 - TOP) * scale
    root = jnp.where(size > 0, root, 0.0)
    return jnp.where(code < 0, -root, root)


def scale_of(message, depth):
    return jnp.max(message[depth : depth + EXTRA, :].astype(F32), axis=(0, 1), keepdims=True)


def fill(message, total, value_at, tile, again=None):
    depth, piece = message.shape[0] - EXTRA, message.shape[1]

    def add(i, top):
        rows = pl.ds(pl.multiple_of(i * tile, tile), tile)
        value = value_at(rows)
        if again is None:
            total[rows, :] = value
        return jnp.maximum(top, jnp.abs(value))

    top = lax.fori_loop(0, depth // tile, add, jnp.zeros((tile, piece), F32))
    top = jnp.maximum(jnp.max(top, axis=(0, 1), keepdims=True), 1e-30)
    scale = jnp.broadcast_to(top, (EXTRA, piece)).astype(BF16)
    message[depth : depth + EXTRA, :] = scale
    inverse = 1.0 / jnp.max(scale.astype(F32), axis=(0, 1), keepdims=True)

    def put(i, carry):
        rows = pl.ds(pl.multiple_of(i * tile, tile), tile)
        value = total[rows, :] if again is None else again(rows)
        message[rows, :] = encode(value, inverse)
        return carry

    lax.fori_loop(0, depth // tile, put, 0)


def halfway_kernel(place_ref, left, *refs, offsets, lines, first):
    pieces, refs = refs[: len(offsets)], refs[len(offsets) :]
    total = refs[-1]
    depth = pieces[0].shape[0]
    total[...] = jnp.zeros_like(total) if first else refs[0][...]
    place = place_ref[0]
    for offset, piece in zip(offsets, pieces):

        @pl.when((place + offset >= 0) & (place + offset < lines))
        def _(offset=offset, piece=piece):
            rows = left[pl.ds(pl.multiple_of((place + offset) * depth, depth), depth), :]
            total[...] += dot(rows, piece[...], ((0,), (0,)))

    refs[-2][...] = total[...]


def halfway(place, left, held, offsets, lines, before):
    pieces = [held[offset] for offset in offsets]
    depth, width = pieces[0].shape
    inner = left.shape[1]
    tile = min(256, inner)
    whole = pl.BlockSpec((depth, width), lambda i, s: (0, 0))
    block = pl.BlockSpec((tile, width), lambda i, s: (i, 0))
    extra = [] if before is None else [before]
    return pl.pallas_call(
        functools.partial(halfway_kernel, offsets=offsets, lines=lines, first=before is None),
        grid_spec=pltpu.PrefetchScalarGridSpec(
            num_scalar_prefetch=1,
            grid=(inner // tile,),
            in_specs=[pl.BlockSpec((left.shape[0], tile), lambda i, s: (0, i))]
            + [whole] * len(pieces)
            + [block] * len(extra),
            out_specs=block,
            scratch_shapes=[pltpu.VMEM((tile, width), F32)],
        ),
        out_shape=jax.ShapeDtypeStruct((inner, width), F32),
        compiler_params=params(48),
        cost_estimate=cost(8 * depth * inner * width, 8 * depth * inner, 0.3),
        name="halfway",
    )(place, left, *pieces, *extra)


def pack_kernel(value, pair, message, *, tile):
    depth, _ = value.shape

    def value_at(rows):
        now = value[rows, :]
        high, low = kernel_split(now)
        pair[0, rows, :] = high
        pair[1, rows, :] = low
        return now

    fill(message, None, value_at, tile, lambda rows: value[rows, :])


def pack(value):
    depth, width = value.shape
    return pl.pallas_call(
        functools.partial(pack_kernel, tile=min(16, depth)),
        out_shape=[
            jax.ShapeDtypeStruct((2, depth, width), BF16),
            jax.ShapeDtypeStruct((depth + EXTRA, width), BF16),
        ],
        compiler_params=params(60),
        cost_estimate=cost(400 * depth * width, 10 * depth * width, 0.3),
        name="pack",
    )(value)


def unpack_kernel(message, scales, pair, *, tile):
    _, depth, _ = pair.shape
    scale = scale_of(scales, 0)

    def put(i, carry):
        rows = pl.ds(pl.multiple_of(i * tile, tile), tile)
        high, low = kernel_split(decode(message[rows, :], scale))
        pair[0, rows, :] = high
        pair[1, rows, :] = low
        return carry

    lax.fori_loop(0, depth // tile, put, 0)


def unpack(message):
    depth, width = message.shape[0] - EXTRA, message.shape[1]
    step = min(256, depth)
    return pl.pallas_call(
        functools.partial(unpack_kernel, tile=min(16, step)),
        grid=(depth // step,),
        in_specs=[
            pl.BlockSpec((step, width), lambda i: (i, 0)),
            pl.BlockSpec((EXTRA, width), lambda i: (depth // EXTRA, 0)),
        ],
        out_specs=pl.BlockSpec((2, step, width), lambda i: (0, i, 0)),
        out_shape=jax.ShapeDtypeStruct((2, depth, width), BF16),
        compiler_params=params(60),
        cost_estimate=cost(400 * depth * width, 6 * depth * width, 0.3),
        name="unpack",
    )(message, message)


def put_kernel(there_ref, piece, *refs):
    right, flipped = refs[-2:]
    right[...] = piece[...]
    flipped[0] = piece[...].T


def put(there, piece, held, blocks):
    depth, width = piece.shape
    extra = [] if held is None else list(held)
    return pl.pallas_call(
        put_kernel,
        grid_spec=pltpu.PrefetchScalarGridSpec(
            num_scalar_prefetch=1,
            grid=(1,),
            in_specs=[pl.BlockSpec((depth, width), lambda i, s: (0, 0))]
            + [pl.BlockSpec(memory_space=pl.ANY)] * len(extra),
            out_specs=[
                pl.BlockSpec((depth, width), lambda i, s: (s[0], 0)),
                pl.BlockSpec((1, width, depth), lambda i, s: (s[0], 0, 0)),
            ],
        ),
        out_shape=[
            jax.ShapeDtypeStruct((blocks * depth, width), BF16),
            jax.ShapeDtypeStruct((blocks, width, depth), BF16),
        ],
        input_output_aliases={2: 0, 3: 1} if extra else {},
        compiler_params=params(60),
        cost_estimate=cost(0, 6 * depth * width, 0.3),
        name="put",
    )(there, piece, *extra)


def rotate_part_kernel(at_ref, *refs, cols, width, far):
    pieces, (right, out, total) = refs[:cols], refs[cols:]
    tile = out.shape[0]
    me, place = at_ref[0], at_ref[1]
    total[...] = jnp.zeros_like(total)
    for distance in range(cols):
        block = me ^ distance
        late = (block == far - place) & ((place == 0) | (place == far))

        @pl.when(jnp.logical_not(late))
        def _(distance=distance, block=block):
            rows = right[pl.ds(pl.multiple_of(block * width, width), width), :]
            total[...] += dot(pieces[distance][...].reshape(2 * tile, width), rows, ((1,), (0,)))

    out[...] = total[:tile, :] + total[tile:, :]


def rotate_part(at, pieces, right, far):
    cols = len(pieces)
    _, depth, width = pieces[0].shape
    tile = min(256, depth)
    return pl.pallas_call(
        functools.partial(rotate_part_kernel, cols=cols, width=width, far=far),
        grid_spec=pltpu.PrefetchScalarGridSpec(
            num_scalar_prefetch=1,
            grid=(depth // tile,),
            in_specs=[pl.BlockSpec((2, tile, width), lambda i, s: (0, i, 0))] * cols
            + [
                pl.BlockSpec(
                    (cols * width, width), lambda i, s: (0, 0), pipeline_mode=pl.Buffered(1)
                )
            ],
            out_specs=pl.BlockSpec((tile, width), lambda i, s: (i, 0)),
            scratch_shapes=[pltpu.VMEM((2 * tile, width), F32)],
        ),
        out_shape=jax.ShapeDtypeStruct((depth, width), F32),
        compiler_params=params(48),
        cost_estimate=cost(4 * depth * width * width * cols, 20 * depth * width, 0.3),
        name="rotate_part",
    )(at, *pieces, right)


def rotate_kernel(at_ref, part, above, below, first, second, *refs, cols, lines):
    pieces, (new_first, new_second, normed, held, last, arrived) = refs[:cols], refs[cols:]
    tile, width = first.shape
    depth = last.shape[0]
    me, place = at_ref[0], at_ref[1]
    step, steps = pl.program_id(0), held.shape[1] // tile
    start = (lines - 1 - place) * depth
    distance_now = me ^ (start // width)

    def copy(distance, at):
        rows = pl.ds(at * tile, tile)
        if depth == width:
            source = pieces[distance].at[:, rows, :]
        else:
            columns = pl.ds(pl.multiple_of(lax.rem(start, width), depth), depth)
            source = pieces[distance].at[:, rows, columns]
        return pltpu.make_async_copy(source, held.at[:, rows, :], arrived.at[at])

    @pl.when(step == 0)
    def _():
        for distance in range(cols):

            @pl.when(distance_now == distance)
            def _(distance=distance):
                for at in range(steps):
                    copy(distance, at).start()

        last[...] = jnp.where(place == 0, above[...], below[...])

    for at in range(steps):

        @pl.when(step == at)
        def _(at=at):
            copy(0, at).wait()

    rows = pl.ds(pl.multiple_of(step * tile, tile), tile)
    both = dot(held[:, rows, :].reshape(2 * tile, depth), last[...], ((1,), (0,)))
    rotated = part[...] + both[:tile] + both[tile:]
    one = BETA_ONE * first[...] + (1.0 - BETA_ONE) * rotated
    two = BETA_TWO * second[...] + (1.0 - BETA_TWO) * rotated * rotated
    new_first[...] = one
    new_second[...] = two
    high, low = kernel_split(one / (jnp.sqrt(two) + EPSILON))
    normed[0] = high
    normed[1] = low


def rotate(at, part, pieces, above, below, first, second, lines):
    cols = len(pieces)
    rows, width = first.shape
    depth = above.shape[0]
    tile = min(256, rows)
    block = pl.BlockSpec((tile, width), lambda i, s: (i, 0))
    pair = pl.BlockSpec((2, tile, width), lambda i, s: (0, i, 0))
    whole = pl.BlockSpec(above.shape, lambda i, s: (0, 0), pipeline_mode=pl.Buffered(1))
    return pl.pallas_call(
        functools.partial(rotate_kernel, cols=cols, lines=lines),
        grid_spec=pltpu.PrefetchScalarGridSpec(
            num_scalar_prefetch=1,
            grid=(rows // tile,),
            in_specs=[block, whole, whole, block, block]
            + [pl.BlockSpec(memory_space=pl.ANY)] * cols,
            out_specs=[block, block, pair],
            scratch_shapes=[
                pltpu.VMEM((2, rows, depth), BF16),
                pltpu.VMEM((depth, width), BF16),
                pltpu.SemaphoreType.DMA((rows // tile,)),
            ],
        ),
        out_shape=[
            jax.ShapeDtypeStruct((rows, width), F32),
            jax.ShapeDtypeStruct((rows, width), F32),
            jax.ShapeDtypeStruct((2, rows, width), BF16),
        ],
        compiler_params=params(40),
        cost_estimate=cost(4 * rows * width * depth, 30 * rows * width),
        name="rotate",
    )(at, part, above, below, first, second, *pieces)


def restore_kernel(me_ref, normed, *refs, cols):
    flipped, outs = refs[:cols], refs[cols:]
    tile = normed.shape[1]
    piece = outs[0].shape[2]
    both = normed[...].reshape(2 * tile, normed.shape[2])
    for distance in range(cols):
        term = dot(both, flipped[distance][0], ((1,), (0,)))
        term = term[:tile] + term[tile:]
        for at in range(len(outs) // 2):
            out = outs[2 * at + distance % 2]
            out[distance // 2] = term[:, at * piece : (at + 1) * piece]


def restore(me, normed, flipped, cols, piece, batch, count):
    _, depth, inner = normed.shape
    wide = flipped.shape[2]
    tile = min(256, depth)
    out = pl.BlockSpec((cols // 2, tile, piece), lambda i, s: (0, i, 0))

    def columns(distance):
        def at(i, s):
            start = (s[0] ^ distance) * inner + batch * count * piece
            return start // wide, 0, lax.rem(start, wide) // (count * piece)

        return pl.BlockSpec((1, inner, count * piece), at, pipeline_mode=pl.Buffered(1))

    outs = pl.pallas_call(
        functools.partial(restore_kernel, cols=cols),
        grid_spec=pltpu.PrefetchScalarGridSpec(
            num_scalar_prefetch=1,
            grid=(depth // tile,),
            in_specs=[pl.BlockSpec((2, tile, inner), lambda i, s: (0, i, 0))]
            + [columns(distance) for distance in range(cols)],
            out_specs=[out] * (2 * count),
        ),
        out_shape=[jax.ShapeDtypeStruct((cols // 2, depth, piece), F32)] * (2 * count),
        compiler_params=params(44),
        cost_estimate=cost(
            4 * depth * inner * count * piece * cols, 8 * depth * count * piece * cols
        ),
        name="restore",
    )(me, normed, *([flipped] * cols))
    return [(outs[2 * at], outs[2 * at + 1]) for at in range(count)]


def summed(keep, mate, codes):
    depth = keep.shape[1]
    scales = [scale_of(code, depth) for code in codes]

    def value_at(rows):
        value = keep[0, rows, :] + mate[0, rows, :]
        for code, scale in zip(codes, scales):
            value = value + decode(code[rows, :], scale)
        return value

    return value_at


def send_kernel(keep, mate, *refs, tile):
    codes, (message, total) = refs[:-2], refs[-2:]
    fill(message, total, summed(keep, mate, codes), tile)


def send(keep, mate, distance, codes):
    _, depth, piece = keep.shape
    tile = min(64, depth)
    pair = pl.BlockSpec((1, depth, piece), lambda i: (distance // 2, 0, 0))
    message = pl.BlockSpec((depth + EXTRA, piece), lambda i: (0, 0))
    return pl.pallas_call(
        functools.partial(send_kernel, tile=tile),
        grid=(1,),
        in_specs=[pair, pair] + [message] * len(codes),
        out_specs=message,
        out_shape=jax.ShapeDtypeStruct((depth + EXTRA, piece), BF16),
        scratch_shapes=[pltpu.VMEM((depth, piece), F32)],
        compiler_params=params(16),
        cost_estimate=cost(400 * depth * piece, 18 * depth * piece, 4),
        name="send",
    )(keep, mate, *codes)


def expand_send_kernel(place_ref, keep, mate, *refs, tile):
    codes, (left, message, both, total) = refs[:-4], refs[-4:]
    depth, piece = total.shape

    @pl.when(pl.program_id(0) == 0)
    def _():
        value_at = summed(keep, mate, codes)

        def put(i, carry):
            rows = pl.ds(pl.multiple_of(i * tile, tile), tile)
            high, low = kernel_split(value_at(rows))
            both[rows, :piece] = high
            both[rows, piece:] = low
            return carry

        lax.fori_loop(0, both.shape[0] // tile, put, 0)

    product = dot(left[...], both[...], ((1,), (0,)))
    total[...] = product[:, :piece] + product[:, piece:]
    fill(message, None, lambda rows: total[rows, :], tile, lambda rows: total[rows, :])


def expand_send(place, keep, mate, codes, left, depth):
    inner, piece = keep.shape[1:]
    count = left.shape[0] // depth // 2
    pair = pl.BlockSpec((1, inner, piece), lambda i, s: (0, 0, 0))
    code = pl.BlockSpec((inner + EXTRA, piece), lambda i, s: (0, 0))
    return pl.pallas_call(
        functools.partial(expand_send_kernel, tile=min(64, depth)),
        grid_spec=pltpu.PrefetchScalarGridSpec(
            num_scalar_prefetch=1,
            grid=(count,),
            in_specs=[pair, pair]
            + [code] * len(codes)
            + [pl.BlockSpec((depth, inner), lambda i, s: (s[0] ^ (2 * i + 1), 0))],
            out_specs=[
                pl.BlockSpec((None, depth + EXTRA, piece), lambda i, s: (i, 0, 0)),
                pl.BlockSpec((inner, 2 * piece), lambda i, s: (0, 0)),
            ],
            scratch_shapes=[pltpu.VMEM((depth, piece), F32)],
        ),
        out_shape=[
            jax.ShapeDtypeStruct((count, depth + EXTRA, piece), BF16),
            jax.ShapeDtypeStruct((inner, 2 * piece), BF16),
        ],
        compiler_params=params(40),
        cost_estimate=cost(4 * count * depth * inner * piece, 4 * depth * inner, 4),
        name="expand_send",
    )(place, keep, mate, *codes, left)


def expand_keep_kernel(place_ref, both, left, out):
    piece = out.shape[1]
    product = dot(left[...], both[...], ((1,), (0,)))
    out[...] = product[:, :piece] + product[:, piece:]


def expand_keep(place, both, left, depth):
    inner, piece = both.shape[0], both.shape[1] // 2
    count = left.shape[0] // depth // 2
    return pl.pallas_call(
        expand_keep_kernel,
        grid_spec=pltpu.PrefetchScalarGridSpec(
            num_scalar_prefetch=1,
            grid=(count,),
            in_specs=[
                pl.BlockSpec((inner, 2 * piece), lambda i, s: (0, 0)),
                pl.BlockSpec((depth, inner), lambda i, s: (s[0] ^ (2 * i), 0)),
            ],
            out_specs=pl.BlockSpec((None, depth, piece), lambda i, s: (i, 0, 0)),
        ),
        out_shape=jax.ShapeDtypeStruct((count, depth, piece), F32),
        compiler_params=params(60),
        cost_estimate=cost(4 * count * depth * inner * piece, 4 * depth * inner, 4),
        name="expand_keep",
    )(place, both, left)


def hop_kernel(kept, *refs, tile):
    arrived, (message, total) = refs[:-2], refs[-2:]
    depth = total.shape[0]
    scales = [scale_of(code, depth) for code in arrived]

    def value_at(rows):
        value = kept[rows, :]
        for code, scale in zip(arrived, scales):
            value = value + decode(code[rows, :], scale)
        return value

    fill(message, total, value_at, tile)


def hop(kept, arrived, step):
    _, depth, piece = kept.shape
    count = arrived[-1].shape[0] // 2

    def at(shift):
        return lambda i: ((2 * i + 1) * 2**shift, 0, 0)

    return pl.pallas_call(
        functools.partial(hop_kernel, tile=min(64, depth)),
        grid=(count,),
        in_specs=[pl.BlockSpec((None, depth, piece), at(step - 1))]
        + [
            pl.BlockSpec((None, depth + EXTRA, piece), at(step - 1 - index))
            for index in range(len(arrived))
        ],
        out_specs=pl.BlockSpec((None, depth + EXTRA, piece), lambda i: (i, 0, 0)),
        out_shape=jax.ShapeDtypeStruct((count, depth + EXTRA, piece), BF16),
        scratch_shapes=[pltpu.VMEM((depth, piece), F32)],
        compiler_params=params(40),
        cost_estimate=cost(400 * count * depth * piece, 12 * count * depth * piece, 4),
        name="hop",
    )(kept, *arrived)


def finish_kernel(kept, *refs, tile, terms):
    arrived, out = refs[:terms], refs[-1]
    depth = out.shape[0]
    scales = [scale_of(code, depth) for code in arrived]

    def add(i, carry):
        rows = pl.ds(pl.multiple_of(i * tile, tile), tile)
        value = kept[rows, :]
        for code, scale in zip(arrived, scales):
            value = value + decode(code[rows, :], scale)
        out[rows, :] = value
        return carry

    lax.fori_loop(0, depth // tile, add, 0)


def finish(kept, arrived, update, chunk, width):
    _, depth, piece = kept.shape
    extra = [] if update is None else [update]
    first = lambda i: (0, 0, 0)
    return pl.pallas_call(
        functools.partial(finish_kernel, tile=min(64, depth), terms=len(arrived)),
        grid=(1,),
        in_specs=[pl.BlockSpec((None, depth, piece), first)]
        + [pl.BlockSpec((None, depth + EXTRA, piece), first)] * len(arrived)
        + [pl.BlockSpec(memory_space=pl.ANY)] * len(extra),
        out_specs=pl.BlockSpec((depth, piece), lambda i: (0, chunk)),
        out_shape=jax.ShapeDtypeStruct((depth, width), F32),
        input_output_aliases={1 + len(arrived): 0} if extra else {},
        compiler_params=params(40),
        cost_estimate=cost(400 * depth * piece, 12 * depth * piece, 0.1),
        name="finish",
    )(kept, *arrived, *extra)


def build(lines, cols):
    def swap(value, distance):
        return lax.ppermute(value, "col", [(i, i ^ distance) for i in range(cols)])

    def by_distance(block):
        held = {0: block}
        for distance in range(2, cols, 2):
            held[distance] = swap(block, distance)
        for distance in range(0, cols, 2):
            held[distance + 1] = swap(held[distance], 1)
        return held

    def place_by_distance(block, me):
        out = jnp.zeros((cols,) + block.shape, block.dtype)
        for distance, value in by_distance(block).items():
            out = lax.dynamic_update_index_in_dim(out, value, me ^ distance, 0)
        return out

    def up(value, senders):
        return lax.ppermute(value, "row", [(i, i + 1) for i in senders])

    def down(value, senders):
        return lax.ppermute(value, "row", [(i, i - 1) for i in senders])

    def after(value, *others):
        return lax.optimization_barrier((value,) + others)[0]

    def walk(held, step):
        held[-step] = up(held[1 - step], range(step - 1, lines - 1))
        held[step] = down(held[step - 1], range(1, lines - step + 1))

    def local(gradient, first_moment, second_moment, left_basis, right_basis):
        me, place = lax.axis_index("col"), lax.axis_index("row")
        depth, width = gradient.shape
        piece = width // CHUNKS
        far = lines - 1
        spot, at = jnp.reshape(place, (1,)), jnp.stack([me, place])
        me_now = jnp.reshape(me, (1,))
        barrier = lax.optimization_barrier
        near = [offset for offset in range(-far, far + 1) if abs(offset) < far]

        left = place_by_distance(left_basis, me).reshape(-1, left_basis.shape[1])
        grads = {0: gradient}
        for step in range(1, lines):
            if step == far:
                left, grads[1 - step], grads[step - 1] = barrier(
                    (left, grads[1 - step], grads[step - 1])
                )
            walk(grads, step)
        before = halfway(spot, left, grads, near, lines, None)

        own, before, grads[-far], grads[far] = barrier(
            (right_basis, before, grads[-far], grads[far])
        )
        rights = {0: own}
        for step in range(1, lines):
            walk(rights, step)
        above, below = rights[far], rights[-far]

        pair, message = pack(halfway(spot, left, grads, [-far, far], lines, before))
        message, rights[-1], rights[1] = barrier((message, rights[-1], rights[1]))
        aligned = depth == width

        def put_block(held, offset):
            there = place + offset
            there = jnp.where((there >= 0) & (there < lines), there, lines)
            return put(jnp.reshape(there, (1,)), rights[offset], held, lines + 1)

        held = None
        for offset in (0, -1, 1):
            held = put_block(held, offset)
        pieces = {1: swap(message, 1)}
        mate_pair = unpack(pieces[1])
        for distance in range(2, cols, 2):
            pieces[distance] = after(swap(message, distance), held[1], mate_pair)
            pieces[distance + 1] = swap(pieces[distance], 1)
        for step in range(2, far if aligned else lines):
            held = put_block(put_block(held, -step), step)
        pieces = [pair, mate_pair] + [unpack(pieces[distance]) for distance in range(2, cols)]
        part = rotate_part(at, pieces, held[0], far if aligned else -1)
        part, above, below = barrier((part, above, below))
        if not aligned:
            above, below = jnp.zeros_like(above), jnp.zeros_like(below)
        new_first, new_second, normed = rotate(
            at, part, pieces, above, below, first_moment, second_moment, lines
        )
        if aligned:
            last = jnp.where(place == 0, after(above, normed), below)
            there = jnp.where((place == 0) | (place == far), far - place, lines)
            held = put(jnp.reshape(there, (1,)), last, held, lines + 1)
        flipped = held[1]

        def cross(value, distance):
            return lax.ppermute(value, "row", [(i, i ^ distance) for i in range(lines)])

        def later_hops(chunk):
            kept, arrived = products[chunk]
            if chunk - 1 in second:
                kept = after(kept, second[chunk - 1])
            if chunk + 1 < len(outgoing):
                kept = after(kept, outgoing[chunk + 1])
            step = 1
            while 2**step < lines:
                message = hop(kept, arrived, step)
                if step == 1:
                    second[chunk] = message
                arrived = arrived + [cross(message, 2**step)]
                step += 1
            products[chunk] = kept, arrived

        products, halves, sent, outgoing, second = [], [], [], [], {}

        def multiply(chunk, *before):
            codes = [swap(code, 2 * index + 2) for index, code in enumerate(sent[chunk])]
            if codes and before:
                codes[0] = after(codes[0], *before)
            message, both = expand_send(spot, *halves[chunk], codes, left, depth)
            outgoing.append(message)
            products.append((expand_keep(spot, both, left, depth), [cross(message, 1)]))

        for batch in range(2):
            ready = after(normed, *sent[0]) if batch else normed
            for keep, mate in restore(me_now, ready, flipped, cols, piece, batch, CHUNKS // 2):
                mate = swap(mate, 1)
                halves.append((keep, mate))
                sent.append([send(keep, mate, distance, []) for distance in range(2, cols, 2)])
        for chunk in range(CHUNKS):
            if chunk >= 2:
                later_hops(chunk - 2)
            multiply(chunk, *([second[chunk - 2]] if chunk - 2 in second else outgoing[-1:]))
        update = None
        for chunk in range(CHUNKS):
            if chunk >= CHUNKS - 2:
                later_hops(chunk)
            update = finish(*products[chunk], update, chunk, width)
        return (new_first, new_second, update)

    return local


def solution(mesh):
    return jax.shard_map(
        build(mesh.shape["row"], mesh.shape["col"]),
        mesh=mesh,
        in_specs=(
            P(("groups", "row"), "col"),
            P(("groups", "row"), "col"),
            P(("groups", "row"), "col"),
            P(("groups", "col"), "row"),
            P(("groups", "row"), "col"),
        ),
        out_specs=(
            P(("groups", "row"), "col"),
            P(("groups", "row"), "col"),
            P(("groups", "row"), "col"),
        ),
        check_vma=False,
    )
```

```python
import functools
import jax
import jax.numpy as jnp
from jax import lax
from jax.experimental import pallas as pl
from jax.experimental.pallas import tpu as pltpu
from jax.sharding import PartitionSpec as P

BETA_ONE = 0.9
BETA_TWO = 0.95
EPSILON = 1e-08
CHUNKS = 4
EXTRA = 16
F32 = jnp.float32
BF16 = jnp.bfloat16
MIB = 2**20


def params(mib):
    return pltpu.CompilerParams(vmem_limit_bytes=mib * MIB)


def cost(flops, moved, weight=4):
    return pl.CostEstimate(
        flops=int(flops * weight), bytes_accessed=int(moved * weight), transcendentals=0
    )


def split(value):
    high = lax.reduce_precision(value, exponent_bits=8, mantissa_bits=7)
    return high.astype(BF16), (value - high).astype(BF16)


def kernel_split(value):
    high = value.astype(BF16)
    return high, (value - high.astype(F32)).astype(BF16)


def dot(a, b, dims):
    return lax.dot_general(a, b, (dims, ((), ())), preferred_element_type=F32)


TOP = 7.5


def encode(value, inverse):
    code = jnp.abs(value) * (inverse * 2.0**TOP)
    for _ in range(4):
        code = code * code
    return jnp.where(value < 0, -code, code).astype(BF16)


def decode(code, scale):
    code = code.astype(F32)
    size = jnp.abs(code)
    root = jnp.exp2(jnp.log2(size) * 0.0625 - TOP) * scale
    root = jnp.where(size > 0, root, 0.0)
    return jnp.where(code < 0, -root, root)


def scale_of(message, depth):
    return jnp.max(message[depth : depth + EXTRA, :].astype(F32), axis=(0, 1), keepdims=True)


def fill(message, total, value_at, tile, again=None):
    depth, piece = message.shape[0] - EXTRA, message.shape[1]

    def add(i, top):
        rows = pl.ds(pl.multiple_of(i * tile, tile), tile)
        value = value_at(rows)
        if again is None:
            total[rows, :] = value
        return jnp.maximum(top, jnp.abs(value))

    top = lax.fori_loop(0, depth // tile, add, jnp.zeros((tile, piece), F32))
    top = jnp.maximum(jnp.max(top, axis=(0, 1), keepdims=True), 1e-30)
    scale = jnp.broadcast_to(top, (EXTRA, piece)).astype(BF16)
    message[depth : depth + EXTRA, :] = scale
    inverse = 1.0 / jnp.max(scale.astype(F32), axis=(0, 1), keepdims=True)

    def put(i, carry):
        rows = pl.ds(pl.multiple_of(i * tile, tile), tile)
        value = total[rows, :] if again is None else again(rows)
        message[rows, :] = encode(value, inverse)
        return carry

    lax.fori_loop(0, depth // tile, put, 0)


def halfway_kernel(place_ref, left, *refs, offsets, lines, first):
    pieces, refs = refs[: len(offsets)], refs[len(offsets) :]
    total = refs[-1]
    depth = pieces[0].shape[0]
    total[...] = jnp.zeros_like(total) if first else refs[0][...]
    place = place_ref[0]
    for offset, piece in zip(offsets, pieces):

        @pl.when((place + offset >= 0) & (place + offset < lines))
        def _(offset=offset, piece=piece):
            rows = left[pl.ds(pl.multiple_of((place + offset) * depth, depth), depth), :]
            total[...] += dot(rows, piece[...], ((0,), (0,)))

    refs[-2][...] = total[...]


def halfway(place, left, held, offsets, lines, before):
    pieces = [held[offset] for offset in offsets]
    depth, width = pieces[0].shape
    inner = left.shape[1]
    tile = min(256, inner)
    whole = pl.BlockSpec((depth, width), lambda i, s: (0, 0))
    block = pl.BlockSpec((tile, width), lambda i, s: (i, 0))
    extra = [] if before is None else [before]
    return pl.pallas_call(
        functools.partial(halfway_kernel, offsets=offsets, lines=lines, first=before is None),
        grid_spec=pltpu.PrefetchScalarGridSpec(
            num_scalar_prefetch=1,
            grid=(inner // tile,),
            in_specs=[pl.BlockSpec((left.shape[0], tile), lambda i, s: (0, i))]
            + [whole] * len(pieces)
            + [block] * len(extra),
            out_specs=block,
            scratch_shapes=[pltpu.VMEM((tile, width), F32)],
        ),
        out_shape=jax.ShapeDtypeStruct((inner, width), F32),
        compiler_params=params(48),
        cost_estimate=cost(8 * depth * inner * width, 8 * depth * inner, 0.3),
        name="halfway",
    )(place, left, *pieces, *extra)


def pack_kernel(value, pair, message, *, tile):
    depth, _ = value.shape

    def value_at(rows):
        now = value[rows, :]
        high, low = kernel_split(now)
        pair[0, rows, :] = high
        pair[1, rows, :] = low
        return now

    fill(message, None, value_at, tile, lambda rows: value[rows, :])


def pack(value):
    depth, width = value.shape
    return pl.pallas_call(
        functools.partial(pack_kernel, tile=min(16, depth)),
        out_shape=[
            jax.ShapeDtypeStruct((2, depth, width), BF16),
            jax.ShapeDtypeStruct((depth + EXTRA, width), BF16),
        ],
        compiler_params=params(60),
        cost_estimate=cost(400 * depth * width, 10 * depth * width, 0.3),
        name="pack",
    )(value)


def unpack_kernel(message, scales, pair, *, tile):
    _, depth, _ = pair.shape
    scale = scale_of(scales, 0)

    def put(i, carry):
        rows = pl.ds(pl.multiple_of(i * tile, tile), tile)
        high, low = kernel_split(decode(message[rows, :], scale))
        pair[0, rows, :] = high
        pair[1, rows, :] = low
        return carry

    lax.fori_loop(0, depth // tile, put, 0)


def unpack(message):
    depth, width = message.shape[0] - EXTRA, message.shape[1]
    step = min(256, depth)
    return pl.pallas_call(
        functools.partial(unpack_kernel, tile=min(16, step)),
        grid=(depth // step,),
        in_specs=[
            pl.BlockSpec((step, width), lambda i: (i, 0)),
            pl.BlockSpec((EXTRA, width), lambda i: (depth // EXTRA, 0)),
        ],
        out_specs=pl.BlockSpec((2, step, width), lambda i: (0, i, 0)),
        out_shape=jax.ShapeDtypeStruct((2, depth, width), BF16),
        compiler_params=params(60),
        cost_estimate=cost(400 * depth * width, 6 * depth * width, 0.3),
        name="unpack",
    )(message, message)


def put_kernel(there_ref, piece, *refs):
    right, flipped = refs[-2:]
    right[...] = piece[...]
    flipped[0] = piece[...].T


def put(there, piece, held, blocks):
    depth, width = piece.shape
    extra = [] if held is None else list(held)
    return pl.pallas_call(
        put_kernel,
        grid_spec=pltpu.PrefetchScalarGridSpec(
            num_scalar_prefetch=1,
            grid=(1,),
            in_specs=[pl.BlockSpec((depth, width), lambda i, s: (0, 0))]
            + [pl.BlockSpec(memory_space=pl.ANY)] * len(extra),
            out_specs=[
                pl.BlockSpec((depth, width), lambda i, s: (s[0], 0)),
                pl.BlockSpec((1, width, depth), lambda i, s: (s[0], 0, 0)),
            ],
        ),
        out_shape=[
            jax.ShapeDtypeStruct((blocks * depth, width), BF16),
            jax.ShapeDtypeStruct((blocks, width, depth), BF16),
        ],
        input_output_aliases={2: 0, 3: 1} if extra else {},
        compiler_params=params(60),
        cost_estimate=cost(0, 6 * depth * width, 0.3),
        name="put",
    )(there, piece, *extra)


def rotate_part_kernel(at_ref, *refs, cols, width, far):
    pieces, (right, out, total) = refs[:cols], refs[cols:]
    tile = out.shape[0]
    me, place = at_ref[0], at_ref[1]
    total[...] = jnp.zeros_like(total)
    for distance in range(cols):
        block = me ^ distance
        late = (block == far - place) & ((place == 0) | (place == far))

        @pl.when(jnp.logical_not(late))
        def _(distance=distance, block=block):
            rows = right[pl.ds(pl.multiple_of(block * width, width), width), :]
            total[...] += dot(pieces[distance][...].reshape(2 * tile, width), rows, ((1,), (0,)))

    out[...] = total[:tile, :] + total[tile:, :]


def rotate_part(at, pieces, right, far):
    cols = len(pieces)
    _, depth, width = pieces[0].shape
    tile = min(256, depth)
    return pl.pallas_call(
        functools.partial(rotate_part_kernel, cols=cols, width=width, far=far),
        grid_spec=pltpu.PrefetchScalarGridSpec(
            num_scalar_prefetch=1,
            grid=(depth // tile,),
            in_specs=[pl.BlockSpec((2, tile, width), lambda i, s: (0, i, 0))] * cols
            + [
                pl.BlockSpec(
                    (cols * width, width), lambda i, s: (0, 0), pipeline_mode=pl.Buffered(1)
                )
            ],
            out_specs=pl.BlockSpec((tile, width), lambda i, s: (i, 0)),
            scratch_shapes=[pltpu.VMEM((2 * tile, width), F32)],
        ),
        out_shape=jax.ShapeDtypeStruct((depth, width), F32),
        compiler_params=params(48),
        cost_estimate=cost(4 * depth * width * width * cols, 20 * depth * width, 0.3),
        name="rotate_part",
    )(at, *pieces, right)


def rotate_kernel(at_ref, part, above, below, first, second, *refs, cols, lines):
    pieces, refs = refs[:cols], refs[cols + 1 :]
    new_first, new_second, normed, flipped, held, last, arrived = refs
    tile, width = first.shape
    depth = last.shape[0]
    me, place = at_ref[0], at_ref[1]
    step, steps = pl.program_id(0), held.shape[1] // tile
    start = (lines - 1 - place) * depth
    distance_now = me ^ (start // width)

    def copy(distance, at):
        rows = pl.ds(at * tile, tile)
        if depth == width:
            source = pieces[distance].at[:, rows, :]
        else:
            columns = pl.ds(pl.multiple_of(lax.rem(start, width), depth), depth)
            source = pieces[distance].at[:, rows, columns]
        return pltpu.make_async_copy(source, held.at[:, rows, :], arrived.at[at])

    @pl.when(step == 0)
    def _():
        for distance in range(cols):

            @pl.when(distance_now == distance)
            def _(distance=distance):
                for at in range(steps):
                    copy(distance, at).start()

        last[...] = jnp.where(place == 0, above[...], below[...])
        flipped[0] = last[...].T

    for at in range(steps):

        @pl.when(step == at)
        def _(at=at):
            copy(0, at).wait()

    rows = pl.ds(pl.multiple_of(step * tile, tile), tile)
    both = dot(held[:, rows, :].reshape(2 * tile, depth), last[...], ((1,), (0,)))
    rotated = part[...] + both[:tile] + both[tile:]
    one = BETA_ONE * first[...] + (1.0 - BETA_ONE) * rotated
    two = BETA_TWO * second[...] + (1.0 - BETA_TWO) * rotated * rotated
    new_first[...] = one
    new_second[...] = two
    high, low = kernel_split(one / (jnp.sqrt(two) + EPSILON))
    normed[0] = high
    normed[1] = low


def rotate(at, part, pieces, above, below, first, second, flipped, lines):
    cols = len(pieces)
    rows, width = first.shape
    depth = above.shape[0]
    tile = min(256, rows)
    block = pl.BlockSpec((tile, width), lambda i, s: (i, 0))
    pair = pl.BlockSpec((2, tile, width), lambda i, s: (0, i, 0))
    whole = pl.BlockSpec(above.shape, lambda i, s: (0, 0), pipeline_mode=pl.Buffered(1))
    return pl.pallas_call(
        functools.partial(rotate_kernel, cols=cols, lines=lines),
        grid_spec=pltpu.PrefetchScalarGridSpec(
            num_scalar_prefetch=1,
            grid=(rows // tile,),
            in_specs=[block, whole, whole, block, block]
            + [pl.BlockSpec(memory_space=pl.ANY)] * (cols + 1),
            out_specs=[
                block,
                block,
                pair,
                pl.BlockSpec((1, width, depth), lambda i, s: (s[2], 0, 0)),
            ],
            scratch_shapes=[
                pltpu.VMEM((2, rows, depth), BF16),
                pltpu.VMEM((depth, width), BF16),
                pltpu.SemaphoreType.DMA((rows // tile,)),
            ],
        ),
        out_shape=[
            jax.ShapeDtypeStruct((rows, width), F32),
            jax.ShapeDtypeStruct((rows, width), F32),
            jax.ShapeDtypeStruct((2, rows, width), BF16),
            jax.ShapeDtypeStruct(flipped.shape, BF16),
        ],
        input_output_aliases={6 + cols: 3},
        compiler_params=params(44),
        cost_estimate=cost(4 * rows * width * depth, 30 * rows * width),
        name="rotate",
    )(at, part, above, below, first, second, *pieces, flipped)


def restore_kernel(me_ref, normed, *refs, cols):
    flipped, outs = refs[:cols], refs[cols:]
    tile = normed.shape[1]
    piece = outs[0].shape[2]
    both = normed[...].reshape(2 * tile, normed.shape[2])
    for distance in range(cols):
        term = dot(both, flipped[distance][0], ((1,), (0,)))
        term = term[:tile] + term[tile:]
        for at in range(len(outs) // 2):
            out = outs[2 * at + distance % 2]
            out[distance // 2] = term[:, at * piece : (at + 1) * piece]


def restore(me, normed, flipped, cols, piece, batch, count):
    _, depth, inner = normed.shape
    wide = flipped.shape[2]
    tile = min(256, depth)
    out = pl.BlockSpec((cols // 2, tile, piece), lambda i, s: (0, i, 0))

    def columns(distance):
        def at(i, s):
            start = (s[0] ^ distance) * inner + batch * count * piece
            return start // wide, 0, lax.rem(start, wide) // (count * piece)

        return pl.BlockSpec((1, inner, count * piece), at, pipeline_mode=pl.Buffered(1))

    outs = pl.pallas_call(
        functools.partial(restore_kernel, cols=cols),
        grid_spec=pltpu.PrefetchScalarGridSpec(
            num_scalar_prefetch=1,
            grid=(depth // tile,),
            in_specs=[pl.BlockSpec((2, tile, inner), lambda i, s: (0, i, 0))]
            + [columns(distance) for distance in range(cols)],
            out_specs=[out] * (2 * count),
        ),
        out_shape=[jax.ShapeDtypeStruct((cols // 2, depth, piece), F32)] * (2 * count),
        compiler_params=params(44),
        cost_estimate=cost(
            4 * depth * inner * count * piece * cols, 8 * depth * count * piece * cols
        ),
        name="restore",
    )(me, normed, *([flipped] * cols))
    return [(outs[2 * at], outs[2 * at + 1]) for at in range(count)]


def summed(keep, mate, codes):
    depth = keep.shape[1]
    scales = [scale_of(code, depth) for code in codes]

    def value_at(rows):
        value = keep[0, rows, :] + mate[0, rows, :]
        for code, scale in zip(codes, scales):
            value = value + decode(code[rows, :], scale)
        return value

    return value_at


def send_kernel(keep, mate, *refs, tile):
    codes, (message, total) = refs[:-2], refs[-2:]
    fill(message, total, summed(keep, mate, codes), tile)


def send(keep, mate, distance, codes):
    _, depth, piece = keep.shape
    tile = min(64, depth)
    pair = pl.BlockSpec((1, depth, piece), lambda i: (distance // 2, 0, 0))
    message = pl.BlockSpec((depth + EXTRA, piece), lambda i: (0, 0))
    return pl.pallas_call(
        functools.partial(send_kernel, tile=tile),
        grid=(1,),
        in_specs=[pair, pair] + [message] * len(codes),
        out_specs=message,
        out_shape=jax.ShapeDtypeStruct((depth + EXTRA, piece), BF16),
        scratch_shapes=[pltpu.VMEM((depth, piece), F32)],
        compiler_params=params(16),
        cost_estimate=cost(400 * depth * piece, 18 * depth * piece, 4),
        name="send",
    )(keep, mate, *codes)


def expand_send_kernel(place_ref, keep, mate, *refs, tile):
    codes, (left, message, both, total) = refs[:-4], refs[-4:]
    depth, piece = total.shape

    @pl.when(pl.program_id(0) == 0)
    def _():
        value_at = summed(keep, mate, codes)

        def put(i, carry):
            rows = pl.ds(pl.multiple_of(i * tile, tile), tile)
            high, low = kernel_split(value_at(rows))
            both[rows, :piece] = high
            both[rows, piece:] = low
            return carry

        lax.fori_loop(0, both.shape[0] // tile, put, 0)

    product = dot(left[...], both[...], ((1,), (0,)))
    total[...] = product[:, :piece] + product[:, piece:]
    fill(message, None, lambda rows: total[rows, :], tile, lambda rows: total[rows, :])


def expand_send(place, keep, mate, codes, left, depth):
    inner, piece = keep.shape[1:]
    count = left.shape[0] // depth // 2
    pair = pl.BlockSpec((1, inner, piece), lambda i, s: (0, 0, 0))
    code = pl.BlockSpec((inner + EXTRA, piece), lambda i, s: (0, 0))
    return pl.pallas_call(
        functools.partial(expand_send_kernel, tile=min(64, depth)),
        grid_spec=pltpu.PrefetchScalarGridSpec(
            num_scalar_prefetch=1,
            grid=(count,),
            in_specs=[pair, pair]
            + [code] * len(codes)
            + [pl.BlockSpec((depth, inner), lambda i, s: (s[0] ^ (2 * i + 1), 0))],
            out_specs=[
                pl.BlockSpec((None, depth + EXTRA, piece), lambda i, s: (i, 0, 0)),
                pl.BlockSpec((inner, 2 * piece), lambda i, s: (0, 0)),
            ],
            scratch_shapes=[pltpu.VMEM((depth, piece), F32)],
        ),
        out_shape=[
            jax.ShapeDtypeStruct((count, depth + EXTRA, piece), BF16),
            jax.ShapeDtypeStruct((inner, 2 * piece), BF16),
        ],
        compiler_params=params(40),
        cost_estimate=cost(4 * count * depth * inner * piece, 4 * depth * inner, 4),
        name="expand_send",
    )(place, keep, mate, *codes, left)


def expand_keep_kernel(place_ref, both, left, out):
    piece = out.shape[1]
    product = dot(left[...], both[...], ((1,), (0,)))
    out[...] = product[:, :piece] + product[:, piece:]


def expand_keep(place, both, left, depth):
    inner, piece = both.shape[0], both.shape[1] // 2
    count = left.shape[0] // depth // 2
    return pl.pallas_call(
        expand_keep_kernel,
        grid_spec=pltpu.PrefetchScalarGridSpec(
            num_scalar_prefetch=1,
            grid=(count,),
            in_specs=[
                pl.BlockSpec((inner, 2 * piece), lambda i, s: (0, 0)),
                pl.BlockSpec((depth, inner), lambda i, s: (s[0] ^ (2 * i), 0)),
            ],
            out_specs=pl.BlockSpec((None, depth, piece), lambda i, s: (i, 0, 0)),
        ),
        out_shape=jax.ShapeDtypeStruct((count, depth, piece), F32),
        compiler_params=params(60),
        cost_estimate=cost(4 * count * depth * inner * piece, 4 * depth * inner, 4),
        name="expand_keep",
    )(place, both, left)


def hop_kernel(kept, *refs, tile):
    arrived, (message, total) = refs[:-2], refs[-2:]
    depth = total.shape[0]
    scales = [scale_of(code, depth) for code in arrived]

    def value_at(rows):
        value = kept[rows, :]
        for code, scale in zip(arrived, scales):
            value = value + decode(code[rows, :], scale)
        return value

    fill(message, total, value_at, tile)


def hop(kept, arrived, step):
    _, depth, piece = kept.shape
    count = arrived[-1].shape[0] // 2

    def at(shift):
        return lambda i: ((2 * i + 1) * 2**shift, 0, 0)

    return pl.pallas_call(
        functools.partial(hop_kernel, tile=min(64, depth)),
        grid=(count,),
        in_specs=[pl.BlockSpec((None, depth, piece), at(step - 1))]
        + [
            pl.BlockSpec((None, depth + EXTRA, piece), at(step - 1 - index))
            for index in range(len(arrived))
        ],
        out_specs=pl.BlockSpec((None, depth + EXTRA, piece), lambda i: (i, 0, 0)),
        out_shape=jax.ShapeDtypeStruct((count, depth + EXTRA, piece), BF16),
        scratch_shapes=[pltpu.VMEM((depth, piece), F32)],
        compiler_params=params(40),
        cost_estimate=cost(400 * count * depth * piece, 12 * count * depth * piece, 4),
        name="hop",
    )(kept, *arrived)


def finish_kernel(kept, *refs, tile, terms):
    arrived, out = refs[:terms], refs[-1]
    depth = out.shape[0]
    scales = [scale_of(code, depth) for code in arrived]

    def add(i, carry):
        rows = pl.ds(pl.multiple_of(i * tile, tile), tile)
        value = kept[rows, :]
        for code, scale in zip(arrived, scales):
            value = value + decode(code[rows, :], scale)
        out[rows, :] = value
        return carry

    lax.fori_loop(0, depth // tile, add, 0)


def finish(kept, arrived, update, chunk, width):
    _, depth, piece = kept.shape
    extra = [] if update is None else [update]
    first = lambda i: (0, 0, 0)
    return pl.pallas_call(
        functools.partial(finish_kernel, tile=min(64, depth), terms=len(arrived)),
        grid=(1,),
        in_specs=[pl.BlockSpec((None, depth, piece), first)]
        + [pl.BlockSpec((None, depth + EXTRA, piece), first)] * len(arrived)
        + [pl.BlockSpec(memory_space=pl.ANY)] * len(extra),
        out_specs=pl.BlockSpec((depth, piece), lambda i: (0, chunk)),
        out_shape=jax.ShapeDtypeStruct((depth, width), F32),
        input_output_aliases={1 + len(arrived): 0} if extra else {},
        compiler_params=params(40),
        cost_estimate=cost(400 * depth * piece, 12 * depth * piece, 0.1),
        name="finish",
    )(kept, *arrived, *extra)


def build(lines, cols):
    def swap(value, distance):
        return lax.ppermute(value, "col", [(i, i ^ distance) for i in range(cols)])

    def by_distance(block):
        held = {0: block}
        for distance in range(2, cols, 2):
            held[distance] = swap(block, distance)
        for distance in range(0, cols, 2):
            held[distance + 1] = swap(held[distance], 1)
        return held

    def place_by_distance(block, me):
        out = jnp.zeros((cols,) + block.shape, block.dtype)
        for distance, value in by_distance(block).items():
            out = lax.dynamic_update_index_in_dim(out, value, me ^ distance, 0)
        return out

    def up(value, senders):
        return lax.ppermute(value, "row", [(i, i + 1) for i in senders])

    def down(value, senders):
        return lax.ppermute(value, "row", [(i, i - 1) for i in senders])

    def after(value, *others):
        return lax.optimization_barrier((value,) + others)[0]

    def walk(held, step):
        held[-step] = up(held[1 - step], range(step - 1, lines - 1))
        held[step] = down(held[step - 1], range(1, lines - step + 1))

    def local(gradient, first_moment, second_moment, left_basis, right_basis):
        me, place = lax.axis_index("col"), lax.axis_index("row")
        depth, width = gradient.shape
        piece = width // CHUNKS
        far = lines - 1
        ends = (place == 0) | (place == far) if depth == width else False
        spot = jnp.reshape(place, (1,))
        at = jnp.stack([me, place, jnp.where(ends, far - place, lines)])
        me_now = jnp.reshape(me, (1,))
        barrier = lax.optimization_barrier
        near = [offset for offset in range(-far, far + 1) if abs(offset) < far]

        left = place_by_distance(left_basis, me).reshape(-1, left_basis.shape[1])
        grads = {0: gradient}
        for step in range(1, lines):
            if step == far:
                left, grads[1 - step], grads[step - 1] = barrier(
                    (left, grads[1 - step], grads[step - 1])
                )
            walk(grads, step)
        before = halfway(spot, left, grads, near, lines, None)

        own, before, grads[-far], grads[far] = barrier(
            (right_basis, before, grads[-far], grads[far])
        )
        rights = {0: own}
        for step in range(1, lines):
            walk(rights, step)
        above, below = rights[far], rights[-far]

        pair, message = pack(halfway(spot, left, grads, [-far, far], lines, before))
        message, rights[-1], rights[1] = barrier((message, rights[-1], rights[1]))
        aligned = depth == width

        def put_block(held, offset):
            there = place + offset
            there = jnp.where((there >= 0) & (there < lines), there, lines)
            return put(jnp.reshape(there, (1,)), rights[offset], held, lines + 1)

        held = None
        for offset in (0, -1, 1):
            held = put_block(held, offset)
        pieces = {1: swap(message, 1)}
        mate_pair = unpack(pieces[1])
        for distance in range(2, cols, 2):
            pieces[distance] = after(swap(message, distance), held[1], mate_pair)
            pieces[distance + 1] = swap(pieces[distance], 1)
        for step in range(2, far if aligned else lines):
            held = put_block(put_block(held, -step), step)
        pieces = [pair, mate_pair] + [unpack(pieces[distance]) for distance in range(2, cols)]
        part = rotate_part(at, pieces, held[0], far if aligned else -1)
        part, above, below = barrier((part, above, below))
        if not aligned:
            above, below = jnp.zeros_like(above), jnp.zeros_like(below)
        new_first, new_second, normed, flipped = rotate(
            at, part, pieces, above, below, first_moment, second_moment, held[1], lines
        )

        def cross(value, distance):
            return lax.ppermute(value, "row", [(i, i ^ distance) for i in range(lines)])

        def later_hops(chunk):
            kept, arrived = products[chunk]
            if chunk - 1 in second:
                kept = after(kept, second[chunk - 1])
            if chunk + 1 < len(outgoing):
                kept = after(kept, outgoing[chunk + 1])
            step = 1
            while 2**step < lines:
                message = hop(kept, arrived, step)
                if step == 1:
                    second[chunk] = message
                arrived = arrived + [cross(message, 2**step)]
                step += 1
            products[chunk] = kept, arrived

        products, halves, sent, outgoing, second = [], [], [], [], {}

        def multiply(chunk, *before):
            codes = [swap(code, 2 * index + 2) for index, code in enumerate(sent[chunk])]
            if codes and before:
                codes[0] = after(codes[0], *before)
            message, both = expand_send(spot, *halves[chunk], codes, left, depth)
            outgoing.append(message)
            products.append((expand_keep(spot, both, left, depth), [cross(message, 1)]))

        def sums(batch, count, *before):
            ready = after(normed, *before) if before else normed
            for keep, mate in restore(me_now, ready, flipped, cols, piece, batch, count):
                mate = swap(mate, 1)
                halves.append((keep, mate))
                sent.append([send(keep, mate, distance, []) for distance in range(2, cols, 2)])

        sums(0, 2)
        sums(1, 2, *sent[0])
        for chunk in range(CHUNKS):
            if chunk >= 2:
                later_hops(chunk - 2)
            multiply(chunk, *([second[chunk - 2]] if chunk - 2 in second else outgoing[-1:]))
        update = None
        for chunk in range(CHUNKS):
            if chunk >= CHUNKS - 2:
                later_hops(chunk)
            update = finish(*products[chunk], update, chunk, width)
        return (new_first, new_second, update)

    return local


def solution(mesh):
    return jax.shard_map(
        build(mesh.shape["row"], mesh.shape["col"]),
        mesh=mesh,
        in_specs=(
            P(("groups", "row"), "col"),
            P(("groups", "row"), "col"),
            P(("groups", "row"), "col"),
            P(("groups", "col"), "row"),
            P(("groups", "row"), "col"),
        ),
        out_specs=(
            P(("groups", "row"), "col"),
            P(("groups", "row"), "col"),
            P(("groups", "row"), "col"),
        ),
        check_vma=False,
    )
```

```python
import functools
import jax
import jax.numpy as jnp
from jax import lax
from jax.experimental import pallas as pl
from jax.experimental.pallas import tpu as pltpu
from jax.sharding import PartitionSpec as P

BETA_ONE = 0.9
BETA_TWO = 0.95
EPSILON = 1e-08
CHUNKS = 4
EXTRA = 16
F32 = jnp.float32
BF16 = jnp.bfloat16
MIB = 2**20


def params(mib):
    return pltpu.CompilerParams(vmem_limit_bytes=mib * MIB)


def cost(flops, moved, weight=4):
    return pl.CostEstimate(
        flops=int(flops * weight), bytes_accessed=int(moved * weight), transcendentals=0
    )


def split(value):
    high = lax.reduce_precision(value, exponent_bits=8, mantissa_bits=7)
    return high.astype(BF16), (value - high).astype(BF16)


def kernel_split(value):
    high = value.astype(BF16)
    return high, (value - high.astype(F32)).astype(BF16)


def dot(a, b, dims):
    return lax.dot_general(a, b, (dims, ((), ())), preferred_element_type=F32)


TOP = 7.5


def encode(value, inverse):
    code = jnp.abs(value) * (inverse * 2.0**TOP)
    for _ in range(4):
        code = code * code
    return jnp.where(value < 0, -code, code).astype(BF16)


def decode(code, scale):
    code = code.astype(F32)
    size = jnp.abs(code)
    root = jnp.exp2(jnp.log2(size) * 0.0625 - TOP) * scale
    root = jnp.where(size > 0, root, 0.0)
    return jnp.where(code < 0, -root, root)


def scale_of(message, depth):
    return jnp.max(message[depth : depth + EXTRA, :].astype(F32), axis=(0, 1), keepdims=True)


def fill(message, total, value_at, tile, again=None):
    depth, piece = message.shape[0] - EXTRA, message.shape[1]

    def add(i, top):
        rows = pl.ds(pl.multiple_of(i * tile, tile), tile)
        value = value_at(rows)
        if again is None:
            total[rows, :] = value
        return jnp.maximum(top, jnp.abs(value))

    top = lax.fori_loop(0, depth // tile, add, jnp.zeros((tile, piece), F32))
    top = jnp.maximum(jnp.max(top, axis=(0, 1), keepdims=True), 1e-30)
    scale = jnp.broadcast_to(top, (EXTRA, piece)).astype(BF16)
    message[depth : depth + EXTRA, :] = scale
    inverse = 1.0 / jnp.max(scale.astype(F32), axis=(0, 1), keepdims=True)

    def put(i, carry):
        rows = pl.ds(pl.multiple_of(i * tile, tile), tile)
        value = total[rows, :] if again is None else again(rows)
        message[rows, :] = encode(value, inverse)
        return carry

    lax.fori_loop(0, depth // tile, put, 0)


def halfway_kernel(place_ref, left, *refs, offsets, lines, first):
    pieces, refs = refs[: len(offsets)], refs[len(offsets) :]
    total = refs[-1]
    depth = pieces[0].shape[0]
    total[...] = jnp.zeros_like(total) if first else refs[0][...]
    place = place_ref[0]
    for offset, piece in zip(offsets, pieces):

        @pl.when((place + offset >= 0) & (place + offset < lines))
        def _(offset=offset, piece=piece):
            rows = left[pl.ds(pl.multiple_of((place + offset) * depth, depth), depth), :]
            total[...] += dot(rows, piece[...], ((0,), (0,)))

    refs[-2][...] = total[...]


def halfway(place, left, held, offsets, lines, before):
    pieces = [held[offset] for offset in offsets]
    depth, width = pieces[0].shape
    inner = left.shape[1]
    tile = min(256, inner)
    whole = pl.BlockSpec((depth, width), lambda i, s: (0, 0))
    block = pl.BlockSpec((tile, width), lambda i, s: (i, 0))
    extra = [] if before is None else [before]
    return pl.pallas_call(
        functools.partial(halfway_kernel, offsets=offsets, lines=lines, first=before is None),
        grid_spec=pltpu.PrefetchScalarGridSpec(
            num_scalar_prefetch=1,
            grid=(inner // tile,),
            in_specs=[pl.BlockSpec((left.shape[0], tile), lambda i, s: (0, i))]
            + [whole] * len(pieces)
            + [block] * len(extra),
            out_specs=block,
            scratch_shapes=[pltpu.VMEM((tile, width), F32)],
        ),
        out_shape=jax.ShapeDtypeStruct((inner, width), F32),
        compiler_params=params(48),
        cost_estimate=cost(8 * depth * inner * width, 8 * depth * inner, 0.3),
        name="halfway",
    )(place, left, *pieces, *extra)


def pack_kernel(value, pair, message, *, tile):
    depth, _ = value.shape

    def value_at(rows):
        now = value[rows, :]
        high, low = kernel_split(now)
        pair[0, rows, :] = high
        pair[1, rows, :] = low
        return now

    fill(message, None, value_at, tile, lambda rows: value[rows, :])


def pack(value):
    depth, width = value.shape
    return pl.pallas_call(
        functools.partial(pack_kernel, tile=min(16, depth)),
        out_shape=[
            jax.ShapeDtypeStruct((2, depth, width), BF16),
            jax.ShapeDtypeStruct((depth + EXTRA, width), BF16),
        ],
        compiler_params=params(60),
        cost_estimate=cost(400 * depth * width, 10 * depth * width, 0.3),
        name="pack",
    )(value)


def unpack_kernel(message, scales, pair, *, tile):
    _, depth, _ = pair.shape
    scale = scale_of(scales, 0)

    def put(i, carry):
        rows = pl.ds(pl.multiple_of(i * tile, tile), tile)
        high, low = kernel_split(decode(message[rows, :], scale))
        pair[0, rows, :] = high
        pair[1, rows, :] = low
        return carry

    lax.fori_loop(0, depth // tile, put, 0)


def unpack(message):
    depth, width = message.shape[0] - EXTRA, message.shape[1]
    step = min(256, depth)
    return pl.pallas_call(
        functools.partial(unpack_kernel, tile=min(16, step)),
        grid=(depth // step,),
        in_specs=[
            pl.BlockSpec((step, width), lambda i: (i, 0)),
            pl.BlockSpec((EXTRA, width), lambda i: (depth // EXTRA, 0)),
        ],
        out_specs=pl.BlockSpec((2, step, width), lambda i: (0, i, 0)),
        out_shape=jax.ShapeDtypeStruct((2, depth, width), BF16),
        compiler_params=params(60),
        cost_estimate=cost(400 * depth * width, 6 * depth * width, 0.3),
        name="unpack",
    )(message, message)


def put_kernel(there_ref, piece, *refs):
    right, flipped = refs[-2:]
    right[...] = piece[...]
    flipped[0] = piece[...].T


def put(there, piece, held, blocks):
    depth, width = piece.shape
    extra = [] if held is None else list(held)
    return pl.pallas_call(
        put_kernel,
        grid_spec=pltpu.PrefetchScalarGridSpec(
            num_scalar_prefetch=1,
            grid=(1,),
            in_specs=[pl.BlockSpec((depth, width), lambda i, s: (0, 0))]
            + [pl.BlockSpec(memory_space=pl.ANY)] * len(extra),
            out_specs=[
                pl.BlockSpec((depth, width), lambda i, s: (s[0], 0)),
                pl.BlockSpec((1, width, depth), lambda i, s: (s[0], 0, 0)),
            ],
        ),
        out_shape=[
            jax.ShapeDtypeStruct((blocks * depth, width), BF16),
            jax.ShapeDtypeStruct((blocks, width, depth), BF16),
        ],
        input_output_aliases={2: 0, 3: 1} if extra else {},
        compiler_params=params(60),
        cost_estimate=cost(0, 6 * depth * width, 0.3),
        name="put",
    )(there, piece, *extra)


def rotate_part_kernel(at_ref, *refs, cols, width, far):
    pieces, (right, out, total) = refs[:cols], refs[cols:]
    tile = out.shape[0]
    me, place = at_ref[0], at_ref[1]
    total[...] = jnp.zeros_like(total)
    for distance in range(cols):
        block = me ^ distance
        late = (block == far - place) & ((place == 0) | (place == far))

        @pl.when(jnp.logical_not(late))
        def _(distance=distance, block=block):
            rows = right[pl.ds(pl.multiple_of(block * width, width), width), :]
            total[...] += dot(pieces[distance][...].reshape(2 * tile, width), rows, ((1,), (0,)))

    out[...] = total[:tile, :] + total[tile:, :]


def rotate_part(at, pieces, right, far):
    cols = len(pieces)
    _, depth, width = pieces[0].shape
    tile = min(256, depth)
    return pl.pallas_call(
        functools.partial(rotate_part_kernel, cols=cols, width=width, far=far),
        grid_spec=pltpu.PrefetchScalarGridSpec(
            num_scalar_prefetch=1,
            grid=(depth // tile,),
            in_specs=[pl.BlockSpec((2, tile, width), lambda i, s: (0, i, 0))] * cols
            + [
                pl.BlockSpec(
                    (cols * width, width), lambda i, s: (0, 0), pipeline_mode=pl.Buffered(1)
                )
            ],
            out_specs=pl.BlockSpec((tile, width), lambda i, s: (i, 0)),
            scratch_shapes=[pltpu.VMEM((2 * tile, width), F32)],
        ),
        out_shape=jax.ShapeDtypeStruct((depth, width), F32),
        compiler_params=params(48),
        cost_estimate=cost(4 * depth * width * width * cols, 20 * depth * width, 0.3),
        name="rotate_part",
    )(at, *pieces, right)


def rotate_kernel(at_ref, part, above, below, first, second, *refs, cols, lines):
    pieces, refs = refs[:cols], refs[cols + 1 :]
    new_first, new_second, normed, flipped, held, last, arrived = refs
    tile, width = first.shape
    depth = last.shape[0]
    me, place = at_ref[0], at_ref[1]
    step, steps = pl.program_id(0), held.shape[1] // tile
    start = (lines - 1 - place) * depth
    distance_now = me ^ (start // width)

    def copy(distance, at):
        rows = pl.ds(at * tile, tile)
        if depth == width:
            source = pieces[distance].at[:, rows, :]
        else:
            columns = pl.ds(pl.multiple_of(lax.rem(start, width), depth), depth)
            source = pieces[distance].at[:, rows, columns]
        return pltpu.make_async_copy(source, held.at[:, rows, :], arrived.at[at])

    @pl.when(step == 0)
    def _():
        for distance in range(cols):

            @pl.when(distance_now == distance)
            def _(distance=distance):
                for at in range(steps):
                    copy(distance, at).start()

        last[...] = jnp.where(place == 0, above[...], below[...])
        flipped[0] = last[...].T

    for at in range(steps):

        @pl.when(step == at)
        def _(at=at):
            copy(0, at).wait()

    rows = pl.ds(pl.multiple_of(step * tile, tile), tile)
    both = dot(held[:, rows, :].reshape(2 * tile, depth), last[...], ((1,), (0,)))
    rotated = part[...] + both[:tile] + both[tile:]
    one = BETA_ONE * first[...] + (1.0 - BETA_ONE) * rotated
    two = BETA_TWO * second[...] + (1.0 - BETA_TWO) * rotated * rotated
    new_first[...] = one
    new_second[...] = two
    high, low = kernel_split(one / (jnp.sqrt(two) + EPSILON))
    normed[0] = high
    normed[1] = low


def rotate(at, part, pieces, above, below, first, second, flipped, lines):
    cols = len(pieces)
    rows, width = first.shape
    depth = above.shape[0]
    tile = min(256, rows)
    block = pl.BlockSpec((tile, width), lambda i, s: (i, 0))
    pair = pl.BlockSpec((2, tile, width), lambda i, s: (0, i, 0))
    whole = pl.BlockSpec(above.shape, lambda i, s: (0, 0), pipeline_mode=pl.Buffered(1))
    return pl.pallas_call(
        functools.partial(rotate_kernel, cols=cols, lines=lines),
        grid_spec=pltpu.PrefetchScalarGridSpec(
            num_scalar_prefetch=1,
            grid=(rows // tile,),
            in_specs=[block, whole, whole, block, block]
            + [pl.BlockSpec(memory_space=pl.ANY)] * (cols + 1),
            out_specs=[
                block,
                block,
                pair,
                pl.BlockSpec((1, width, depth), lambda i, s: (s[2], 0, 0)),
            ],
            scratch_shapes=[
                pltpu.VMEM((2, rows, depth), BF16),
                pltpu.VMEM((depth, width), BF16),
                pltpu.SemaphoreType.DMA((rows // tile,)),
            ],
        ),
        out_shape=[
            jax.ShapeDtypeStruct((rows, width), F32),
            jax.ShapeDtypeStruct((rows, width), F32),
            jax.ShapeDtypeStruct((2, rows, width), BF16),
            jax.ShapeDtypeStruct(flipped.shape, BF16),
        ],
        input_output_aliases={6 + cols: 3},
        compiler_params=params(44),
        cost_estimate=cost(4 * rows * width * depth, 30 * rows * width),
        name="rotate",
    )(at, part, above, below, first, second, *pieces, flipped)


def restore_kernel(me_ref, normed, *refs, cols):
    flipped, outs = refs[:cols], refs[cols:]
    tile = normed.shape[1]
    piece = outs[0].shape[2]
    both = normed[...].reshape(2 * tile, normed.shape[2])
    for distance in range(cols):
        term = dot(both, flipped[distance][0], ((1,), (0,)))
        term = term[:tile] + term[tile:]
        for at in range(len(outs) // 2):
            out = outs[2 * at + distance % 2]
            out[distance // 2] = term[:, at * piece : (at + 1) * piece]


def restore(me, normed, flipped, cols, piece, batch, count):
    _, depth, inner = normed.shape
    wide = flipped.shape[2]
    tile = min(256, depth)
    out = pl.BlockSpec((cols // 2, tile, piece), lambda i, s: (0, i, 0))

    def columns(distance):
        def at(i, s):
            start = (s[0] ^ distance) * inner + batch * count * piece
            return start // wide, 0, lax.rem(start, wide) // (count * piece)

        return pl.BlockSpec((1, inner, count * piece), at, pipeline_mode=pl.Buffered(1))

    outs = pl.pallas_call(
        functools.partial(restore_kernel, cols=cols),
        grid_spec=pltpu.PrefetchScalarGridSpec(
            num_scalar_prefetch=1,
            grid=(depth // tile,),
            in_specs=[pl.BlockSpec((2, tile, inner), lambda i, s: (0, i, 0))]
            + [columns(distance) for distance in range(cols)],
            out_specs=[out] * (2 * count),
        ),
        out_shape=[jax.ShapeDtypeStruct((cols // 2, depth, piece), F32)] * (2 * count),
        compiler_params=params(44),
        cost_estimate=cost(
            4 * depth * inner * count * piece * cols, 8 * depth * count * piece * cols
        ),
        name="restore",
    )(me, normed, *([flipped] * cols))
    return [(outs[2 * at], outs[2 * at + 1]) for at in range(count)]


def summed(keep, mate, codes):
    depth = keep.shape[1]
    scales = [scale_of(code, depth) for code in codes]

    def value_at(rows):
        value = keep[0, rows, :] + mate[0, rows, :]
        for code, scale in zip(codes, scales):
            value = value + decode(code[rows, :], scale)
        return value

    return value_at


def send_kernel(keep, mate, *refs, tile):
    codes, (message, total) = refs[:-2], refs[-2:]
    fill(message, total, summed(keep, mate, codes), tile)


def send(keep, mate, distance, codes):
    _, depth, piece = keep.shape
    tile = min(64, depth)
    pair = pl.BlockSpec((1, depth, piece), lambda i: (distance // 2, 0, 0))
    message = pl.BlockSpec((depth + EXTRA, piece), lambda i: (0, 0))
    return pl.pallas_call(
        functools.partial(send_kernel, tile=tile),
        grid=(1,),
        in_specs=[pair, pair] + [message] * len(codes),
        out_specs=message,
        out_shape=jax.ShapeDtypeStruct((depth + EXTRA, piece), BF16),
        scratch_shapes=[pltpu.VMEM((depth, piece), F32)],
        compiler_params=params(16),
        cost_estimate=cost(400 * depth * piece, 18 * depth * piece, 4),
        name="send",
    )(keep, mate, *codes)


def expand_send_kernel(place_ref, keep, mate, *refs, tile):
    codes, (left, message, both, total) = refs[:-4], refs[-4:]
    depth, piece = total.shape

    @pl.when(pl.program_id(0) == 0)
    def _():
        value_at = summed(keep, mate, codes)

        def put(i, carry):
            rows = pl.ds(pl.multiple_of(i * tile, tile), tile)
            high, low = kernel_split(value_at(rows))
            both[rows, :piece] = high
            both[rows, piece:] = low
            return carry

        lax.fori_loop(0, both.shape[0] // tile, put, 0)

    product = dot(left[...], both[...], ((1,), (0,)))
    total[...] = product[:, :piece] + product[:, piece:]
    fill(message, None, lambda rows: total[rows, :], tile, lambda rows: total[rows, :])


def expand_send(place, keep, mate, codes, left, depth):
    inner, piece = keep.shape[1:]
    count = left.shape[0] // depth // 2
    pair = pl.BlockSpec((1, inner, piece), lambda i, s: (0, 0, 0))
    code = pl.BlockSpec((inner + EXTRA, piece), lambda i, s: (0, 0))
    return pl.pallas_call(
        functools.partial(expand_send_kernel, tile=min(64, depth)),
        grid_spec=pltpu.PrefetchScalarGridSpec(
            num_scalar_prefetch=1,
            grid=(count,),
            in_specs=[pair, pair]
            + [code] * len(codes)
            + [pl.BlockSpec((depth, inner), lambda i, s: (s[0] ^ (2 * i + 1), 0))],
            out_specs=[
                pl.BlockSpec((None, depth + EXTRA, piece), lambda i, s: (i, 0, 0)),
                pl.BlockSpec((inner, 2 * piece), lambda i, s: (0, 0)),
            ],
            scratch_shapes=[pltpu.VMEM((depth, piece), F32)],
        ),
        out_shape=[
            jax.ShapeDtypeStruct((count, depth + EXTRA, piece), BF16),
            jax.ShapeDtypeStruct((inner, 2 * piece), BF16),
        ],
        compiler_params=params(40),
        cost_estimate=cost(4 * count * depth * inner * piece, 4 * depth * inner, 4),
        name="expand_send",
    )(place, keep, mate, *codes, left)


def expand_keep_kernel(place_ref, both, left, out):
    piece = out.shape[1]
    product = dot(left[...], both[...], ((1,), (0,)))
    out[...] = product[:, :piece] + product[:, piece:]


def expand_keep(place, both, left, depth):
    inner, piece = both.shape[0], both.shape[1] // 2
    count = left.shape[0] // depth // 2
    return pl.pallas_call(
        expand_keep_kernel,
        grid_spec=pltpu.PrefetchScalarGridSpec(
            num_scalar_prefetch=1,
            grid=(count,),
            in_specs=[
                pl.BlockSpec((inner, 2 * piece), lambda i, s: (0, 0)),
                pl.BlockSpec((depth, inner), lambda i, s: (s[0] ^ (2 * i), 0)),
            ],
            out_specs=pl.BlockSpec((None, depth, piece), lambda i, s: (i, 0, 0)),
        ),
        out_shape=jax.ShapeDtypeStruct((count, depth, piece), F32),
        compiler_params=params(60),
        cost_estimate=cost(4 * count * depth * inner * piece, 4 * depth * inner, 4),
        name="expand_keep",
    )(place, both, left)


def hop_kernel(kept, *refs, tile):
    arrived, (message, total) = refs[:-2], refs[-2:]
    depth = total.shape[0]
    scales = [scale_of(code, depth) for code in arrived]

    def value_at(rows):
        value = kept[rows, :]
        for code, scale in zip(arrived, scales):
            value = value + decode(code[rows, :], scale)
        return value

    fill(message, total, value_at, tile)


def hop(kept, arrived, step):
    _, depth, piece = kept.shape
    count = arrived[-1].shape[0] // 2

    def at(shift):
        return lambda i: ((2 * i + 1) * 2**shift, 0, 0)

    return pl.pallas_call(
        functools.partial(hop_kernel, tile=min(64, depth)),
        grid=(count,),
        in_specs=[pl.BlockSpec((None, depth, piece), at(step - 1))]
        + [
            pl.BlockSpec((None, depth + EXTRA, piece), at(step - 1 - index))
            for index in range(len(arrived))
        ],
        out_specs=pl.BlockSpec((None, depth + EXTRA, piece), lambda i: (i, 0, 0)),
        out_shape=jax.ShapeDtypeStruct((count, depth + EXTRA, piece), BF16),
        scratch_shapes=[pltpu.VMEM((depth, piece), F32)],
        compiler_params=params(40),
        cost_estimate=cost(400 * count * depth * piece, 12 * count * depth * piece, 4),
        name="hop",
    )(kept, *arrived)


def finish_kernel(kept, *refs, tile, terms):
    arrived, out = refs[:terms], refs[-1]
    depth = out.shape[0]
    scales = [scale_of(code, depth) for code in arrived]

    def add(i, carry):
        rows = pl.ds(pl.multiple_of(i * tile, tile), tile)
        value = kept[rows, :]
        for code, scale in zip(arrived, scales):
            value = value + decode(code[rows, :], scale)
        out[rows, :] = value
        return carry

    lax.fori_loop(0, depth // tile, add, 0)


def finish(kept, arrived, update, chunk, width):
    _, depth, piece = kept.shape
    extra = [] if update is None else [update]
    first = lambda i: (0, 0, 0)
    return pl.pallas_call(
        functools.partial(finish_kernel, tile=min(64, depth), terms=len(arrived)),
        grid=(1,),
        in_specs=[pl.BlockSpec((None, depth, piece), first)]
        + [pl.BlockSpec((None, depth + EXTRA, piece), first)] * len(arrived)
        + [pl.BlockSpec(memory_space=pl.ANY)] * len(extra),
        out_specs=pl.BlockSpec((depth, piece), lambda i: (0, chunk)),
        out_shape=jax.ShapeDtypeStruct((depth, width), F32),
        input_output_aliases={1 + len(arrived): 0} if extra else {},
        compiler_params=params(40),
        cost_estimate=cost(400 * depth * piece, 12 * depth * piece, 0.1),
        name="finish",
    )(kept, *arrived, *extra)


def build(lines, cols):
    def swap(value, distance):
        return lax.ppermute(value, "col", [(i, i ^ distance) for i in range(cols)])

    def by_distance(block):
        held = {0: block}
        for distance in range(2, cols, 2):
            held[distance] = swap(block, distance)
        for distance in range(0, cols, 2):
            held[distance + 1] = swap(held[distance], 1)
        return held

    def place_by_distance(block, me):
        out = jnp.zeros((cols,) + block.shape, block.dtype)
        for distance, value in by_distance(block).items():
            out = lax.dynamic_update_index_in_dim(out, value, me ^ distance, 0)
        return out

    def up(value, senders):
        return lax.ppermute(value, "row", [(i, i + 1) for i in senders])

    def down(value, senders):
        return lax.ppermute(value, "row", [(i, i - 1) for i in senders])

    def after(value, *others):
        return lax.optimization_barrier((value,) + others)[0]

    def walk(held, step):
        held[-step] = up(held[1 - step], range(step - 1, lines - 1))
        held[step] = down(held[step - 1], range(1, lines - step + 1))

    def local(gradient, first_moment, second_moment, left_basis, right_basis):
        me, place = lax.axis_index("col"), lax.axis_index("row")
        depth, width = gradient.shape
        piece = width // CHUNKS
        far = lines - 1
        ends = (place == 0) | (place == far) if depth == width else False
        spot = jnp.reshape(place, (1,))
        at = jnp.stack([me, place, jnp.where(ends, far - place, lines)])
        me_now = jnp.reshape(me, (1,))
        barrier = lax.optimization_barrier
        near = [offset for offset in range(-far, far + 1) if abs(offset) < far]

        left = place_by_distance(left_basis, me).reshape(-1, left_basis.shape[1])
        grads = {0: gradient}
        for step in range(1, lines):
            if step == far:
                left, grads[1 - step], grads[step - 1] = barrier(
                    (left, grads[1 - step], grads[step - 1])
                )
            walk(grads, step)
        before = halfway(spot, left, grads, near, lines, None)

        inner = after(right_basis, grads[1 - far], grads[far - 1])
        own, before, grads[-far], grads[far] = barrier(
            (right_basis, before, grads[-far], grads[far])
        )
        rights = {0: right_basis}
        inner_up, inner_down, end_up, end_down = inner, inner, own, own
        for step in range(1, lines):
            from_up = up(end_up, [lines - 2])
            from_down = down(end_down, [1])
            if step < far:
                inner_up = up(inner_up, range(step - 1, lines - 2))
                inner_down = down(inner_down, range(2, lines - step + 1))
                end_up = after(inner_up, own) if step == 1 else inner_up
                end_down = after(inner_down, own) if step == 1 else inner_down
                rights[-step] = jnp.where(place == far, from_up, inner_up)
                rights[step] = jnp.where(place == 0, from_down, inner_down)
                if step == 1:
                    first_blocks = inner_up, inner_down
            else:
                rights[-step], rights[step] = from_up, from_down
        above, below = rights[far], rights[-far]

        pair, message = pack(halfway(spot, left, grads, [-far, far], lines, before))
        message = after(message, *first_blocks)
        aligned = depth == width

        def put_block(held, offset):
            there = place + offset
            there = jnp.where((there >= 0) & (there < lines), there, lines)
            return put(jnp.reshape(there, (1,)), rights[offset], held, lines + 1)

        held = None
        for offset in (0, -1, 1):
            held = put_block(held, offset)
        pieces = {1: swap(message, 1)}
        mate_pair = unpack(pieces[1])
        for distance in range(2, cols, 2):
            pieces[distance] = after(swap(message, distance), held[1], mate_pair)
            pieces[distance + 1] = swap(pieces[distance], 1)
        for step in range(2, far if aligned else lines):
            held = put_block(put_block(held, -step), step)
        pieces = [pair, mate_pair] + [unpack(pieces[distance]) for distance in range(2, cols)]
        part = rotate_part(at, pieces, held[0], far if aligned else -1)
        part, above, below = barrier((part, above, below))
        if not aligned:
            above, below = jnp.zeros_like(above), jnp.zeros_like(below)
        new_first, new_second, normed, flipped = rotate(
            at, part, pieces, above, below, first_moment, second_moment, held[1], lines
        )

        def cross(value, distance):
            return lax.ppermute(value, "row", [(i, i ^ distance) for i in range(lines)])

        def later_hops(chunk):
            kept, arrived = products[chunk]
            if chunk - 1 in second:
                kept = after(kept, second[chunk - 1])
            if chunk + 1 < len(outgoing):
                kept = after(kept, outgoing[chunk + 1])
            step = 1
            while 2**step < lines:
                message = hop(kept, arrived, step)
                if step == 1:
                    second[chunk] = message
                arrived = arrived + [cross(message, 2**step)]
                step += 1
            products[chunk] = kept, arrived

        products, halves, sent, outgoing, second = [], [], [], [], {}

        def multiply(chunk, *before):
            codes = [swap(code, 2 * index + 2) for index, code in enumerate(sent[chunk])]
            if codes and before:
                codes[0] = after(codes[0], *before)
            message, both = expand_send(spot, *halves[chunk], codes, left, depth)
            outgoing.append(message)
            products.append((expand_keep(spot, both, left, depth), [cross(message, 1)]))

        def sums(batch, count, *before):
            ready = after(normed, *before) if before else normed
            for keep, mate in restore(me_now, ready, flipped, cols, piece, batch, count):
                mate = swap(mate, 1)
                halves.append((keep, mate))
                sent.append([send(keep, mate, distance, []) for distance in range(2, cols, 2)])

        sums(0, 2)
        sums(1, 2, *sent[0])
        for chunk in range(CHUNKS):
            if chunk >= 2:
                later_hops(chunk - 2)
            multiply(chunk, *([second[chunk - 2]] if chunk - 2 in second else outgoing[-1:]))
        update = None
        for chunk in range(CHUNKS):
            if chunk >= CHUNKS - 2:
                later_hops(chunk)
            update = finish(*products[chunk], update, chunk, width)
        return (new_first, new_second, update)

    return local


def solution(mesh):
    return jax.shard_map(
        build(mesh.shape["row"], mesh.shape["col"]),
        mesh=mesh,
        in_specs=(
            P(("groups", "row"), "col"),
            P(("groups", "row"), "col"),
            P(("groups", "row"), "col"),
            P(("groups", "col"), "row"),
            P(("groups", "row"), "col"),
        ),
        out_specs=(
            P(("groups", "row"), "col"),
            P(("groups", "row"), "col"),
            P(("groups", "row"), "col"),
        ),
        check_vma=False,
    )
```

```python
import functools
import jax
import jax.numpy as jnp
from jax import lax
from jax.experimental import pallas as pl
from jax.experimental.pallas import tpu as pltpu
from jax.sharding import PartitionSpec as P

BETA_ONE = 0.9
BETA_TWO = 0.95
EPSILON = 1e-08
CHUNKS = 4
EXTRA = 16
F32 = jnp.float32
BF16 = jnp.bfloat16
MIB = 2**20


def params(mib):
    return pltpu.CompilerParams(vmem_limit_bytes=mib * MIB)


def cost(flops, moved, weight=4):
    return pl.CostEstimate(
        flops=int(flops * weight), bytes_accessed=int(moved * weight), transcendentals=0
    )


def split(value):
    high = lax.reduce_precision(value, exponent_bits=8, mantissa_bits=7)
    return high.astype(BF16), (value - high).astype(BF16)


def kernel_split(value):
    high = value.astype(BF16)
    return high, (value - high.astype(F32)).astype(BF16)


def dot(a, b, dims):
    return lax.dot_general(a, b, (dims, ((), ())), preferred_element_type=F32)


TOP = 7.5


def encode(value, inverse):
    code = jnp.abs(value) * (inverse * 2.0**TOP)
    for _ in range(4):
        code = code * code
    return jnp.where(value < 0, -code, code).astype(BF16)


def decode(code, scale):
    code = code.astype(F32)
    size = jnp.abs(code)
    root = jnp.exp2(jnp.log2(size) * 0.0625 - TOP) * scale
    root = jnp.where(size > 0, root, 0.0)
    return jnp.where(code < 0, -root, root)


def scale_of(message, depth):
    return jnp.max(message[depth : depth + EXTRA, :].astype(F32), axis=(0, 1), keepdims=True)


def fill(message, total, value_at, tile, again=None):
    depth, piece = message.shape[0] - EXTRA, message.shape[1]

    def add(i, top):
        rows = pl.ds(pl.multiple_of(i * tile, tile), tile)
        value = value_at(rows)
        if again is None:
            total[rows, :] = value
        return jnp.maximum(top, jnp.abs(value))

    top = lax.fori_loop(0, depth // tile, add, jnp.zeros((tile, piece), F32))
    top = jnp.maximum(jnp.max(top, axis=(0, 1), keepdims=True), 1e-30)
    scale = jnp.broadcast_to(top, (EXTRA, piece)).astype(BF16)
    message[depth : depth + EXTRA, :] = scale
    inverse = 1.0 / jnp.max(scale.astype(F32), axis=(0, 1), keepdims=True)

    def put(i, carry):
        rows = pl.ds(pl.multiple_of(i * tile, tile), tile)
        value = total[rows, :] if again is None else again(rows)
        message[rows, :] = encode(value, inverse)
        return carry

    lax.fori_loop(0, depth // tile, put, 0)


def halfway_kernel(place_ref, left, *refs, offsets, lines, first):
    pieces, refs = refs[: len(offsets)], refs[len(offsets) :]
    total = refs[-1]
    depth = pieces[0].shape[0]
    total[...] = jnp.zeros_like(total) if first else refs[0][...]
    place = place_ref[0]
    for offset, piece in zip(offsets, pieces):

        @pl.when((place + offset >= 0) & (place + offset < lines))
        def _(offset=offset, piece=piece):
            rows = left[pl.ds(pl.multiple_of((place + offset) * depth, depth), depth), :]
            total[...] += dot(rows, piece[...], ((0,), (0,)))

    refs[-2][...] = total[...]


def halfway(place, left, held, offsets, lines, before):
    pieces = [held[offset] for offset in offsets]
    depth, width = pieces[0].shape
    inner = left.shape[1]
    tile = min(256, inner)
    whole = pl.BlockSpec((depth, width), lambda i, s: (0, 0))
    block = pl.BlockSpec((tile, width), lambda i, s: (i, 0))
    extra = [] if before is None else [before]
    return pl.pallas_call(
        functools.partial(halfway_kernel, offsets=offsets, lines=lines, first=before is None),
        grid_spec=pltpu.PrefetchScalarGridSpec(
            num_scalar_prefetch=1,
            grid=(inner // tile,),
            in_specs=[pl.BlockSpec((left.shape[0], tile), lambda i, s: (0, i))]
            + [whole] * len(pieces)
            + [block] * len(extra),
            out_specs=block,
            scratch_shapes=[pltpu.VMEM((tile, width), F32)],
        ),
        out_shape=jax.ShapeDtypeStruct((inner, width), F32),
        compiler_params=params(48),
        cost_estimate=cost(8 * depth * inner * width, 8 * depth * inner, 0.3),
        name="halfway",
    )(place, left, *pieces, *extra)


def pack_kernel(value, pair, message, *, tile):
    depth, _ = value.shape

    def value_at(rows):
        now = value[rows, :]
        high, low = kernel_split(now)
        pair[0, rows, :] = high
        pair[1, rows, :] = low
        return now

    fill(message, None, value_at, tile, lambda rows: value[rows, :])


def pack(value):
    depth, width = value.shape
    return pl.pallas_call(
        functools.partial(pack_kernel, tile=min(16, depth)),
        out_shape=[
            jax.ShapeDtypeStruct((2, depth, width), BF16),
            jax.ShapeDtypeStruct((depth + EXTRA, width), BF16),
        ],
        compiler_params=params(60),
        cost_estimate=cost(400 * depth * width, 10 * depth * width, 0.3),
        name="pack",
    )(value)


def unpack_kernel(message, scales, pair, *, tile):
    _, depth, _ = pair.shape
    scale = scale_of(scales, 0)

    def put(i, carry):
        rows = pl.ds(pl.multiple_of(i * tile, tile), tile)
        high, low = kernel_split(decode(message[rows, :], scale))
        pair[0, rows, :] = high
        pair[1, rows, :] = low
        return carry

    lax.fori_loop(0, depth // tile, put, 0)


def unpack(message):
    depth, width = message.shape[0] - EXTRA, message.shape[1]
    step = min(256, depth)
    return pl.pallas_call(
        functools.partial(unpack_kernel, tile=min(16, step)),
        grid=(depth // step,),
        in_specs=[
            pl.BlockSpec((step, width), lambda i: (i, 0)),
            pl.BlockSpec((EXTRA, width), lambda i: (depth // EXTRA, 0)),
        ],
        out_specs=pl.BlockSpec((2, step, width), lambda i: (0, i, 0)),
        out_shape=jax.ShapeDtypeStruct((2, depth, width), BF16),
        compiler_params=params(60),
        cost_estimate=cost(400 * depth * width, 6 * depth * width, 0.3),
        name="unpack",
    )(message, message)


def put_kernel(there_ref, piece, *refs):
    right, flipped = refs[-2:]
    right[...] = piece[...]
    flipped[0] = piece[...].T


def put(there, piece, held, blocks):
    depth, width = piece.shape
    extra = [] if held is None else list(held)
    return pl.pallas_call(
        put_kernel,
        grid_spec=pltpu.PrefetchScalarGridSpec(
            num_scalar_prefetch=1,
            grid=(1,),
            in_specs=[pl.BlockSpec((depth, width), lambda i, s: (0, 0))]
            + [pl.BlockSpec(memory_space=pl.ANY)] * len(extra),
            out_specs=[
                pl.BlockSpec((depth, width), lambda i, s: (s[0], 0)),
                pl.BlockSpec((1, width, depth), lambda i, s: (s[0], 0, 0)),
            ],
        ),
        out_shape=[
            jax.ShapeDtypeStruct((blocks * depth, width), BF16),
            jax.ShapeDtypeStruct((blocks, width, depth), BF16),
        ],
        input_output_aliases={2: 0, 3: 1} if extra else {},
        compiler_params=params(60),
        cost_estimate=cost(0, 6 * depth * width, 0.3),
        name="put",
    )(there, piece, *extra)


def rotate_part_kernel(at_ref, *refs, cols, width, far):
    pieces, (right, out, total) = refs[:cols], refs[cols:]
    tile = out.shape[0]
    me, place = at_ref[0], at_ref[1]
    total[...] = jnp.zeros_like(total)
    for distance in range(cols):
        block = me ^ distance
        late = (block == far - place) & ((place == 0) | (place == far))

        @pl.when(jnp.logical_not(late))
        def _(distance=distance, block=block):
            rows = right[pl.ds(pl.multiple_of(block * width, width), width), :]
            total[...] += dot(pieces[distance][...].reshape(2 * tile, width), rows, ((1,), (0,)))

    out[...] = total[:tile, :] + total[tile:, :]


def rotate_part(at, pieces, right, far):
    cols = len(pieces)
    _, depth, width = pieces[0].shape
    tile = min(256, depth)
    return pl.pallas_call(
        functools.partial(rotate_part_kernel, cols=cols, width=width, far=far),
        grid_spec=pltpu.PrefetchScalarGridSpec(
            num_scalar_prefetch=1,
            grid=(depth // tile,),
            in_specs=[pl.BlockSpec((2, tile, width), lambda i, s: (0, i, 0))] * cols
            + [
                pl.BlockSpec(
                    (cols * width, width), lambda i, s: (0, 0), pipeline_mode=pl.Buffered(1)
                )
            ],
            out_specs=pl.BlockSpec((tile, width), lambda i, s: (i, 0)),
            scratch_shapes=[pltpu.VMEM((2 * tile, width), F32)],
        ),
        out_shape=jax.ShapeDtypeStruct((depth, width), F32),
        compiler_params=params(48),
        cost_estimate=cost(4 * depth * width * width * cols, 20 * depth * width, 0.3),
        name="rotate_part",
    )(at, *pieces, right)


def rotate_kernel(at_ref, part, above, below, first, second, *refs, cols, lines):
    pieces, refs = refs[:cols], refs[cols + 1 :]
    new_first, new_second, normed, flipped, held, last, arrived = refs
    tile, width = first.shape
    depth = last.shape[0]
    me, place = at_ref[0], at_ref[1]
    step, steps = pl.program_id(0), held.shape[1] // tile
    start = (lines - 1 - place) * depth
    distance_now = me ^ (start // width)

    def copy(distance, at):
        rows = pl.ds(at * tile, tile)
        if depth == width:
            source = pieces[distance].at[:, rows, :]
        else:
            columns = pl.ds(pl.multiple_of(lax.rem(start, width), depth), depth)
            source = pieces[distance].at[:, rows, columns]
        return pltpu.make_async_copy(source, held.at[:, rows, :], arrived.at[at])

    @pl.when(step == 0)
    def _():
        for distance in range(cols):

            @pl.when(distance_now == distance)
            def _(distance=distance):
                for at in range(steps):
                    copy(distance, at).start()

        last[...] = jnp.where(place == 0, above[...], below[...])
        flipped[0] = last[...].T

    for at in range(steps):

        @pl.when(step == at)
        def _(at=at):
            copy(0, at).wait()

    rows = pl.ds(pl.multiple_of(step * tile, tile), tile)
    both = dot(held[:, rows, :].reshape(2 * tile, depth), last[...], ((1,), (0,)))
    rotated = part[...] + both[:tile] + both[tile:]
    one = BETA_ONE * first[...] + (1.0 - BETA_ONE) * rotated
    two = BETA_TWO * second[...] + (1.0 - BETA_TWO) * rotated * rotated
    new_first[...] = one
    new_second[...] = two
    high, low = kernel_split(one / (jnp.sqrt(two) + EPSILON))
    normed[0] = high
    normed[1] = low


def rotate(at, part, pieces, above, below, first, second, flipped, lines):
    cols = len(pieces)
    rows, width = first.shape
    depth = above.shape[0]
    tile = min(256, rows)
    block = pl.BlockSpec((tile, width), lambda i, s: (i, 0))
    pair = pl.BlockSpec((2, tile, width), lambda i, s: (0, i, 0))
    whole = pl.BlockSpec(above.shape, lambda i, s: (0, 0), pipeline_mode=pl.Buffered(1))
    return pl.pallas_call(
        functools.partial(rotate_kernel, cols=cols, lines=lines),
        grid_spec=pltpu.PrefetchScalarGridSpec(
            num_scalar_prefetch=1,
            grid=(rows // tile,),
            in_specs=[block, whole, whole, block, block]
            + [pl.BlockSpec(memory_space=pl.ANY)] * (cols + 1),
            out_specs=[
                block,
                block,
                pair,
                pl.BlockSpec((1, width, depth), lambda i, s: (s[2], 0, 0)),
            ],
            scratch_shapes=[
                pltpu.VMEM((2, rows, depth), BF16),
                pltpu.VMEM((depth, width), BF16),
                pltpu.SemaphoreType.DMA((rows // tile,)),
            ],
        ),
        out_shape=[
            jax.ShapeDtypeStruct((rows, width), F32),
            jax.ShapeDtypeStruct((rows, width), F32),
            jax.ShapeDtypeStruct((2, rows, width), BF16),
            jax.ShapeDtypeStruct(flipped.shape, BF16),
        ],
        input_output_aliases={6 + cols: 3},
        compiler_params=params(44),
        cost_estimate=cost(4 * rows * width * depth, 30 * rows * width),
        name="rotate",
    )(at, part, above, below, first, second, *pieces, flipped)


def restore_kernel(me_ref, normed, *refs, cols):
    flipped, outs = refs[:cols], refs[cols:]
    tile = normed.shape[1]
    piece = outs[0].shape[2]
    both = normed[...].reshape(2 * tile, normed.shape[2])
    for distance in range(cols):
        term = dot(both, flipped[distance][0], ((1,), (0,)))
        term = term[:tile] + term[tile:]
        for at in range(len(outs) // 2):
            out = outs[2 * at + distance % 2]
            out[distance // 2] = term[:, at * piece : (at + 1) * piece]


def restore(me, normed, flipped, cols, piece, batch, count):
    _, depth, inner = normed.shape
    wide = flipped.shape[2]
    tile = min(256, depth)
    out = pl.BlockSpec((cols // 2, tile, piece), lambda i, s: (0, i, 0))

    def columns(distance):
        def at(i, s):
            start = (s[0] ^ distance) * inner + batch * count * piece
            return start // wide, 0, lax.rem(start, wide) // (count * piece)

        return pl.BlockSpec((1, inner, count * piece), at, pipeline_mode=pl.Buffered(1))

    outs = pl.pallas_call(
        functools.partial(restore_kernel, cols=cols),
        grid_spec=pltpu.PrefetchScalarGridSpec(
            num_scalar_prefetch=1,
            grid=(depth // tile,),
            in_specs=[pl.BlockSpec((2, tile, inner), lambda i, s: (0, i, 0))]
            + [columns(distance) for distance in range(cols)],
            out_specs=[out] * (2 * count),
        ),
        out_shape=[jax.ShapeDtypeStruct((cols // 2, depth, piece), F32)] * (2 * count),
        compiler_params=params(44),
        cost_estimate=cost(
            4 * depth * inner * count * piece * cols, 8 * depth * count * piece * cols
        ),
        name="restore",
    )(me, normed, *([flipped] * cols))
    return [(outs[2 * at], outs[2 * at + 1]) for at in range(count)]


def summed(keep, mate, codes):
    depth = keep.shape[1]
    scales = [scale_of(code, depth) for code in codes]

    def value_at(rows):
        value = keep[0, rows, :] + mate[0, rows, :]
        for code, scale in zip(codes, scales):
            value = value + decode(code[rows, :], scale)
        return value

    return value_at


def send_kernel(keep, mate, *refs, tile):
    codes, (message, total) = refs[:-2], refs[-2:]
    fill(message, total, summed(keep, mate, codes), tile)


def send(keep, mate, distance, codes):
    _, depth, piece = keep.shape
    tile = min(64, depth)
    pair = pl.BlockSpec((1, depth, piece), lambda i: (distance // 2, 0, 0))
    message = pl.BlockSpec((depth + EXTRA, piece), lambda i: (0, 0))
    return pl.pallas_call(
        functools.partial(send_kernel, tile=tile),
        grid=(1,),
        in_specs=[pair, pair] + [message] * len(codes),
        out_specs=message,
        out_shape=jax.ShapeDtypeStruct((depth + EXTRA, piece), BF16),
        scratch_shapes=[pltpu.VMEM((depth, piece), F32)],
        compiler_params=params(16),
        cost_estimate=cost(400 * depth * piece, 18 * depth * piece, 4),
        name="send",
    )(keep, mate, *codes)


def expand_send_kernel(place_ref, keep, mate, *refs, tile):
    codes, (left, message, both, total) = refs[:-4], refs[-4:]
    depth, piece = total.shape

    @pl.when(pl.program_id(0) == 0)
    def _():
        value_at = summed(keep, mate, codes)

        def put(i, carry):
            rows = pl.ds(pl.multiple_of(i * tile, tile), tile)
            high, low = kernel_split(value_at(rows))
            both[rows, :piece] = high
            both[rows, piece:] = low
            return carry

        lax.fori_loop(0, both.shape[0] // tile, put, 0)

    product = dot(left[...], both[...], ((1,), (0,)))
    total[...] = product[:, :piece] + product[:, piece:]
    fill(message, None, lambda rows: total[rows, :], tile, lambda rows: total[rows, :])


def expand_send(place, keep, mate, codes, left, depth):
    inner, piece = keep.shape[1:]
    count = left.shape[0] // depth // 2
    pair = pl.BlockSpec((1, inner, piece), lambda i, s: (0, 0, 0))
    code = pl.BlockSpec((inner + EXTRA, piece), lambda i, s: (0, 0))
    return pl.pallas_call(
        functools.partial(expand_send_kernel, tile=min(64, depth)),
        grid_spec=pltpu.PrefetchScalarGridSpec(
            num_scalar_prefetch=1,
            grid=(count,),
            in_specs=[pair, pair]
            + [code] * len(codes)
            + [pl.BlockSpec((depth, inner), lambda i, s: (s[0] ^ (2 * i + 1), 0))],
            out_specs=[
                pl.BlockSpec((None, depth + EXTRA, piece), lambda i, s: (i, 0, 0)),
                pl.BlockSpec((inner, 2 * piece), lambda i, s: (0, 0)),
            ],
            scratch_shapes=[pltpu.VMEM((depth, piece), F32)],
        ),
        out_shape=[
            jax.ShapeDtypeStruct((count, depth + EXTRA, piece), BF16),
            jax.ShapeDtypeStruct((inner, 2 * piece), BF16),
        ],
        compiler_params=params(40),
        cost_estimate=cost(4 * count * depth * inner * piece, 4 * depth * inner, 4),
        name="expand_send",
    )(place, keep, mate, *codes, left)


def expand_keep_kernel(place_ref, both, left, out):
    piece = out.shape[1]
    product = dot(left[...], both[...], ((1,), (0,)))
    out[...] = product[:, :piece] + product[:, piece:]


def expand_keep(place, both, left, depth):
    inner, piece = both.shape[0], both.shape[1] // 2
    count = left.shape[0] // depth // 2
    return pl.pallas_call(
        expand_keep_kernel,
        grid_spec=pltpu.PrefetchScalarGridSpec(
            num_scalar_prefetch=1,
            grid=(count,),
            in_specs=[
                pl.BlockSpec((inner, 2 * piece), lambda i, s: (0, 0)),
                pl.BlockSpec((depth, inner), lambda i, s: (s[0] ^ (2 * i), 0)),
            ],
            out_specs=pl.BlockSpec((None, depth, piece), lambda i, s: (i, 0, 0)),
        ),
        out_shape=jax.ShapeDtypeStruct((count, depth, piece), F32),
        compiler_params=params(60),
        cost_estimate=cost(4 * count * depth * inner * piece, 4 * depth * inner, 4),
        name="expand_keep",
    )(place, both, left)


def hop_kernel(kept, *refs, tile):
    arrived, (message, total) = refs[:-2], refs[-2:]
    depth = total.shape[0]
    scales = [scale_of(code, depth) for code in arrived]

    def value_at(rows):
        value = kept[rows, :]
        for code, scale in zip(arrived, scales):
            value = value + decode(code[rows, :], scale)
        return value

    fill(message, total, value_at, tile)


def hop(kept, arrived, step):
    _, depth, piece = kept.shape
    count = arrived[-1].shape[0] // 2

    def at(shift):
        return lambda i: ((2 * i + 1) * 2**shift, 0, 0)

    return pl.pallas_call(
        functools.partial(hop_kernel, tile=min(64, depth)),
        grid=(count,),
        in_specs=[pl.BlockSpec((None, depth, piece), at(step - 1))]
        + [
            pl.BlockSpec((None, depth + EXTRA, piece), at(step - 1 - index))
            for index in range(len(arrived))
        ],
        out_specs=pl.BlockSpec((None, depth + EXTRA, piece), lambda i: (i, 0, 0)),
        out_shape=jax.ShapeDtypeStruct((count, depth + EXTRA, piece), BF16),
        scratch_shapes=[pltpu.VMEM((depth, piece), F32)],
        compiler_params=params(40),
        cost_estimate=cost(400 * count * depth * piece, 12 * count * depth * piece, 4),
        name="hop",
    )(kept, *arrived)


def finish_kernel(kept, *refs, tile, terms):
    arrived, out = refs[:terms], refs[-1]
    depth = out.shape[0]
    scales = [scale_of(code, depth) for code in arrived]

    def add(i, carry):
        rows = pl.ds(pl.multiple_of(i * tile, tile), tile)
        value = kept[rows, :]
        for code, scale in zip(arrived, scales):
            value = value + decode(code[rows, :], scale)
        out[rows, :] = value
        return carry

    lax.fori_loop(0, depth // tile, add, 0)


def finish(kept, arrived, update, chunk, width):
    _, depth, piece = kept.shape
    extra = [] if update is None else [update]
    first = lambda i: (0, 0, 0)
    return pl.pallas_call(
        functools.partial(finish_kernel, tile=min(64, depth), terms=len(arrived)),
        grid=(1,),
        in_specs=[pl.BlockSpec((None, depth, piece), first)]
        + [pl.BlockSpec((None, depth + EXTRA, piece), first)] * len(arrived)
        + [pl.BlockSpec(memory_space=pl.ANY)] * len(extra),
        out_specs=pl.BlockSpec((depth, piece), lambda i: (0, chunk)),
        out_shape=jax.ShapeDtypeStruct((depth, width), F32),
        input_output_aliases={1 + len(arrived): 0} if extra else {},
        compiler_params=params(40),
        cost_estimate=cost(400 * depth * piece, 12 * depth * piece, 0.1),
        name="finish",
    )(kept, *arrived, *extra)


def build(lines, cols):
    def swap(value, distance):
        return lax.ppermute(value, "col", [(i, i ^ distance) for i in range(cols)])

    def by_distance(block):
        held = {0: block}
        for distance in range(2, cols, 2):
            held[distance] = swap(block, distance)
        for distance in range(0, cols, 2):
            held[distance + 1] = swap(held[distance], 1)
        return held

    def place_by_distance(block, me):
        out = jnp.zeros((cols,) + block.shape, block.dtype)
        for distance, value in by_distance(block).items():
            out = lax.dynamic_update_index_in_dim(out, value, me ^ distance, 0)
        return out

    def up(value, senders):
        return lax.ppermute(value, "row", [(i, i + 1) for i in senders])

    def down(value, senders):
        return lax.ppermute(value, "row", [(i, i - 1) for i in senders])

    def after(value, *others):
        return lax.optimization_barrier((value,) + others)[0]

    def walk(held, step):
        held[-step] = up(held[1 - step], range(step - 1, lines - 1))
        held[step] = down(held[step - 1], range(1, lines - step + 1))

    def local(gradient, first_moment, second_moment, left_basis, right_basis):
        me, place = lax.axis_index("col"), lax.axis_index("row")
        depth, width = gradient.shape
        piece = width // CHUNKS
        far = lines - 1
        ends = (place == 0) | (place == far) if depth == width else False
        spot = jnp.reshape(place, (1,))
        at = jnp.stack([me, place, jnp.where(ends, far - place, lines)])
        me_now = jnp.reshape(me, (1,))
        barrier = lax.optimization_barrier
        near = [offset for offset in range(-far, far + 1) if abs(offset) < far]

        left = place_by_distance(left_basis, me).reshape(-1, left_basis.shape[1])
        grads = {0: gradient}
        for step in range(1, lines):
            if step == far:
                left, grads[1 - step], grads[step - 1] = barrier(
                    (left, grads[1 - step], grads[step - 1])
                )
            walk(grads, step)
        before = halfway(spot, left, grads, near, lines, None)

        inner = after(right_basis, grads[1 - far], grads[far - 1])
        own, before, grads[-far], grads[far] = barrier(
            (right_basis, before, grads[-far], grads[far])
        )
        rights = {0: right_basis}
        inner_up, inner_down, end_up, end_down = inner, inner, own, own
        for step in range(1, lines):
            from_up = up(end_up, [lines - 2])
            from_down = down(end_down, [1])
            if step < far:
                inner_up = up(inner_up, range(step - 1, lines - 2))
                inner_down = down(inner_down, range(2, lines - step + 1))
                end_up = after(inner_up, own) if step == 1 else inner_up
                end_down = after(inner_down, own) if step == 1 else inner_down
                rights[-step] = jnp.where(place == far, from_up, inner_up)
                rights[step] = jnp.where(place == 0, from_down, inner_down)
                if step == 1:
                    first_blocks = inner_up, inner_down
            else:
                rights[-step], rights[step] = from_up, from_down
        above, below = rights[far], rights[-far]

        pair, message = pack(halfway(spot, left, grads, [-far, far], lines, before))
        message = after(message, *first_blocks)
        aligned = depth == width

        def put_block(held, offset):
            there = place + offset
            there = jnp.where((there >= 0) & (there < lines), there, lines)
            return put(jnp.reshape(there, (1,)), rights[offset], held, lines + 1)

        held = None
        for offset in (0, -1, 1):
            held = put_block(held, offset)
        pieces = {1: swap(message, 1)}
        mate_pair = unpack(pieces[1])
        for distance in range(2, cols, 2):
            pieces[distance] = after(swap(message, distance), held[1], mate_pair)
            pieces[distance + 1] = swap(pieces[distance], 1)
        pieces = [pair, mate_pair] + [unpack(pieces[distance]) for distance in range(2, cols)]
        for step in range(2, far if aligned else lines):
            rights[-step] = after(rights[-step], *pieces[2:])
            rights[step] = after(rights[step], *pieces[2:])
            held = put_block(put_block(held, -step), step)
        part = rotate_part(at, pieces, held[0], far if aligned else -1)
        part, above, below = barrier((part, above, below))
        if not aligned:
            above, below = jnp.zeros_like(above), jnp.zeros_like(below)
        new_first, new_second, normed, flipped = rotate(
            at, part, pieces, above, below, first_moment, second_moment, held[1], lines
        )

        def cross(value, distance):
            return lax.ppermute(value, "row", [(i, i ^ distance) for i in range(lines)])

        def later_hops(chunk):
            kept, arrived = products[chunk]
            if chunk - 1 in second:
                kept = after(kept, second[chunk - 1])
            if chunk + 1 < len(outgoing):
                kept = after(kept, outgoing[chunk + 1])
            step = 1
            while 2**step < lines:
                message = hop(kept, arrived, step)
                if step == 1:
                    second[chunk] = message
                arrived = arrived + [cross(message, 2**step)]
                step += 1
            products[chunk] = kept, arrived

        products, halves, sent, outgoing, second = [], [], [], [], {}

        def multiply(chunk, *before):
            codes = [swap(code, 2 * index + 2) for index, code in enumerate(sent[chunk])]
            if codes and before:
                codes[0] = after(codes[0], *before)
            message, both = expand_send(spot, *halves[chunk], codes, left, depth)
            outgoing.append(message)
            products.append((expand_keep(spot, both, left, depth), [cross(message, 1)]))

        def sums(batch, count, *before):
            ready = after(normed, *before) if before else normed
            for keep, mate in restore(me_now, ready, flipped, cols, piece, batch, count):
                mate = swap(mate, 1)
                halves.append((keep, mate))
                sent.append([send(keep, mate, distance, []) for distance in range(2, cols, 2)])

        sums(0, 2)
        sums(1, 2, *sent[0])
        for chunk in range(CHUNKS):
            if chunk >= 2:
                later_hops(chunk - 2)
            multiply(chunk, *([second[chunk - 2]] if chunk - 2 in second else outgoing[-1:]))
        update = None
        for chunk in range(CHUNKS):
            if chunk >= CHUNKS - 2:
                later_hops(chunk)
            update = finish(*products[chunk], update, chunk, width)
        return (new_first, new_second, update)

    return local


def solution(mesh):
    return jax.shard_map(
        build(mesh.shape["row"], mesh.shape["col"]),
        mesh=mesh,
        in_specs=(
            P(("groups", "row"), "col"),
            P(("groups", "row"), "col"),
            P(("groups", "row"), "col"),
            P(("groups", "col"), "row"),
            P(("groups", "row"), "col"),
        ),
        out_specs=(
            P(("groups", "row"), "col"),
            P(("groups", "row"), "col"),
            P(("groups", "row"), "col"),
        ),
        check_vma=False,
    )
```
